128 devices in a mesh: row: 8 (over x_lo, y), col: 16 (over x_hi, z, core).
Axes of the slice: x: 4 (x_hi: 2, x_lo: 2; x = x_hi * 2 + x_lo), y: 4, z: 4, core: 2. Of those that a mesh axis runs over, the one named last changes fastest.
Arguments:
- perturbations: float32 [512, 16384], P('row', 'col'), may hold values from -200 to 200
- probes: float32 [16384, 128], P(('col', 'row')), may hold values from -6 to 6
Outputs:
- localized: float32 [16384, 8192], P('col', 'row')
- sampled: float32 [16384, 128], P(('col', 'row'))
The draws below stay inside these ranges and needn't reach their ends.
All inputs are finite; a program needn't handle non-finite values.
Results may differ from the reference program's by a relative error of at most 0.00013.
Values sent between devices are 32-bit elements; how exact they have to be, the bound alone decides.
A program may use at most 128 MiB of HBM per device.

```python
import math
import jax
import jax.numpy as jnp
from jax import lax

MEMBERS = 512
PROBES = 128
STEPS = 3
STATES = 16384
WINDOW = 4096
N_COL = 16


def draw_perturbations(key, part):
    subkeys = jax.random.split(jax.random.fold_in(key, 17), 6)
    member_noise = jax.random.normal(subkeys[0], (MEMBERS, STATES), jnp.float32)
    state_scale = jnp.exp(jax.random.uniform(subkeys[1], (STATES,), jnp.float32, 0.0, math.log(10.0)))
    member_scale = jnp.exp(jax.random.uniform(subkeys[2], (MEMBERS, 1), jnp.float32, 0.0, math.log(4.0)))
    offsets = 2.0 * jax.random.normal(subkeys[3], (STATES,), jnp.float32)
    factor = jax.random.normal(subkeys[4], (MEMBERS, 1), jnp.float32)
    loading = 0.3 * jax.random.normal(subkeys[5], (STATES,), jnp.float32)
    values = state_scale * (offsets + member_scale * member_noise + factor * loading)
    return jnp.clip(values, -200.0, 200.0)


def level_of(own_key, extent, cuts, low, largest):
    factor_of = 1.0
    for axis_at, blocks in cuts:
        draws = jax.random.uniform(jax.random.fold_in(jax.random.fold_in(own_key, 6), axis_at), (blocks,), jnp.float32, low / len(cuts), largest / len(cuts))
        factor_of = factor_of * jnp.repeat(jnp.exp(draws), extent[axis_at] // blocks).reshape((-1,) + (1,) * (len(extent) - 1 - axis_at))
    return factor_of


def noise(key, shape, deviation, reach, cuts=(), kind=jnp.bfloat16):
    values = jax.random.normal(key, shape, jnp.float32) * deviation
    if len(cuts) > 0:
        values = level_of(key, shape, cuts, -0.22, 0.18) * values
    return jnp.clip(values, min=-reach, max=reach).astype(kind)


def setup_inputs(seed: int = 0) -> dict:
    streams_of = jax.random.split(jax.random.key(seed), 3)
    perturbations = draw_perturbations(jax.random.fold_in(streams_of[2], 71), 0)
    probes = noise(streams_of[1], (STATES, PROBES), 1.0, 6.0, ((0, 128),), jnp.float32)
    return dict(perturbations=perturbations, probes=probes)


epsilon = 1e-06
power_terms = (2.0 / math.pi - 4.0 / (3.0 * math.pi) - 4.0 / (15.0 * math.pi) - 4.0 / (35.0 * math.pi), 8.0 / (3.0 * math.pi) + 32.0 / (15.0 * math.pi) + 72.0 / (35.0 * math.pi), -32.0 / (15.0 * math.pi) - 192.0 / (35.0 * math.pi), 128.0 / (35.0 * math.pi))

def skew_rows(block, width):
    height = block.shape[0]
    length = block.shape[1]
    flattened = jnp.concatenate([block.reshape(-1), jnp.zeros((height,), block.dtype)])
    return flattened.reshape(height, length + 1)[:, :width]

def unskew_rows(band_rows):
    height = band_rows.shape[0]
    width = band_rows.shape[1]
    length = height + width
    padded = jnp.pad(band_rows, ((0, 0), (0, length + 1 - width)))
    return padded.reshape(-1)[:height * length].reshape(height, length)

def reference(perturbations, probes):
    member_mean = lax.optimization_barrier(jnp.sum(perturbations, 0)) / MEMBERS
    centered = perturbations - member_mean
    spread = jnp.sqrt(lax.optimization_barrier(jnp.sum(centered * centered, 0)) + epsilon)
    normed = centered / spread
    block_rows = STATES // N_COL
    extended = jnp.concatenate([normed[:, STATES - WINDOW:], normed, normed[:, :WINDOW]], 1)
    offsets = jnp.arange(2 * WINDOW, dtype=jnp.int32)
    taper = jnp.maximum(jnp.float32(0.0), 1.0 - jnp.abs(offsets - WINDOW).astype(jnp.float32) / WINDOW)

    def one_block(begin_row):
        row_panel = lax.dynamic_slice_in_dim(normed, begin_row, block_rows, 1)
        col_panel = lax.dynamic_slice_in_dim(extended, begin_row, block_rows + 2 * WINDOW, 1)
        gram_block = jnp.dot(row_panel.T, col_panel, precision=lax.Precision.HIGHEST, preferred_element_type=jnp.float32)
        return skew_rows(gram_block, 2 * WINDOW) * taper
    starts = jnp.arange(N_COL, dtype=jnp.int32) * block_rows
    localized = lax.map(one_block, starts).reshape(STATES, 2 * WINDOW)
    scale_norm = jnp.sum(localized * localized) / STATES

    def apply_band(vector):
        vector_ext = jnp.concatenate([vector[STATES - WINDOW:], vector, vector[:WINDOW]], 0)

        def one_product(begin_row):
            band_rows = lax.dynamic_slice_in_dim(localized, begin_row, block_rows, 0)
            window_rows = lax.dynamic_slice_in_dim(vector_ext, begin_row, block_rows + 2 * WINDOW, 0)
            return jnp.dot(unskew_rows(band_rows), window_rows, precision=lax.Precision.HIGHEST, preferred_element_type=jnp.float32)
        return lax.map(one_product, starts).reshape(STATES, PROBES)
    vector = probes
    summed_terms = power_terms[0] * probes
    for power in range(1, STEPS + 1):
        vector = apply_band(vector) / scale_norm
        summed_terms = summed_terms + power_terms[power] * vector
    sampled = jnp.sqrt(scale_norm) * summed_terms
    return (localized, sampled)
```

```python
import functools
import math

import jax
import jax.numpy as jnp
from jax import lax
from jax.experimental import pallas as pl
from jax.experimental.pallas import tpu as pltpu
from jax.sharding import PartitionSpec as P

MEMBERS = 512
STATES = 16384
WINDOW = 4096
ROWS = 8
COLS = 16
BLOCK = 1024
PIECE = 128
SUB = 256
SPAN = SUB + BLOCK
STEPS = 3
MESH = pl.DeviceIdType.MESH
VMEM_LIMIT = 58 * 2**20

epsilon = 1e-06
power_terms = (
    2.0 / math.pi - 4.0 / (3.0 * math.pi) - 4.0 / (15.0 * math.pi) - 4.0 / (35.0 * math.pi),
    8.0 / (3.0 * math.pi) + 32.0 / (15.0 * math.pi) + 72.0 / (35.0 * math.pi),
    -32.0 / (15.0 * math.pi) - 192.0 / (35.0 * math.pi),
    128.0 / (35.0 * math.pi),
)


def here():
    return lax.axis_index("row"), lax.axis_index("col")


def at(row, col):
    return {"row": row, "col": col}


def reached(r, c):
    found = []
    for panel in range(2):
        for row in range(ROWS):
            col = lax.rem(c + (4 - panel) - row + 2 * COLS, COLS)
            own = (r == row) if row == 4 - panel else None
            found.append((row, col, panel, own))
    return found


def unless(own, step):
    if own is None:
        step()
    else:
        pl.when(jnp.logical_not(own))(step)


def copied(src, dst, send, recv, row, col):
    return pltpu.make_async_remote_copy(
        src_ref=src, dst_ref=dst, send_sem=send, recv_sem=recv,
        device_id=at(row, col), device_id_type=MESH,
    )


def gather_kernel(x_ref, out_ref, send_row, send_need, recv):
    r, c = here()
    barrier = pltpu.get_barrier_semaphore()
    for shift in range(1, ROWS):
        pl.semaphore_signal(barrier, inc=1, device_id=at(lax.rem(r + shift, ROWS), c), device_id_type=MESH)
    for panel in range(2):
        block = lax.rem(c + r - 4 + panel + COLS, COLS)
        for row in range(ROWS):
            own = None
            if row == 4 - panel:
                own = r == row

            def greet(row=row, block=block):
                pl.semaphore_signal(barrier, inc=1, device_id=at(row, block), device_id_type=MESH)

            unless(own, greet)
    pl.semaphore_wait(barrier, 7 + 16 - jnp.where((r == 3) | (r == 4), 1, 0))

    for row, col, panel, own in reached(r, c):
        def go(row=row, col=col, panel=panel):
            copied(x_ref, out_ref.at[1 + panel, r], send_need.at[panel, row], recv.at[1 + panel, r], row, col).start()

        unless(own, go)
        if own is not None:
            @pl.when(own)
            def _(panel=panel):
                pltpu.make_async_copy(x_ref, out_ref.at[1 + panel, r], recv.at[1 + panel, r]).start()
    for shift in range(1, ROWS):
        copied(x_ref, out_ref.at[0, r], send_row.at[shift], recv.at[0, r], lax.rem(r + shift, ROWS), c).start()
    pltpu.make_async_copy(x_ref, out_ref.at[0, r], recv.at[0, r]).start()

    for row, col, panel, own in reached(r, c):
        def done(row=row, col=col, panel=panel):
            copied(x_ref, out_ref.at[1 + panel, r], send_need.at[panel, row], recv.at[1 + panel, r], row, col).wait_send()

        unless(own, done)
    for shift in range(1, ROWS):
        copied(x_ref, out_ref.at[0, r], send_row.at[shift], recv.at[0, r], lax.rem(r + shift, ROWS), c).wait_send()
    for panel in range(3):
        for row in range(ROWS):
            pltpu.make_async_copy(x_ref, out_ref.at[panel, row], recv.at[panel, row]).wait()


def gathered(block):
    return pl.pallas_call(
        gather_kernel,
        name="gather_members",
        out_shape=jax.ShapeDtypeStruct((3, ROWS, MEMBERS // ROWS, BLOCK), jnp.float32),
        in_specs=[pl.BlockSpec(memory_space=pl.ANY)],
        out_specs=pl.BlockSpec(memory_space=pl.ANY),
        scratch_shapes=[
            pltpu.SemaphoreType.DMA((ROWS,)),
            pltpu.SemaphoreType.DMA((2, ROWS)),
            pltpu.SemaphoreType.DMA((3, ROWS)),
        ],
        compiler_params=pltpu.CompilerParams(collective_id=1, has_side_effects=True),
    )(block)


def parted(values):
    high = values.astype(jnp.bfloat16)
    low = (values - high.astype(jnp.float32)).astype(jnp.bfloat16)
    return high, low


def dotted(a, b, dims):
    return lax.dot_general(a, b, (dims, ((), ())), preferred_element_type=jnp.float32)


def skewed(rows, shift):
    sub = lax.broadcasted_iota(jnp.int32, rows.shape, 0)
    if shift:
        rows = pltpu.roll(rows, SPAN - shift, 1)
    for bit in (1, 2, 4):
        rows = jnp.where((sub & bit) != 0, pltpu.roll(rows, SPAN - bit, 1), rows)
    return rows[:, :BLOCK]


def band_kernel(x_ref, local_ref, high_ref, low_ref, square_ref, xh, xl):
    r, _ = here()
    for panel in range(3):
        for first in range(0, BLOCK, SUB):
            values = x_ref[panel, :, first : first + SUB]
            centered = values - jnp.sum(values, 0, keepdims=True) / MEMBERS
            spread = jnp.sqrt(jnp.sum(centered * centered, 0, keepdims=True) + epsilon)
            high, low = parted(centered / spread)
            lo_at = (panel - 1) * BLOCK + first if panel else 2 * BLOCK + first
            xh[:, lo_at : lo_at + SUB] = high
            xl[:, lo_at : lo_at + SUB] = low
    squares = jnp.zeros((8, 128), jnp.float32)
    gap = lax.broadcasted_iota(jnp.int32, (SUB, SPAN), 1) - lax.broadcasted_iota(jnp.int32, (SUB, SPAN), 0)
    taper = jnp.maximum(0.0, 1.0 - jnp.abs(gap + (r * BLOCK - WINDOW)).astype(jnp.float32) / WINDOW)
    taper = jnp.where((gap >= 0) & (gap < BLOCK), taper, 0.0)
    for tile in range(BLOCK // SUB):
        first = tile * SUB
        rows_h = xh[:, 2 * BLOCK + first : 2 * BLOCK + first + SUB]
        rows_l = xl[:, 2 * BLOCK + first : 2 * BLOCK + first + SUB]
        cols_h = xh[:, first : first + SPAN]
        cols_l = xl[:, first : first + SPAN]
        over = ((0,), (0,))
        gram = dotted(rows_h, cols_h, over) + (dotted(rows_h, cols_l, over) + dotted(rows_l, cols_h, over))
        band = gram * taper
        high, low = parted(band)
        high_ref[tile] = high
        low_ref[tile] = low
        squares = squares + jnp.sum((band * band).reshape(SUB // 8, 8, SPAN // 128, 128), (0, 2))
        for group in range(0, SUB, 8):
            local_ref[first + group : first + group + 8, :] = skewed(band[group : group + 8, :], group)
    square_ref[...] = squares


def banded(panels):
    return pl.pallas_call(
        band_kernel,
        name="band",
        out_shape=(
            jax.ShapeDtypeStruct((BLOCK, BLOCK), jnp.float32),
            jax.ShapeDtypeStruct((BLOCK // SUB, SUB, SPAN), jnp.bfloat16),
            jax.ShapeDtypeStruct((BLOCK // SUB, SUB, SPAN), jnp.bfloat16),
            jax.ShapeDtypeStruct((8, 128), jnp.float32),
        ),
        in_specs=[pl.BlockSpec(memory_space=pltpu.VMEM)],
        out_specs=[pl.BlockSpec(memory_space=pltpu.VMEM)] * 4,
        scratch_shapes=[
            pltpu.VMEM((MEMBERS, 3 * BLOCK), jnp.bfloat16),
            pltpu.VMEM((MEMBERS, 3 * BLOCK), jnp.bfloat16),
        ],
        compiler_params=pltpu.CompilerParams(vmem_limit_bytes=VMEM_LIMIT),
    )(panels)


def product_kernel(
    w_ref, high_ref, low_ref, square_ref, out_ref,
    iterate, window, wide, parts, sums, row_squares, col_squares, row_total,
    send_w, recv_w, send_y, recv_y, send_r, recv_r, send_c, recv_c,
):
    r, c = here()
    barrier = pltpu.get_barrier_semaphore()
    for shift in range(1, ROWS):
        pl.semaphore_signal(barrier, inc=1, device_id=at(lax.rem(r + shift, ROWS), c), device_id_type=MESH)
    for shift in range(1, COLS):
        pl.semaphore_signal(barrier, inc=1, device_id=at(r, lax.rem(c + shift, COLS)), device_id_type=MESH)
    for panel in range(2):
        block = lax.rem(c + r - 4 + panel + COLS, COLS)
        for row in range(ROWS):
            own = (r == row) if row == 4 - panel else None

            def greet(row=row, block=block):
                pl.semaphore_signal(barrier, inc=1, device_id=at(row, block), device_id_type=MESH)

            unless(own, greet)
    pl.semaphore_wait(barrier, 7 + 15 + 16 - jnp.where((r == 3) | (r == 4), 1, 0))

    def send_iterate(step, source):
        for row, col, panel, own in reached(r, c):
            def go(row=row, col=col, panel=panel):
                copied(source, window.at[step, panel, r], send_w.at[step, panel, row], recv_w.at[step, panel, r], row, col).start()

            unless(own, go)
            if own is not None:
                @pl.when(own)
                def _(panel=panel):
                    pltpu.make_async_copy(source, window.at[step, panel, r], recv_w.at[step, panel, r]).start()

    for shift in range(1, ROWS):
        copied(square_ref, row_squares.at[r], send_r.at[shift], recv_r.at[r], lax.rem(r + shift, ROWS), c).start()
    pltpu.make_async_copy(square_ref, row_squares.at[r], recv_r.at[r]).start()
    send_iterate(0, w_ref)
    for row in range(ROWS):
        pltpu.make_async_copy(square_ref, row_squares.at[row], recv_r.at[row]).wait()
    row_total[...] = jnp.sum(row_squares[...], 0)
    for shift in range(1, COLS):
        copied(row_total, col_squares.at[c], send_c.at[shift], recv_c.at[c], r, lax.rem(c + shift, COLS)).start()
    pltpu.make_async_copy(row_total, col_squares.at[c], recv_c.at[c]).start()

    total = None
    summed = power_terms[0] * w_ref[...]
    for step in range(STEPS):
        for panel in range(2):
            for row in range(ROWS):
                pltpu.make_async_copy(w_ref, window.at[step, panel, row], recv_w.at[step, panel, row]).wait()
                high, low = parted(window[step, panel, row])
                first = (panel * ROWS + row) * PIECE
                wide[first : first + PIECE, :PIECE] = high
                wide[first : first + PIECE, PIECE:] = low
        for tile in range(BLOCK // SUB):
            first = tile * SUB
            over = ((1,), (0,))
            both = dotted(high_ref[tile], wide[first : first + SPAN, :], over)
            rest = dotted(low_ref[tile], wide[first : first + SPAN, :PIECE], over)
            parts[step, first : first + SUB, :] = both[:, :PIECE] + (both[:, PIECE:] + rest)
            for row in range(first // PIECE, (first + SUB) // PIECE):
                def go(row=row):
                    copied(
                        parts.at[step, row * PIECE : (row + 1) * PIECE], sums.at[step, r],
                        send_y.at[step, row], recv_y.at[step, r], row, c,
                    ).start()

                unless(r == row, go)
        if step == 0:
            for col in range(COLS):
                pltpu.make_async_copy(row_total, col_squares.at[col], recv_c.at[col]).wait()
            total = jnp.sum(jnp.sum(col_squares[...], 0), keepdims=True) / STATES
        vector = parts[step, pl.ds(pl.multiple_of(r * PIECE, PIECE), PIECE), :]
        for row in range(ROWS):
            def landed(row=row):
                pltpu.make_async_copy(w_ref, sums.at[step, row], recv_y.at[step, row]).wait()

            unless(r == row, landed)
            vector = vector + jnp.where(r == row, 0.0, sums[step, row])
        vector = vector / total
        summed = summed + power_terms[step + 1] * vector
        if step < STEPS - 1:
            iterate[step] = vector
            send_iterate(step + 1, iterate.at[step])
    out_ref[...] = jnp.sqrt(total) * summed

    for shift in range(1, ROWS):
        copied(square_ref, row_squares.at[r], send_r.at[shift], recv_r.at[r], lax.rem(r + shift, ROWS), c).wait_send()
    for shift in range(1, COLS):
        copied(row_total, col_squares.at[c], send_c.at[shift], recv_c.at[c], r, lax.rem(c + shift, COLS)).wait_send()
    for step in range(STEPS):
        for row, col, panel, own in reached(r, c):
            def sent(row=row, col=col, panel=panel):
                copied(w_ref, window.at[step, panel, r], send_w.at[step, panel, row], recv_w.at[step, panel, r], row, col).wait_send()

            unless(own, sent)
        for row in range(ROWS):
            def gone(row=row):
                copied(w_ref, sums.at[step, r], send_y.at[step, row], recv_y.at[step, r], row, c).wait_send()

            unless(r == row, gone)


def sampler(probes, high, low, squares):
    return pl.pallas_call(
        product_kernel,
        name="products",
        out_shape=jax.ShapeDtypeStruct((PIECE, PIECE), jnp.float32),
        in_specs=[pl.BlockSpec(memory_space=pltpu.VMEM)] * 4,
        out_specs=pl.BlockSpec(memory_space=pltpu.VMEM),
        scratch_shapes=[
            pltpu.VMEM((STEPS - 1, PIECE, PIECE), jnp.float32),
            pltpu.VMEM((STEPS, 2, ROWS, PIECE, PIECE), jnp.float32),
            pltpu.VMEM((2 * BLOCK, 2 * PIECE), jnp.bfloat16),
            pltpu.VMEM((STEPS, BLOCK, PIECE), jnp.float32),
            pltpu.VMEM((STEPS, ROWS, PIECE, PIECE), jnp.float32),
            pltpu.VMEM((ROWS, 8, 128), jnp.float32),
            pltpu.VMEM((COLS, 8, 128), jnp.float32),
            pltpu.VMEM((8, 128), jnp.float32),
            pltpu.SemaphoreType.DMA((STEPS, 2, ROWS)),
            pltpu.SemaphoreType.DMA((STEPS, 2, ROWS)),
            pltpu.SemaphoreType.DMA((STEPS, ROWS)),
            pltpu.SemaphoreType.DMA((STEPS, ROWS)),
            pltpu.SemaphoreType.DMA((ROWS,)),
            pltpu.SemaphoreType.DMA((ROWS,)),
            pltpu.SemaphoreType.DMA((COLS,)),
            pltpu.SemaphoreType.DMA((COLS,)),
        ],
        compiler_params=pltpu.CompilerParams(
            collective_id=2, has_side_effects=True, vmem_limit_bytes=VMEM_LIMIT
        ),
    )(probes, high, low, squares)


def on_device(perturbations, probes):
    panels = gathered(perturbations).reshape(3, MEMBERS, BLOCK)
    localized, high, low, squares = banded(panels)
    return localized, sampler(probes, high, low, squares)


def solution(mesh):
    return jax.shard_map(
        on_device,
        mesh=mesh,
        in_specs=(P("row", "col"), P(("col", "row"), None)),
        out_specs=(P("col", "row"), P(("col", "row"), None)),
        check_vma=False,
    )
```

```python
import functools
import math

import jax
import jax.numpy as jnp
from jax import lax
from jax.experimental import pallas as pl
from jax.experimental.pallas import tpu as pltpu
from jax.sharding import PartitionSpec as P

MEMBERS = 512
STATES = 16384
WINDOW = 4096
ROWS = 8
COLS = 16
BLOCK = 1024
PIECE = 128
SUB = 256
SPAN = SUB + BLOCK
STEPS = 3
MESH = pl.DeviceIdType.MESH
VMEM_LIMIT = 58 * 2**20

epsilon = 1e-06
power_terms = (
    2.0 / math.pi - 4.0 / (3.0 * math.pi) - 4.0 / (15.0 * math.pi) - 4.0 / (35.0 * math.pi),
    8.0 / (3.0 * math.pi) + 32.0 / (15.0 * math.pi) + 72.0 / (35.0 * math.pi),
    -32.0 / (15.0 * math.pi) - 192.0 / (35.0 * math.pi),
    128.0 / (35.0 * math.pi),
)

ROUTES = (
    (0x8e4662f1386c2e0b028f46e28008742a0d00000000000874220d00000000000874260f01, 0x8ec662d100000000008e46e2f100000000008e4662f1186c2c01008f46a2b10004220d02, 0x8f466291386c2a0b028f46e291386c2e09028fc62291387c260b028ec66291186c2e0d03, 0x8f4622b1187c220d02004662f1187c2e0f038fc6e2d108642a0b038e4662d1386c220b00, 0x46e29110000000008ec6c0000004220f000046a2e00874220f010046a2f11864260901, 0x8ec662d12000020f010046a2b12000020b030046229118780001038e80000008742e0b03),
    (0x8fc6a2c00874220d010000000008642e0f0200000000086c260f030000000008642e0b02, 0x8fc6229120000000008ec6a2b120000000008f4622b100000000008e4662913004280100, 0x8fc6a2f1187c220f018fc6001118642a0f018e46e2f108642a0d008fc600110004240101, 0x8e46a2f1386c2e0f0000462291386c220b008ec622f1287c2209018f46229128642a0901, 0x4622b120000000000046000000042a0d010000000000042a09030046400000042e0a00, 0x8fc6a2913000020d00004622d130000001010046a2b13860000000000000000878020f01),
    (0x86c6e0a008642a110087000000081c3e4f2100000000084c2a150f00426e97186c1a0903, 0x8e46a2b15006af4ba38dfea33130000001e188453ef16f6002040089c62231d97c362b05, 0x8e46e2b108542e09008746a6d3285c120b03874662d12f642fc9018e46e6912004680100, 0x46631028ec3fcf0388c6e0d1786427cf21884666b118e43215028ec6e2f118f4360d02, 0x88fee2710ce6672fe088c67ee008e46e0510c6800011f81c660d11004630d8285c220f0d, 0x8f4522b11d76ac01039ec2a2f000066e1710004ea0d108e0024a00004e30d828041a110d),
    (0xdec6000008542609038c000000086c364d200045c0000854164b0c00002eb7287c320d00, 0x89c6e2f1e000034fa18fc6227140000000008fc6e27120000001108fc6e2d1684c661510, 0x874622312004260d0386464011e8e41fc9008f46a6d3286c222f238cc6a6b3184c640102, 0x46e0d1281427cd019fc2e6910cf43e09200046a29138f42611000046a6b1087c2e1503, 0x877e20d02cfe6b2d93000000000cf43e031200000018084c1601050046c01808e42a1113, 0x86c5e0b108400001020042e0f1f0000210000000237128f0020104006280180960000113),
    (0x42e10008441e17e78d43e3731824261123848026f6285c72033000002e77085e2611f1, 0x88f62271f0069b51158bc523111e772e33f18ec5a371cf5eee19ec894d2211f80c621b04, 0x8c802211e85c17c4008e4da4f0e8dfe60d128ecaa6b0ef5f93cb038f0024d1d00463ee00, 0x24d10c6c2a08009efea4f618efebcde7aec226f3386c2fce00888022b1689c7be800, 0x8642a2318fe66f0bf081cd801fff1c6a1302b60030535884622b16b8dec01858d4362b06, 0x42a2f1fd066e1fa39f4663311c700329e70045a150f85f925600d7e372b859e0022323),
    (0x422210387c1213e6004d8012087c1609e5854aecd608447a472100002cd6284c3e4140, 0x89452230ee600000008f46623170067bc000897ea211e0000202008de222f1c89802071d, 0x860024b01fe7efc2008ece66b21f77922b228c4da651c874522be187002631fffc1a2c00, 0x122876661000884364b148e437c901888024b3ffe43fee00880026933874240000, 0x814260901bf66001f28c8000134f7416270d0000001908446e2712b75e31590fe43e2916, 0x426090ecfe63519396ce6170c900021314004da0f0c8fe5e5108004d715358cc6e8b24),
    (0x8445217e785c0a05939b4d21d3085c225f01af576033187c36090100002e378ae4121550, 0x8dc7a3595ee763620089c463d15e06ee31f68dc7e1df1f200207e788cda2519818023d1f, 0x8d0026b0084f8b0a008cc9e6512fcc27cc0085cd62b208ec5fce008c002551300423e600, 0xa78026b068fc37d200a646a2d128bfa3f502af5762b3780c37d1e7000024d3180c4c0000, 0x8541e2519006371000b0c273327fcc322f1bb5c731962fe436371cb65ab1b848fc4e2d0a, 0x884aa171e89e3763a186c26110290e3f37c395002311dc4f96070d006231bf195c3e9600),
    (0xa7c26120084fa20e000043643238541a1f03a68024765a04320b3400002c9618043a0352, 0x8f7562117e1eec010e88c42291df26e2220088e2e2918ee7bf69eb8849a3b119fede2913, 0x8d8020303e67862c009ecd64d108f797ea0086cca4f30ee41a08008d8020f2fef7de2000, 0xa6002551480477e6000042a6d238ffabe600a7002572c8eff3ebf79980241148946bcc00, 0xfec43afdffde2f218382003f525f841a09e10047b03608a42e211ec4da4019d8c43a07f4, 0x9144231159ee2f33ad9ccd61b06e76d801a09fc7a251ed76af6feb99e6707908dc3a911c),
    (0x2f39382c1615fb004fe5f2783c760b22a7002bb22864060502b5002e5408445a0105, 0x8845e251cecebc00008c7f22d19ee797f51589fe62d13f3ebe1fe88b4c63f149f4da2119, 0x84002631fe7467e6008dcea491f854200000a64a64133ef4620e0086002772c004162e00, 0xa08025b15cffabd600a04ea491687433f7faa60025125817a7e800ae002771781433d000, 0xf1c120517f1617efe9938022571cc4762be7b24470767c547e130fb159f3d728f4060000, 0x85cb62317dce2321b393c7a090edb45f1db19b4ca330b8179e1db198e273d3dd4c5a2719),
    (0xe98023d05e1c361bf300416c56084c7204000053a5b348341a1305ae0000179834061706, 0x834563d8ee86b801bc8cffa211f007ee3df38d7e2251ffbe2fedf68ecaa331eef44a1716, 0x87cee471c8dc63c8008c4ee251cf4c17e0008dc526121e6c5a0000868024f33e742bcc00, 0xae00001178e7ebd000a14ee0f0081c2bea00ae0020f2688fea1600a5002553d8043fc800, 0xf240bb5e6f0f9b17959b49b31e5fa47e07e5b4cd6416c8bc761b18c0dc001788944a17e6, 0x8a496111cd7e163bbc9acea3d1c946d3a31d96436110d8047703f5c9cfb298488c061328),
    (0x838020191a4ff61e00004ca3f70b54131c00a1556d57d814de1723a5002c550a14165d49, 0x8a507e5dfe77576600887c7ef0eecfb79000007ee3917fc75bf8008a4de310ee76222fe8, 0x84800010ee7c13ea008d4e2431d84c562c008ccbe692ceb457ea008d0022730f541fe200, 0xac8027d3581ff7f200a20024d02807e7d000a880249288747bbbf4af8024f3f8ffeaae00, 0xf8c061507c465313eb8a5032395cd42e1be6b3c06fd68fd4321de6a1d900179834420400, 0x84c0a1518dde9b67b9984460d1bdfeb75f1992c9e0916f24dff9dcc1e63219d8b4d23514),
    (0xe8d720751a9c7753e80049a3942aec1e1200aad32db4ca0c1e073dae8000152a0c0a05ce, 0x8af7a3f0cea6db52008a44a3906e7eb772000046a35148b7535c008be2a37189072e2511, 0x86802690c8cfbff20086c923f338446bd2008d482491f84c13e800878026503ee003c800, 0xa8002692a89467c800ae00211068f7e3c400a00026d0081c47d200a1802710181fefd600, 0x897e63ffbbc6273d6785d961d47fbc2629f2bbd331f708943e29f1b5588019f8840a1f1e, 0x99cd63d0cd8eef538591cde311899e3743b399c820b038ef7747c0dfe4b179f82fce3b15),
    (0xa4d660f75c3c3a3b85000023b40844320600004defd70a440a5339af802d57783c5e470a, 0x8bc421dd5e5e8774008978637ffed6afa600000023115ff7377600006371b12004de3f4b, 0x8500261228c797c60087802bd23e7c1bc400844c2671df7417e200858025f1ee5003e000, 0xe1800012d86463d400a3d125701f3ff3d400898024f1689fbb9e009e80273028ec3bf400, 0x837a61bf3c3d0701f9b55eec548f3c1e2df9bc57a4364ffc522d1da1584011bfbc5e21e4, 0x9acc6131bdb6b801b49d422351a006af3fb097cfa051c8dfd79fdedf6db2f939149a190e),
    (0x2f1e880f700000ab802d94782c5e4400005700164824020000ab002ff46824021800, 0x8b5421914ebf537a008b0023516f96a3600000002331bf36b400000064801209ee2a1f18, 0xaa0026720f7fb3da00850026720ed003dc0083456590ce7467cc0084802590eec003e400, 0xa18025300fe7efc600ab8020b4880fffda009f8021303f67e7de009f8025d038e7e7d200, 0x82fa23927bd67f078eb2512c170f446221fccb53aed6b8ac0225eaa080001990040227ea, 0x91c8e1b08d2ed801b595c1a150d006ff39a39acc213178375b5ba2d000325ce004c63318),
    (0xa5002e3288247c01f500002c34c8ac3a1800000000152a9c3e1e00a2002db67add1a1f59, 0x3dd1ae3e4f59ae000023f18efe940000000023f19f872f7e0000000012b9de360200, 0x858028400f2c6be40096802473fed803ee008541e5d1ee141fec0084002513deec57de00, 0xa4802570389c6ff400ad002540089ffbee00910027d17897e3f5cfa88024915f57e3f600, 0xfcff61dc5007670f8583db61f168fc52011eb0dbef976f940e0be5b90033f680047e25eb, 0x954d2390f0068759ae9dc761f0f006a33ba796cd217018c6de39cd006df3f990040a312d),
    (0xc38021985a8c00000000002c7480040e7a0000000015882c121a00a6002f94982c7e3800, 0x1dde477b7200000023b1aedf180000000023bfbeb77f7800000000117ec6874200, 0xab8027a00e4803ec009d002052eef803ec00820022531ef803c600838025d3eef803c400, 0xa7002740080ffffa00a48027200817f7e800918025301ff7ee3400a28024400f40023400, 0xfa70f5200005400168b94b2f576f2c3a19febf480012bfa44e170bb30000000004763b18, 0x96cca19090000001b89a472050a0061401dc9bc922d1a0073b83b4de8031f96934aa3757),
    (0x1f50040c0000000031d5000458000000002ff590043a2200a2802dd5b8540e7800, 0x3dff6e171b700000000010fe8f6c0000000000106e7f237a0000000010c9c7bf1a00, 0x9d8028000f6003e000848029000eb803e400000020600ea800000082002492ded003fc00, 0xa98026e0088c73e800af8000000000039200908000000000038200a08025200f3803ae00, 0xf5f7000000000001a8b6d733d3dfd40239fbb357001240000223fdb280000000000001fa, 0x4c000000000000009c4cc00000069799a59940a3f0800757bbdddd8030391004f61d20),
    (0x15400448000000002df4400000000000000017f000000000a08000153004540000, 0xe37477600000000000eb7380000000000000efe9400000000001cbed6480000, 0x25800e5003e200000020200e90000000000000000eb8000000000024a00eb003c000, 0xaf802640000003f000ac800000000003d800000000000000000000a98000000000023600, 0xf38000000000031800bb57a8936fac7801f8b854400000000001fe000000000000000112, 0x94c8c0000006c8000094c000000007d001d60000001980055c012b),
    (0x2fd6e00000000000000014b000000000000000179000000000a78000187004e40000, 0x11de2e8b5c00000000000e2f580000000000000ebf1400000000000000075c0000, 0x2b400ff800000000002a600000000000000000000000000000000025200e2003c600, 0xa5802580000003e200ae8000000000000000a78000000000000000a78000000000038600, 0x1750051ead730000001e20050000000000000000000000000000001e9, 0x920000000006980000934b000000073001ccdc5bc0000000000000),
    (0x150000000000000000156000000000000000148000000000000000159000000000, 0x116ed7280000000000000e97040000000000000007480000000000000006c00000, 0xed0000000000000000000000000000000000000000000000025600e6003c200, 0xa20025e00000000000ac0000000000000000000000000000000000aa8000000000039a00, 0x55eb924000000000004cc00000000000000000000000000001fb, 0x7c00000944880000007c401cf000000000000000000),
    (0x157000000000000000000000000000000000000000000000000000000000000000, 0xeaf740000000000000ea0000000000000000007180000000000000000000000, 0xe28000000, 0xa38000000000000000000000000000000000000000000000000000a68000000000000000, 0x56800000000000000053c0000000000000000000000000000000, 0x904b800000077001ef000000000000000000),
    (0x156000000000000000000000000000000000000000000000000000000000000000, 0x0, 0xe08000000, 0xa90000000000000000000000000000000000000000000000000000000000000000000000, 0x57c0000000000000000000000000000000000000000000000000, 0x980000000000000000000000000000000000),
    (0x153000000000000000000000000000000000000000000000000000000000000000, 0x0, 0xe78000000, 0xa40000000000000000000000000000000000000000000000000000000000000000000000, 0x0, 0x0),
)


def here():
    return lax.axis_index("row"), lax.axis_index("col")


def at(row, col):
    return {"row": row, "col": col}


def reached(r, c):
    found = []
    for panel in range(2):
        for row in range(ROWS):
            col = lax.rem(c + (4 - panel) - row + 2 * COLS, COLS)
            own = (r == row) if row == 4 - panel else None
            found.append((row, col, panel, own))
    return found


def unless(own, step):
    if own is None:
        step()
    else:
        pl.when(jnp.logical_not(own))(step)


def copied(src, dst, send, recv, row, col):
    return pltpu.make_async_remote_copy(
        src_ref=src, dst_ref=dst, send_sem=send, recv_sem=recv,
        device_id=at(row, col), device_id_type=MESH,
    )


DIRECTIONS = ((1, 0, 0), (-1, 0, 0), (0, 1, 0), (0, -1, 0), (0, 0, 1), (0, 0, -1))
QUARTER = MEMBERS // ROWS // 4
LAG = 2


def place_of(i):
    return (i % 8) // 4, i % 4, i // 8


def arrivals():
    table = []
    for sends in ROUTES:
        by_direction = []
        for (dx, dy, dz), packed in zip(DIRECTIONS, sends):
            entries = []
            for i in range(32):
                x, y, z = place_of(i)
                fx, fy, fz = (x - dx) % 4, (y - dy) % 4, (z - dz) % 4
                entry = packed >> (9 * (fz * 8 + (fx % 2) * 4 + fy)) & 511
                if entry:
                    pair = (fx // 2) * 4 + fz + (entry >> 5 & 7)
                    entry = 256 | (pair - z) % 8 << 5 | entry & 31
                entries.append(entry)
            by_direction.append(entries)
        table.append(by_direction)
    return table


def departures():
    return [[[packed >> (9 * i) & 511 for i in range(32)] for packed in sends] for sends in ROUTES]


def words(table):
    return [
        [[d[i] | e[i] << 9 | f[i] << 18 for i in range(32)] for d, e, f in (sends[:3], sends[3:])]
        for sends in table
    ]


def looked_up(values, bits):
    if len(set(values)) == 1:
        return jnp.int32(values[0])
    low = looked_up(values[: len(values) // 2], bits[:-1])
    high = looked_up(values[len(values) // 2 :], bits[:-1])
    return jnp.where(bits[-1], high, low)


def gather_kernel(x_ref, out_ref, send, recv, across_send, across_recv, own_sem):
    r, c = here()
    core = lax.rem(c, 2)
    pair = lax.div(c, 2)
    z = lax.rem(pair, 4)
    x = lax.div(pair, 4) * 2 + lax.div(r, 4)
    y = lax.rem(r, 4)
    first = core == 0
    sign = 1 - 2 * core
    index = jnp.where(first, z * 8 + r, (3 - z) * 8 + 7 - r)
    bits = [lax.rem(lax.div(index, 2**b), 2) == 1 for b in range(5)]

    def neighbour(direction):
        dx, dy, dz = DIRECTIONS[direction]
        nx, ny, nz = (lax.rem(v + sign * d + 4, 4) for v, d in ((x, dx), (y, dy), (z, dz)))
        return lax.rem(nx, 2) * 4 + ny, lax.div(nx, 2) * 8 + nz * 2 + core

    sides = [neighbour(d) for d in range(6)]
    other = (r, c + sign)

    across = lax.rem(2 * pair - 4 + r + 2 - core - lax.rem(r, 2) + COLS, COLS)

    own = pltpu.make_async_copy(x_ref, out_ref.at[c, r], own_sem)
    own.start()
    barrier = pltpu.get_barrier_semaphore()
    for row, col in sides + [other]:
        pl.semaphore_signal(barrier, inc=1, device_id=at(row, col), device_id_type=MESH)
    pl.semaphore_wait(barrier, 7)
    own.wait()

    def unit(entry):
        relative = lax.rem(lax.div(entry, 32), 8)
        row = lax.rem(lax.div(entry, 4), 8)
        block = lax.rem(pair + sign * relative + 8, 8) * 2 + core
        row = jnp.where(first, row, 7 - row)
        quarter = pl.multiple_of(lax.rem(entry, 4) * QUARTER, QUARTER)
        return block, out_ref.at[block, row, pl.ds(quarter, QUARTER)]

    def entries(table):
        found = []
        for word in table:
            word = looked_up(word, bits)
            found += [lax.rem(word, 512), lax.rem(lax.div(word, 512), 512), lax.div(word, 512 * 512)]
        return found

    whole = out_ref.at[c, r]
    piece = out_ref.at[c, r, pl.ds(0, QUARTER)]

    def pass_across(block, ref):
        @pl.when(block == across)
        def _():
            copied(ref, ref, across_send, across_recv, *other).start()

    def take(step):
        for d, entry in enumerate(entries(incoming[step])):
            @pl.when(entry >= 256)
            def _(d=d, entry=entry):
                block, ref = unit(entry)
                pltpu.make_async_copy(ref, ref, recv.at[step, d]).wait()
                pass_across(block, ref)

    incoming, outgoing = words(arrivals()), words(departures())
    pass_across(c, whole)
    rounds = len(ROUTES)
    for step in range(rounds + LAG):
        if step >= LAG:
            take(step - LAG)
        if step < rounds:
            for d, entry in enumerate(entries(outgoing[step])):
                @pl.when(entry >= 256)
                def _(d=d, entry=entry):
                    _, ref = unit(entry)
                    copied(ref, ref, send.at[step, d], recv.at[step, d], *sides[d]).start()
    for step in range(rounds):
        for d, entry in enumerate(entries(outgoing[step])):
            @pl.when(entry >= 256)
            def _(d=d):
                copied(piece, piece, send.at[step, d], recv.at[step, d], *sides[d]).wait_send()
    block = out_ref.at[c]
    sent = copied(block, block, across_send, across_recv, *other)
    sent.wait_send()
    sent.wait_recv()


def gathered(block):
    rounds = len(ROUTES)
    return pl.pallas_call(
        gather_kernel,
        name="gather_members",
        out_shape=jax.ShapeDtypeStruct((COLS, ROWS, MEMBERS // ROWS, BLOCK), jnp.float32),
        in_specs=[pl.BlockSpec(memory_space=pl.ANY)],
        out_specs=pl.BlockSpec(memory_space=pl.ANY),
        scratch_shapes=[
            pltpu.SemaphoreType.DMA((rounds, 6)),
            pltpu.SemaphoreType.DMA((rounds, 6)),
            pltpu.SemaphoreType.DMA,
            pltpu.SemaphoreType.DMA,
            pltpu.SemaphoreType.DMA,
        ],
        compiler_params=pltpu.CompilerParams(collective_id=1, has_side_effects=True),
    )(block)


def parted(values):
    high = values.astype(jnp.bfloat16)
    low = (values - high.astype(jnp.float32)).astype(jnp.bfloat16)
    return high, low


def dotted(a, b, dims):
    return lax.dot_general(a, b, (dims, ((), ())), preferred_element_type=jnp.float32)


def skewed(rows, shift):
    sub = lax.broadcasted_iota(jnp.int32, rows.shape, 0)
    if shift:
        rows = pltpu.roll(rows, SPAN - shift, 1)
    for bit in (1, 2, 4):
        rows = jnp.where((sub & bit) != 0, pltpu.roll(rows, SPAN - bit, 1), rows)
    return rows[:, :BLOCK]


def band_kernel(all_ref, local_ref, high_ref, low_ref, square_ref, x_ref, xh, xl, sems):
    r, c = here()
    loads = []
    for panel, block in enumerate((c, lax.rem(c + r - 4 + COLS, COLS), lax.rem(c + r - 3 + COLS, COLS))):
        loads.append(pltpu.make_async_copy(all_ref.at[block], x_ref.at[panel], sems.at[panel]))
        loads[-1].start()
    for panel in range(3):
        loads[panel].wait()
        for first in range(0, BLOCK, SUB):
            values = x_ref[panel, :, first : first + SUB]
            centered = values - jnp.sum(values, 0, keepdims=True) / MEMBERS
            spread = jnp.sqrt(jnp.sum(centered * centered, 0, keepdims=True) + epsilon)
            high, low = parted(centered / spread)
            lo_at = (panel - 1) * BLOCK + first if panel else 2 * BLOCK + first
            xh[:, lo_at : lo_at + SUB] = high
            xl[:, lo_at : lo_at + SUB] = low
    squares = jnp.zeros((8, 128), jnp.float32)
    gap = lax.broadcasted_iota(jnp.int32, (SUB, SPAN), 1) - lax.broadcasted_iota(jnp.int32, (SUB, SPAN), 0)
    taper = jnp.maximum(0.0, 1.0 - jnp.abs(gap + (r * BLOCK - WINDOW)).astype(jnp.float32) / WINDOW)
    taper = jnp.where((gap >= 0) & (gap < BLOCK), taper, 0.0)
    for tile in range(BLOCK // SUB):
        first = tile * SUB
        rows_h = xh[:, 2 * BLOCK + first : 2 * BLOCK + first + SUB]
        rows_l = xl[:, 2 * BLOCK + first : 2 * BLOCK + first + SUB]
        cols_h = xh[:, first : first + SPAN]
        cols_l = xl[:, first : first + SPAN]
        over = ((0,), (0,))
        gram = dotted(rows_h, cols_h, over) + (dotted(rows_h, cols_l, over) + dotted(rows_l, cols_h, over))
        band = gram * taper
        high, low = parted(band)
        high_ref[tile] = high
        low_ref[tile] = low
        squares = squares + jnp.sum((band * band).reshape(SUB // 8, 8, SPAN // 128, 128), (0, 2))
        for group in range(0, SUB, 8):
            local_ref[first + group : first + group + 8, :] = skewed(band[group : group + 8, :], group)
    square_ref[...] = squares


def banded(panels):
    return pl.pallas_call(
        band_kernel,
        name="band",
        out_shape=(
            jax.ShapeDtypeStruct((BLOCK, BLOCK), jnp.float32),
            jax.ShapeDtypeStruct((BLOCK // SUB, SUB, SPAN), jnp.bfloat16),
            jax.ShapeDtypeStruct((BLOCK // SUB, SUB, SPAN), jnp.bfloat16),
            jax.ShapeDtypeStruct((8, 128), jnp.float32),
        ),
        in_specs=[pl.BlockSpec(memory_space=pl.ANY)],
        out_specs=[pl.BlockSpec(memory_space=pltpu.VMEM)] * 4,
        scratch_shapes=[
            pltpu.VMEM((3, MEMBERS, BLOCK), jnp.float32),
            pltpu.VMEM((MEMBERS, 3 * BLOCK), jnp.bfloat16),
            pltpu.VMEM((MEMBERS, 3 * BLOCK), jnp.bfloat16),
            pltpu.SemaphoreType.DMA((3,)),
        ],
        compiler_params=pltpu.CompilerParams(vmem_limit_bytes=VMEM_LIMIT),
    )(panels)


def product_kernel(
    w_ref, high_ref, low_ref, square_ref, out_ref,
    iterate, window, wide, parts, sums, row_squares, col_squares, row_total,
    send_w, recv_w, send_y, recv_y, send_r, recv_r, send_c, recv_c,
):
    r, c = here()
    barrier = pltpu.get_barrier_semaphore()
    for shift in range(1, ROWS):
        pl.semaphore_signal(barrier, inc=1, device_id=at(lax.rem(r + shift, ROWS), c), device_id_type=MESH)
    for shift in range(1, COLS):
        pl.semaphore_signal(barrier, inc=1, device_id=at(r, lax.rem(c + shift, COLS)), device_id_type=MESH)
    for panel in range(2):
        block = lax.rem(c + r - 4 + panel + COLS, COLS)
        for row in range(ROWS):
            own = (r == row) if row == 4 - panel else None

            def greet(row=row, block=block):
                pl.semaphore_signal(barrier, inc=1, device_id=at(row, block), device_id_type=MESH)

            unless(own, greet)
    pl.semaphore_wait(barrier, 7 + 15 + 16 - jnp.where((r == 3) | (r == 4), 1, 0))

    def send_iterate(step, source):
        for row, col, panel, own in reached(r, c):
            def go(row=row, col=col, panel=panel):
                copied(source, window.at[step, panel, r], send_w.at[step, panel, row], recv_w.at[step, panel, r], row, col).start()

            unless(own, go)
            if own is not None:
                @pl.when(own)
                def _(panel=panel):
                    pltpu.make_async_copy(source, window.at[step, panel, r], recv_w.at[step, panel, r]).start()

    for shift in range(1, ROWS):
        copied(square_ref, row_squares.at[r], send_r.at[shift], recv_r.at[r], lax.rem(r + shift, ROWS), c).start()
    pltpu.make_async_copy(square_ref, row_squares.at[r], recv_r.at[r]).start()
    send_iterate(0, w_ref)
    for row in range(ROWS):
        pltpu.make_async_copy(square_ref, row_squares.at[row], recv_r.at[row]).wait()
    row_total[...] = jnp.sum(row_squares[...], 0)
    for shift in range(1, COLS):
        copied(row_total, col_squares.at[c], send_c.at[shift], recv_c.at[c], r, lax.rem(c + shift, COLS)).start()
    pltpu.make_async_copy(row_total, col_squares.at[c], recv_c.at[c]).start()

    total = None
    summed = power_terms[0] * w_ref[...]
    for step in range(STEPS):
        for panel in range(2):
            for row in range(ROWS):
                pltpu.make_async_copy(w_ref, window.at[step, panel, row], recv_w.at[step, panel, row]).wait()
                high, low = parted(window[step, panel, row])
                first = (panel * ROWS + row) * PIECE
                wide[first : first + PIECE, :PIECE] = high
                wide[first : first + PIECE, PIECE:] = low
        for tile in range(BLOCK // SUB):
            first = tile * SUB
            over = ((1,), (0,))
            both = dotted(high_ref[tile], wide[first : first + SPAN, :], over)
            rest = dotted(low_ref[tile], wide[first : first + SPAN, :PIECE], over)
            parts[step, first : first + SUB, :] = both[:, :PIECE] + (both[:, PIECE:] + rest)
            for row in range(first // PIECE, (first + SUB) // PIECE):
                def go(row=row):
                    copied(
                        parts.at[step, row * PIECE : (row + 1) * PIECE], sums.at[step, r],
                        send_y.at[step, row], recv_y.at[step, r], row, c,
                    ).start()

                unless(r == row, go)
        if step == 0:
            for col in range(COLS):
                pltpu.make_async_copy(row_total, col_squares.at[col], recv_c.at[col]).wait()
            total = jnp.sum(jnp.sum(col_squares[...], 0), keepdims=True) / STATES
        vector = parts[step, pl.ds(pl.multiple_of(r * PIECE, PIECE), PIECE), :]
        for row in range(ROWS):
            def landed(row=row):
                pltpu.make_async_copy(w_ref, sums.at[step, row], recv_y.at[step, row]).wait()

            unless(r == row, landed)
            vector = vector + jnp.where(r == row, 0.0, sums[step, row])
        vector = vector / total
        summed = summed + power_terms[step + 1] * vector
        if step < STEPS - 1:
            iterate[step] = vector
            send_iterate(step + 1, iterate.at[step])
    out_ref[...] = jnp.sqrt(total) * summed

    for shift in range(1, ROWS):
        copied(square_ref, row_squares.at[r], send_r.at[shift], recv_r.at[r], lax.rem(r + shift, ROWS), c).wait_send()
    for shift in range(1, COLS):
        copied(row_total, col_squares.at[c], send_c.at[shift], recv_c.at[c], r, lax.rem(c + shift, COLS)).wait_send()
    for step in range(STEPS):
        for row, col, panel, own in reached(r, c):
            def sent(row=row, col=col, panel=panel):
                copied(w_ref, window.at[step, panel, r], send_w.at[step, panel, row], recv_w.at[step, panel, r], row, col).wait_send()

            unless(own, sent)
        for row in range(ROWS):
            def gone(row=row):
                copied(w_ref, sums.at[step, r], send_y.at[step, row], recv_y.at[step, r], row, c).wait_send()

            unless(r == row, gone)


def sampler(probes, high, low, squares):
    return pl.pallas_call(
        product_kernel,
        name="products",
        out_shape=jax.ShapeDtypeStruct((PIECE, PIECE), jnp.float32),
        in_specs=[pl.BlockSpec(memory_space=pltpu.VMEM)] * 4,
        out_specs=pl.BlockSpec(memory_space=pltpu.VMEM),
        scratch_shapes=[
            pltpu.VMEM((STEPS - 1, PIECE, PIECE), jnp.float32),
            pltpu.VMEM((STEPS, 2, ROWS, PIECE, PIECE), jnp.float32),
            pltpu.VMEM((2 * BLOCK, 2 * PIECE), jnp.bfloat16),
            pltpu.VMEM((STEPS, BLOCK, PIECE), jnp.float32),
            pltpu.VMEM((STEPS, ROWS, PIECE, PIECE), jnp.float32),
            pltpu.VMEM((ROWS, 8, 128), jnp.float32),
            pltpu.VMEM((COLS, 8, 128), jnp.float32),
            pltpu.VMEM((8, 128), jnp.float32),
            pltpu.SemaphoreType.DMA((STEPS, 2, ROWS)),
            pltpu.SemaphoreType.DMA((STEPS, 2, ROWS)),
            pltpu.SemaphoreType.DMA((STEPS, ROWS)),
            pltpu.SemaphoreType.DMA((STEPS, ROWS)),
            pltpu.SemaphoreType.DMA((ROWS,)),
            pltpu.SemaphoreType.DMA((ROWS,)),
            pltpu.SemaphoreType.DMA((COLS,)),
            pltpu.SemaphoreType.DMA((COLS,)),
        ],
        compiler_params=pltpu.CompilerParams(
            collective_id=2, has_side_effects=True, vmem_limit_bytes=VMEM_LIMIT
        ),
    )(probes, high, low, squares)


def on_device(perturbations, probes):
    panels = gathered(perturbations).reshape(COLS, MEMBERS, BLOCK)
    localized, high, low, squares = banded(panels)
    return localized, sampler(probes, high, low, squares)


def solution(mesh):
    return jax.shard_map(
        on_device,
        mesh=mesh,
        in_specs=(P("row", "col"), P(("col", "row"), None)),
        out_specs=(P("col", "row"), P(("col", "row"), None)),
        check_vma=False,
    )
```

```python
import functools
import math

import jax
import jax.numpy as jnp
from jax import lax
from jax.experimental import pallas as pl
from jax.experimental.pallas import tpu as pltpu
from jax.sharding import PartitionSpec as P

MEMBERS = 512
STATES = 16384
WINDOW = 4096
ROWS = 8
COLS = 16
BLOCK = 1024
PIECE = 128
SUB = 256
SPAN = SUB + BLOCK
STEPS = 3
MESH = pl.DeviceIdType.MESH
VMEM_LIMIT = 58 * 2**20

epsilon = 1e-06
power_terms = (
    2.0 / math.pi - 4.0 / (3.0 * math.pi) - 4.0 / (15.0 * math.pi) - 4.0 / (35.0 * math.pi),
    8.0 / (3.0 * math.pi) + 32.0 / (15.0 * math.pi) + 72.0 / (35.0 * math.pi),
    -32.0 / (15.0 * math.pi) - 192.0 / (35.0 * math.pi),
    128.0 / (35.0 * math.pi),
)

ROUTES = (
    (0x8e4662f1386c2e0b028f46e28008742a0d00000000000874220d00000000000874260f01, 0x8ec662d100000000008e46e2f100000000008e4662f1186c2c01008f46a2b10004220d02, 0x8f466291386c2a0b028f46e291386c2e09028fc62291387c260b028ec66291186c2e0d03, 0x8f4622b1187c220d02004662f1187c2e0f038fc6e2d108642a0b038e4662d1386c220b00, 0x46e29110000000008ec6c0000004220f000046a2e00874220f010046a2f11864260901, 0x8ec662d12000020f010046a2b12000020b030046229118780001038e80000008742e0b03),
    (0x8fc6a2c00874220d010000000008642e0f0200000000086c260f030000000008642e0b02, 0x8fc6229120000000008ec6a2b120000000008f4622b100000000008e4662913004280100, 0x8fc6a2f1187c220f018fc6001118642a0f018e46e2f108642a0d008fc600110004240101, 0x8e46a2f1386c2e0f0000462291386c220b008ec622f1287c2209018f46229128642a0901, 0x4622b120000000000046000000042a0d010000000000042a09030046400000042e0a00, 0x8fc6a2913000020d00004622d130000001010046a2b13860000000000000000878020f01),
    (0x86c6e0a008642a110087000000081c3e4f2100000000084c2a150f00426e97186c1a0903, 0x8e46a2b15006af4ba38dfea33130000001e188453ef16f6002040089c62231d97c362b05, 0x8e46e2b108542e09008746a6d3285c120b03874662d12f642fc9018e46e6912004680100, 0x46631028ec3fcf0388c6e0d1786427cf21884666b118e43215028ec6e2f118f4360d02, 0x88fee2710ce6672fe088c67ee008e46e0510c6800011f81c660d11004630d8285c220f0d, 0x8f4522b11d76ac01039ec2a2f000066e1710004ea0d108e0024a00004e30d828041a110d),
    (0xdec6000008542609038c000000086c364d200045c0000854164b0c00002eb7287c320d00, 0x89c6e2f1e000034fa18fc6227140000000008fc6e27120000001108fc6e2d1684c661510, 0x874622312004260d0386464011e8e41fc9008f46a6d3286c222f238cc6a6b3184c640102, 0x46e0d1281427cd019fc2e6910cf43e09200046a29138f42611000046a6b1087c2e1503, 0x877e20d02cfe6b2d93000000000cf43e031200000018084c1601050046c01808e42a1113, 0x86c5e0b108400001020042e0f1f0000210000000237128f0020104006280180960000113),
    (0x42e10008441e17e78d43e3731824261123848026f6285c72033000002e77085e2611f1, 0x88f62271f0069b51158bc523111e772e33f18ec5a371cf5eee19ec894d2211f80c621b04, 0x8c802211e85c17c4008e4da4f0e8dfe60d128ecaa6b0ef5f93cb038f0024d1d00463ee00, 0x24d10c6c2a08009efea4f618efebcde7aec226f3386c2fce00888022b1689c7be800, 0x8642a2318fe66f0bf081cd801fff1c6a1302b60030535884622b16b8dec01858d4362b06, 0x42a2f1fd066e1fa39f4663311c700329e70045a150f85f925600d7e372b859e0022323),
    (0x422210387c1213e6004d8012087c1609e5854aecd608447a472100002cd6284c3e4140, 0x89452230ee600000008f46623170067bc000897ea211e0000202008de222f1c89802071d, 0x860024b01fe7efc2008ece66b21f77922b228c4da651c874522be187002631fffc1a2c00, 0x122876661000884364b148e437c901888024b3ffe43fee00880026933874240000, 0x814260901bf66001f28c8000134f7416270d0000001908446e2712b75e31590fe43e2916, 0x426090ecfe63519396ce6170c900021314004da0f0c8fe5e5108004d715358cc6e8b24),
    (0x8445217e785c0a05939b4d21d3085c225f01af576033187c36090100002e378ae4121550, 0x8dc7a3595ee763620089c463d15e06ee31f68dc7e1df1f200207e788cda2519818023d1f, 0x8d0026b0084f8b0a008cc9e6512fcc27cc0085cd62b208ec5fce008c002551300423e600, 0xa78026b068fc37d200a646a2d128bfa3f502af5762b3780c37d1e7000024d3180c4c0000, 0x8541e2519006371000b0c273327fcc322f1bb5c731962fe436371cb65ab1b848fc4e2d0a, 0x884aa171e89e3763a186c26110290e3f37c395002311dc4f96070d006231bf195c3e9600),
    (0xa7c26120084fa20e000043643238541a1f03a68024765a04320b3400002c9618043a0352, 0x8f7562117e1eec010e88c42291df26e2220088e2e2918ee7bf69eb8849a3b119fede2913, 0x8d8020303e67862c009ecd64d108f797ea0086cca4f30ee41a08008d8020f2fef7de2000, 0xa6002551480477e6000042a6d238ffabe600a7002572c8eff3ebf79980241148946bcc00, 0xfec43afdffde2f218382003f525f841a09e10047b03608a42e211ec4da4019d8c43a07f4, 0x9144231159ee2f33ad9ccd61b06e76d801a09fc7a251ed76af6feb99e6707908dc3a911c),
    (0x2f39382c1615fb004fe5f2783c760b22a7002bb22864060502b5002e5408445a0105, 0x8845e251cecebc00008c7f22d19ee797f51589fe62d13f3ebe1fe88b4c63f149f4da2119, 0x84002631fe7467e6008dcea491f854200000a64a64133ef4620e0086002772c004162e00, 0xa08025b15cffabd600a04ea491687433f7faa60025125817a7e800ae002771781433d000, 0xf1c120517f1617efe9938022571cc4762be7b24470767c547e130fb159f3d728f4060000, 0x85cb62317dce2321b393c7a090edb45f1db19b4ca330b8179e1db198e273d3dd4c5a2719),
    (0xe98023d05e1c361bf300416c56084c7204000053a5b348341a1305ae0000179834061706, 0x834563d8ee86b801bc8cffa211f007ee3df38d7e2251ffbe2fedf68ecaa331eef44a1716, 0x87cee471c8dc63c8008c4ee251cf4c17e0008dc526121e6c5a0000868024f33e742bcc00, 0xae00001178e7ebd000a14ee0f0081c2bea00ae0020f2688fea1600a5002553d8043fc800, 0xf240bb5e6f0f9b17959b49b31e5fa47e07e5b4cd6416c8bc761b18c0dc001788944a17e6, 0x8a496111cd7e163bbc9acea3d1c946d3a31d96436110d8047703f5c9cfb298488c061328),
    (0x838020191a4ff61e00004ca3f70b54131c00a1556d57d814de1723a5002c550a14165d49, 0x8a507e5dfe77576600887c7ef0eecfb79000007ee3917fc75bf8008a4de310ee76222fe8, 0x84800010ee7c13ea008d4e2431d84c562c008ccbe692ceb457ea008d0022730f541fe200, 0xac8027d3581ff7f200a20024d02807e7d000a880249288747bbbf4af8024f3f8ffeaae00, 0xf8c061507c465313eb8a5032395cd42e1be6b3c06fd68fd4321de6a1d900179834420400, 0x84c0a1518dde9b67b9984460d1bdfeb75f1992c9e0916f24dff9dcc1e63219d8b4d23514),
    (0xe8d720751a9c7753e80049a3942aec1e1200aad32db4ca0c1e073dae8000152a0c0a05ce, 0x8af7a3f0cea6db52008a44a3906e7eb772000046a35148b7535c008be2a37189072e2511, 0x86802690c8cfbff20086c923f338446bd2008d482491f84c13e800878026503ee003c800, 0xa8002692a89467c800ae00211068f7e3c400a00026d0081c47d200a1802710181fefd600, 0x897e63ffbbc6273d6785d961d47fbc2629f2bbd331f708943e29f1b5588019f8840a1f1e, 0x99cd63d0cd8eef538591cde311899e3743b399c820b038ef7747c0dfe4b179f82fce3b15),
    (0xa4d660f75c3c3a3b85000023b40844320600004defd70a440a5339af802d57783c5e470a, 0x8bc421dd5e5e8774008978637ffed6afa600000023115ff7377600006371b12004de3f4b, 0x8500261228c797c60087802bd23e7c1bc400844c2671df7417e200858025f1ee5003e000, 0xe1800012d86463d400a3d125701f3ff3d400898024f1689fbb9e009e80273028ec3bf400, 0x837a61bf3c3d0701f9b55eec548f3c1e2df9bc57a4364ffc522d1da1584011bfbc5e21e4, 0x9acc6131bdb6b801b49d422351a006af3fb097cfa051c8dfd79fdedf6db2f939149a190e),
    (0x2f1e880f700000ab802d94782c5e4400005700164824020000ab002ff46824021800, 0x8b5421914ebf537a008b0023516f96a3600000002331bf36b400000064801209ee2a1f18, 0xaa0026720f7fb3da00850026720ed003dc0083456590ce7467cc0084802590eec003e400, 0xa18025300fe7efc600ab8020b4880fffda009f8021303f67e7de009f8025d038e7e7d200, 0x82fa23927bd67f078eb2512c170f446221fccb53aed6b8ac0225eaa080001990040227ea, 0x91c8e1b08d2ed801b595c1a150d006ff39a39acc213178375b5ba2d000325ce004c63318),
    (0xa5002e3288247c01f500002c34c8ac3a1800000000152a9c3e1e00a2002db67add1a1f59, 0x3dd1ae3e4f59ae000023f18efe940000000023f19f872f7e0000000012b9de360200, 0x858028400f2c6be40096802473fed803ee008541e5d1ee141fec0084002513deec57de00, 0xa4802570389c6ff400ad002540089ffbee00910027d17897e3f5cfa88024915f57e3f600, 0xfcff61dc5007670f8583db61f168fc52011eb0dbef976f940e0be5b90033f680047e25eb, 0x954d2390f0068759ae9dc761f0f006a33ba796cd217018c6de39cd006df3f990040a312d),
    (0xc38021985a8c00000000002c7480040e7a0000000015882c121a00a6002f94982c7e3800, 0x1dde477b7200000023b1aedf180000000023bfbeb77f7800000000117ec6874200, 0xab8027a00e4803ec009d002052eef803ec00820022531ef803c600838025d3eef803c400, 0xa7002740080ffffa00a48027200817f7e800918025301ff7ee3400a28024400f40023400, 0xfa70f5200005400168b94b2f576f2c3a19febf480012bfa44e170bb30000000004763b18, 0x96cca19090000001b89a472050a0061401dc9bc922d1a0073b83b4de8031f96934aa3757),
    (0x1f50040c0000000031d5000458000000002ff590043a2200a2802dd5b8540e7800, 0x3dff6e171b700000000010fe8f6c0000000000106e7f237a0000000010c9c7bf1a00, 0x9d8028000f6003e000848029000eb803e400000020600ea800000082002492ded003fc00, 0xa98026e0088c73e800af8000000000039200908000000000038200a08025200f3803ae00, 0xf5f7000000000001a8b6d733d3dfd40239fbb357001240000223fdb280000000000001fa, 0x4c000000000000009c4cc00000069799a59940a3f0800757bbdddd8030391004f61d20),
    (0x15400448000000002df4400000000000000017f000000000a08000153004540000, 0xe37477600000000000eb7380000000000000efe9400000000001cbed6480000, 0x25800e5003e200000020200e90000000000000000eb8000000000024a00eb003c000, 0xaf802640000003f000ac800000000003d800000000000000000000a98000000000023600, 0xf38000000000031800bb57a8936fac7801f8b854400000000001fe000000000000000112, 0x94c8c0000006c8000094c000000007d001d60000001980055c012b),
    (0x2fd6e00000000000000014b000000000000000179000000000a78000187004e40000, 0x11de2e8b5c00000000000e2f580000000000000ebf1400000000000000075c0000, 0x2b400ff800000000002a600000000000000000000000000000000025200e2003c600, 0xa5802580000003e200ae8000000000000000a78000000000000000a78000000000038600, 0x1750051ead730000001e20050000000000000000000000000000001e9, 0x920000000006980000934b000000073001ccdc5bc0000000000000),
    (0x150000000000000000156000000000000000148000000000000000159000000000, 0x116ed7280000000000000e97040000000000000007480000000000000006c00000, 0xed0000000000000000000000000000000000000000000000025600e6003c200, 0xa20025e00000000000ac0000000000000000000000000000000000aa8000000000039a00, 0x55eb924000000000004cc00000000000000000000000000001fb, 0x7c00000944880000007c401cf000000000000000000),
    (0x157000000000000000000000000000000000000000000000000000000000000000, 0xeaf740000000000000ea0000000000000000007180000000000000000000000, 0xe28000000, 0xa38000000000000000000000000000000000000000000000000000a68000000000000000, 0x56800000000000000053c0000000000000000000000000000000, 0x904b800000077001ef000000000000000000),
    (0x156000000000000000000000000000000000000000000000000000000000000000, 0x0, 0xe08000000, 0xa90000000000000000000000000000000000000000000000000000000000000000000000, 0x57c0000000000000000000000000000000000000000000000000, 0x980000000000000000000000000000000000),
    (0x153000000000000000000000000000000000000000000000000000000000000000, 0x0, 0xe78000000, 0xa40000000000000000000000000000000000000000000000000000000000000000000000, 0x0, 0x0),
)


def here():
    return lax.axis_index("row"), lax.axis_index("col")


def at(row, col):
    return {"row": row, "col": col}


def unless(own, step):
    if own is None:
        step()
    else:
        pl.when(jnp.logical_not(own))(step)


def copied(src, dst, send, recv, row, col):
    return pltpu.make_async_remote_copy(
        src_ref=src, dst_ref=dst, send_sem=send, recv_sem=recv,
        device_id=at(row, col), device_id_type=MESH,
    )


DIRECTIONS = ((1, 0, 0), (-1, 0, 0), (0, 1, 0), (0, -1, 0), (0, 0, 1), (0, 0, -1))
QUARTER = MEMBERS // ROWS // 4
LAG = 2


def place_of(i):
    return (i % 8) // 4, i % 4, i // 8


def arrivals():
    table = []
    for sends in ROUTES:
        by_direction = []
        for (dx, dy, dz), packed in zip(DIRECTIONS, sends):
            entries = []
            for i in range(32):
                x, y, z = place_of(i)
                fx, fy, fz = (x - dx) % 4, (y - dy) % 4, (z - dz) % 4
                entry = packed >> (9 * (fz * 8 + (fx % 2) * 4 + fy)) & 511
                if entry:
                    pair = (fx // 2) * 4 + fz + (entry >> 5 & 7)
                    entry = 256 | (pair - z) % 8 << 5 | entry & 31
                entries.append(entry)
            by_direction.append(entries)
        table.append(by_direction)
    return table


def departures():
    return [[[packed >> (9 * i) & 511 for i in range(32)] for packed in sends] for sends in ROUTES]


def words(table):
    return [
        [[d[i] | e[i] << 9 | f[i] << 18 for i in range(32)] for d, e, f in (sends[:3], sends[3:])]
        for sends in table
    ]


def looked_up(values, bits):
    if len(set(values)) == 1:
        return jnp.int32(values[0])
    low = looked_up(values[: len(values) // 2], bits[:-1])
    high = looked_up(values[len(values) // 2 :], bits[:-1])
    return jnp.where(bits[-1], high, low)


def gather_kernel(x_ref, out_ref, send, recv, across_send, across_recv, own_sem):
    r, c = here()
    core = lax.rem(c, 2)
    pair = lax.div(c, 2)
    z = lax.rem(pair, 4)
    x = lax.div(pair, 4) * 2 + lax.div(r, 4)
    y = lax.rem(r, 4)
    first = core == 0
    sign = 1 - 2 * core
    index = jnp.where(first, z * 8 + r, (3 - z) * 8 + 7 - r)
    bits = [lax.rem(lax.div(index, 2**b), 2) == 1 for b in range(5)]

    def neighbour(direction):
        dx, dy, dz = DIRECTIONS[direction]
        nx, ny, nz = (lax.rem(v + sign * d + 4, 4) for v, d in ((x, dx), (y, dy), (z, dz)))
        return lax.rem(nx, 2) * 4 + ny, lax.div(nx, 2) * 8 + nz * 2 + core

    sides = [neighbour(d) for d in range(6)]
    other = (r, c + sign)

    across = lax.rem(2 * pair - 4 + r + 2 - core - lax.rem(r, 2) + COLS, COLS)

    own = pltpu.make_async_copy(x_ref, out_ref.at[c, r], own_sem)
    own.start()
    barrier = pltpu.get_barrier_semaphore()
    for row, col in sides + [other]:
        pl.semaphore_signal(barrier, inc=1, device_id=at(row, col), device_id_type=MESH)
    pl.semaphore_wait(barrier, 7)
    own.wait()

    def unit(entry):
        relative = lax.rem(lax.div(entry, 32), 8)
        row = lax.rem(lax.div(entry, 4), 8)
        block = lax.rem(pair + sign * relative + 8, 8) * 2 + core
        row = jnp.where(first, row, 7 - row)
        quarter = pl.multiple_of(lax.rem(entry, 4) * QUARTER, QUARTER)
        return block, out_ref.at[block, row, pl.ds(quarter, QUARTER)]

    def entries(table):
        found = []
        for word in table:
            word = looked_up(word, bits)
            found += [lax.rem(word, 512), lax.rem(lax.div(word, 512), 512), lax.div(word, 512 * 512)]
        return found

    whole = out_ref.at[c, r]
    piece = out_ref.at[c, r, pl.ds(0, QUARTER)]

    def pass_across(block, ref):
        @pl.when(block == across)
        def _():
            copied(ref, ref, across_send, across_recv, *other).start()

    def take(step):
        for d, entry in enumerate(entries(incoming[step])):
            @pl.when(entry >= 256)
            def _(d=d, entry=entry):
                block, ref = unit(entry)
                pltpu.make_async_copy(ref, ref, recv.at[step, d]).wait()
                pass_across(block, ref)

    incoming, outgoing = words(arrivals()), words(departures())
    pass_across(c, whole)
    rounds = len(ROUTES)
    for step in range(rounds + LAG):
        if step >= LAG:
            take(step - LAG)
        if step < rounds:
            for d, entry in enumerate(entries(outgoing[step])):
                @pl.when(entry >= 256)
                def _(d=d, entry=entry):
                    _, ref = unit(entry)
                    copied(ref, ref, send.at[step, d], recv.at[step, d], *sides[d]).start()
    for step in range(rounds):
        for d, entry in enumerate(entries(outgoing[step])):
            @pl.when(entry >= 256)
            def _(d=d):
                copied(piece, piece, send.at[step, d], recv.at[step, d], *sides[d]).wait_send()
    block = out_ref.at[c]
    sent = copied(block, block, across_send, across_recv, *other)
    sent.wait_send()
    sent.wait_recv()


def gathered(block):
    rounds = len(ROUTES)
    return pl.pallas_call(
        gather_kernel,
        name="gather_members",
        out_shape=jax.ShapeDtypeStruct((COLS, ROWS, MEMBERS // ROWS, BLOCK), jnp.float32),
        in_specs=[pl.BlockSpec(memory_space=pl.ANY)],
        out_specs=pl.BlockSpec(memory_space=pl.ANY),
        scratch_shapes=[
            pltpu.SemaphoreType.DMA((rounds, 6)),
            pltpu.SemaphoreType.DMA((rounds, 6)),
            pltpu.SemaphoreType.DMA,
            pltpu.SemaphoreType.DMA,
            pltpu.SemaphoreType.DMA,
        ],
        compiler_params=pltpu.CompilerParams(collective_id=1, has_side_effects=True),
    )(block)


def parted(values):
    high = values.astype(jnp.bfloat16)
    low = (values - high.astype(jnp.float32)).astype(jnp.bfloat16)
    return high, low


def dotted(a, b, dims):
    return lax.dot_general(a, b, (dims, ((), ())), preferred_element_type=jnp.float32)


def skewed(rows, shift):
    sub = lax.broadcasted_iota(jnp.int32, rows.shape, 0)
    if shift:
        rows = pltpu.roll(rows, SPAN - shift, 1)
    for bit in (1, 2, 4):
        rows = jnp.where((sub & bit) != 0, pltpu.roll(rows, SPAN - bit, 1), rows)
    return rows[:, :BLOCK]


def main_kernel(
    all_ref, w_ref, local_out, out_ref,
    x_ref, xh, xl, band_ref, high_ref, low_ref, local_ref,
    iterate, window, wide, parts, sums, square_ref, row_squares, col_squares, row_total,
    load_sem, store_sem, send_w, recv_w, send_x, send_y, recv_y, send_r, recv_r, send_c, recv_c,
):
    r, c = here()
    core = lax.rem(c, 2)
    pair = lax.div(c, 2)
    loads = []
    for panel, block in enumerate((c, lax.rem(c + r - 4 + COLS, COLS), lax.rem(c + r - 3 + COLS, COLS))):
        loads.append(pltpu.make_async_copy(all_ref.at[block], x_ref.at[panel], load_sem.at[panel]))
        loads[-1].start()

    other = (r, c + 1 - 2 * core)
    shared = 1 - core
    passes = core == lax.rem(r + 1, 2)

    def targets():
        found = []
        for s in range(4):
            row = 2 * s + core
            found.append((3 * s, row, lax.rem(pair + 2 - s + 8, 8) * 2, 0, (core == 0) & (r == 4) if s == 2 else None))
            found.append((3 * s + 1, row, lax.rem(pair + 1 - s + 8, 8) * 2 + 1, 1, (core == 1) & (r == 3) if s == 1 else None))
            row = 2 * s + 1 - core
            own = None
            if s in (1, 2):
                own = (core == s - 1) & (r == row)
            found.append((3 * s + 2, row, lax.rem(pair + 1 - s + core + 8, 8) * 2 + core, shared, own))
        return found

    barrier = pltpu.get_barrier_semaphore()

    def greet(row, col):
        pl.semaphore_signal(barrier, inc=1, device_id=at(row, col), device_id_type=MESH)

    for shift in range(1, ROWS):
        greet(lax.rem(r + shift, ROWS), c)
    for shift in range(1, COLS):
        greet(r, lax.rem(c + shift, COLS))
    greet(*other)
    outer = lax.rem(c + r - 4 + core + COLS, COLS)
    inner = lax.rem(c + r - 3 - core + COLS, COLS)
    for row in range(ROWS):
        unless((outer == c) & (r == row), lambda row=row: greet(row, outer))
        unless(jnp.logical_not(passes) | ((inner == c) & (r == row)), lambda row=row: greet(row, inner))
    pl.semaphore_wait(barrier, 7 + 15 + 1 + 12 - jnp.where((r == 3) | (r == 4), 1, 0))

    def send_iterate(step, source):
        for slot, row, col, panel, own in targets():
            def go(slot=slot, row=row, col=col, panel=panel):
                copied(source, window.at[step, panel, r], send_w.at[step, slot], recv_w.at[step, panel, r], row, col).start()

            unless(own, go)
            if own is not None:
                @pl.when(own)
                def _(panel=panel):
                    pltpu.make_async_copy(source, window.at[step, panel, r], recv_w.at[step, panel, r]).start()

    def take_iterate(step):
        @pl.when(passes)
        def _():
            for row in range(ROWS):
                block = window.at[step, shared, row]
                pltpu.make_async_copy(block, block, recv_w.at[step, shared, row]).wait()
                there = window.at[step, 1 - shared, row]
                copied(block, there, send_x.at[step, row], recv_w.at[step, 1 - shared, row], *other).start()
                split(step, shared, row)
        for row in range(ROWS):
            landed(step, core, row)
        @pl.when(jnp.logical_not(passes))
        def _():
            for row in range(ROWS):
                landed(step, shared, row)

    def split(step, panel, row):
        high, low = parted(window[step, panel, row])
        first = pl.multiple_of((panel * ROWS + row) * PIECE, PIECE)
        wide[pl.ds(first, PIECE), :PIECE] = high
        wide[pl.ds(first, PIECE), PIECE:] = low

    def landed(step, panel, row):
        block = window.at[step, panel, row]
        pltpu.make_async_copy(block, block, recv_w.at[step, panel, row]).wait()
        split(step, panel, row)

    send_iterate(0, w_ref)

    for panel in range(3):
        loads[panel].wait()
        for first in range(0, BLOCK, SUB):
            values = x_ref[panel, :, first : first + SUB]
            centered = values - jnp.sum(values, 0, keepdims=True) / MEMBERS
            spread = jnp.sqrt(jnp.sum(centered * centered, 0, keepdims=True) + epsilon)
            high, low = parted(centered / spread)
            lo_at = (panel - 1) * BLOCK + first if panel else 2 * BLOCK + first
            xh[:, lo_at : lo_at + SUB] = high
            xl[:, lo_at : lo_at + SUB] = low
    squares = jnp.zeros((8, 128), jnp.float32)
    gap = lax.broadcasted_iota(jnp.int32, (SUB, SPAN), 1) - lax.broadcasted_iota(jnp.int32, (SUB, SPAN), 0)
    taper = jnp.maximum(0.0, 1.0 - jnp.abs(gap + (r * BLOCK - WINDOW)).astype(jnp.float32) / WINDOW)
    taper = jnp.where((gap >= 0) & (gap < BLOCK), taper, 0.0)
    for tile in range(BLOCK // SUB):
        first = tile * SUB
        rows_h = xh[:, 2 * BLOCK + first : 2 * BLOCK + first + SUB]
        rows_l = xl[:, 2 * BLOCK + first : 2 * BLOCK + first + SUB]
        cols_h = xh[:, first : first + SPAN]
        cols_l = xl[:, first : first + SPAN]
        over = ((0,), (0,))
        gram = dotted(rows_h, cols_h, over) + (dotted(rows_h, cols_l, over) + dotted(rows_l, cols_h, over))
        band = gram * taper
        band_ref[tile] = band
        high, low = parted(band)
        high_ref[tile] = high
        low_ref[tile] = low
        squares = squares + jnp.sum((band * band).reshape(SUB // 8, 8, SPAN // 128, 128), (0, 2))
    square_ref[...] = squares

    for shift in range(1, ROWS):
        copied(square_ref, row_squares.at[r], send_r.at[shift], recv_r.at[r], lax.rem(r + shift, ROWS), c).start()
    pltpu.make_async_copy(square_ref, row_squares.at[r], recv_r.at[r]).start()

    stores = []

    def skew(tile):
        first = tile * SUB
        for group in range(0, SUB, 8):
            local_ref[first + group : first + group + 8, :] = skewed(band_ref[tile, group : group + 8, :], group)
        stores.append(pltpu.make_async_copy(local_ref.at[first : first + SUB], local_out.at[first : first + SUB], store_sem.at[tile]))
        stores[-1].start()

    total = None
    summed = power_terms[0] * w_ref[...]
    for step in range(STEPS):
        take_iterate(step)
        for tile in range(BLOCK // SUB):
            first = tile * SUB
            over = ((1,), (0,))
            both = dotted(high_ref[tile], wide[first : first + SPAN, :], over)
            rest = dotted(low_ref[tile], wide[first : first + SPAN, :PIECE], over)
            parts[step, first : first + SUB, :] = both[:, :PIECE] + (both[:, PIECE:] + rest)
            for row in range(first // PIECE, (first + SUB) // PIECE):
                def go(row=row):
                    copied(
                        parts.at[step, row * PIECE : (row + 1) * PIECE], sums.at[step, r],
                        send_y.at[step, row], recv_y.at[step, r], row, c,
                    ).start()

                unless(r == row, go)
        if step == 0:
            for row in range(ROWS):
                pltpu.make_async_copy(square_ref, row_squares.at[row], recv_r.at[row]).wait()
            row_total[...] = jnp.sum(row_squares[...], 0)
            for shift in range(1, COLS):
                copied(row_total, col_squares.at[c], send_c.at[shift], recv_c.at[c], r, lax.rem(c + shift, COLS)).start()
            pltpu.make_async_copy(row_total, col_squares.at[c], recv_c.at[c]).start()
        if step < 2:
            skew(2 * step)
        if step == 0:
            for col in range(COLS):
                pltpu.make_async_copy(row_total, col_squares.at[col], recv_c.at[col]).wait()
            total = jnp.sum(jnp.sum(col_squares[...], 0), keepdims=True) / STATES
        vector = parts[step, pl.ds(pl.multiple_of(r * PIECE, PIECE), PIECE), :]
        for row in range(ROWS):
            def arrived(row=row):
                pltpu.make_async_copy(w_ref, sums.at[step, row], recv_y.at[step, row]).wait()

            unless(r == row, arrived)
            vector = vector + jnp.where(r == row, 0.0, sums[step, row])
        vector = vector / total
        summed = summed + power_terms[step + 1] * vector
        if step < STEPS - 1:
            iterate[step] = vector
            send_iterate(step + 1, iterate.at[step])
            skew(2 * step + 1)
    out_ref[...] = jnp.sqrt(total) * summed

    for copy in stores:
        copy.wait()
    for shift in range(1, ROWS):
        copied(square_ref, row_squares.at[r], send_r.at[shift], recv_r.at[r], lax.rem(r + shift, ROWS), c).wait_send()
    for shift in range(1, COLS):
        copied(row_total, col_squares.at[c], send_c.at[shift], recv_c.at[c], r, lax.rem(c + shift, COLS)).wait_send()
    for step in range(STEPS):
        for slot, row, col, panel, own in targets():
            def sent(slot=slot, row=row, col=col, panel=panel):
                copied(w_ref, window.at[step, panel, r], send_w.at[step, slot], recv_w.at[step, panel, r], row, col).wait_send()

            unless(own, sent)
        @pl.when(passes)
        def _(step=step):
            for row in range(ROWS):
                copied(w_ref, window.at[step, core, row], send_x.at[step, row], recv_w.at[step, core, row], *other).wait_send()
        for row in range(ROWS):
            def gone(row=row):
                copied(w_ref, sums.at[step, r], send_y.at[step, row], recv_y.at[step, r], row, c).wait_send()

            unless(r == row, gone)


def band_and_sample(members, probes):
    return pl.pallas_call(
        main_kernel,
        name="band_and_sample",
        out_shape=(
            jax.ShapeDtypeStruct((BLOCK, BLOCK), jnp.float32),
            jax.ShapeDtypeStruct((PIECE, PIECE), jnp.float32),
        ),
        in_specs=[pl.BlockSpec(memory_space=pl.ANY), pl.BlockSpec(memory_space=pltpu.VMEM)],
        out_specs=[pl.BlockSpec(memory_space=pl.ANY), pl.BlockSpec(memory_space=pltpu.VMEM)],
        scratch_shapes=[
            pltpu.VMEM((3, MEMBERS, BLOCK), jnp.float32),
            pltpu.VMEM((MEMBERS, 3 * BLOCK), jnp.bfloat16),
            pltpu.VMEM((MEMBERS, 3 * BLOCK), jnp.bfloat16),
            pltpu.VMEM((BLOCK // SUB, SUB, SPAN), jnp.float32),
            pltpu.VMEM((BLOCK // SUB, SUB, SPAN), jnp.bfloat16),
            pltpu.VMEM((BLOCK // SUB, SUB, SPAN), jnp.bfloat16),
            pltpu.VMEM((BLOCK, BLOCK), jnp.float32),
            pltpu.VMEM((STEPS - 1, PIECE, PIECE), jnp.float32),
            pltpu.VMEM((STEPS, 2, ROWS, PIECE, PIECE), jnp.float32),
            pltpu.VMEM((2 * BLOCK, 2 * PIECE), jnp.bfloat16),
            pltpu.VMEM((STEPS, BLOCK, PIECE), jnp.float32),
            pltpu.VMEM((STEPS, ROWS, PIECE, PIECE), jnp.float32),
            pltpu.VMEM((8, 128), jnp.float32),
            pltpu.VMEM((ROWS, 8, 128), jnp.float32),
            pltpu.VMEM((COLS, 8, 128), jnp.float32),
            pltpu.VMEM((8, 128), jnp.float32),
            pltpu.SemaphoreType.DMA((3,)),
            pltpu.SemaphoreType.DMA((BLOCK // SUB,)),
            pltpu.SemaphoreType.DMA((STEPS, 12)),
            pltpu.SemaphoreType.DMA((STEPS, 2, ROWS)),
            pltpu.SemaphoreType.DMA((STEPS, ROWS)),
            pltpu.SemaphoreType.DMA((STEPS, ROWS)),
            pltpu.SemaphoreType.DMA((STEPS, ROWS)),
            pltpu.SemaphoreType.DMA((ROWS,)),
            pltpu.SemaphoreType.DMA((ROWS,)),
            pltpu.SemaphoreType.DMA((COLS,)),
            pltpu.SemaphoreType.DMA((COLS,)),
        ],
        compiler_params=pltpu.CompilerParams(
            collective_id=2, has_side_effects=True, vmem_limit_bytes=VMEM_LIMIT
        ),
    )(members, probes)


def on_device(perturbations, probes):
    return band_and_sample(gathered(perturbations).reshape(COLS, MEMBERS, BLOCK), probes)


def solution(mesh):
    return jax.shard_map(
        on_device,
        mesh=mesh,
        in_specs=(P("row", "col"), P(("col", "row"), None)),
        out_specs=(P("col", "row"), P(("col", "row"), None)),
        check_vma=False,
    )
```

```python
import functools
import math

import jax
import jax.numpy as jnp
from jax import lax
from jax.experimental import pallas as pl
from jax.experimental.pallas import tpu as pltpu
from jax.sharding import PartitionSpec as P

MEMBERS = 512
STATES = 16384
WINDOW = 4096
ROWS = 8
COLS = 16
BLOCK = 1024
PIECE = 128
SUB = 256
SPAN = SUB + BLOCK
STEPS = 3
MESH = pl.DeviceIdType.MESH
VMEM_LIMIT = 58 * 2**20

epsilon = 1e-06
power_terms = (
    2.0 / math.pi - 4.0 / (3.0 * math.pi) - 4.0 / (15.0 * math.pi) - 4.0 / (35.0 * math.pi),
    8.0 / (3.0 * math.pi) + 32.0 / (15.0 * math.pi) + 72.0 / (35.0 * math.pi),
    -32.0 / (15.0 * math.pi) - 192.0 / (35.0 * math.pi),
    128.0 / (35.0 * math.pi),
)

ROUTES = (
    (0x22f1386c260b0000000000086c260d0100000000086c260b0100000000086c2a0d01, 0x8e4622f130000000008ec6a2b100000001008f4662b1087c2c01038ec6a2d130042e0d01, 0x8fc622b1386c220b018ec6e2f1086c260d008fc66291386c2e0f018ec622b1186c2a0903, 0x8ec6e2f1386c2209008ec622d11864260b038fc662f1387c260b038ec6a2f118742a0d00, 0x8ec6629100000001038fc6e2b118742e0d010046a2c008742a0b01004622f1086c2e0b01, 0x8e4622f1286c2a0f038f46a2b12004220b018e4622d1386c24010000468000087c220f03),
    (0x8642e0d0200000000087c2e09000000000008642a0f0300000000087c220b02, 0x8fc662d120000000008f46e2f120000000008ec6229110000000008e46e29120042a0b00, 0x8e46e2912864260d028f4622d1287c220b018f46a2f108742a09028f46e2f128742e0d01, 0x8fc622d1087c2e0d028fc6a2f1387c220f018e46e2b1286c2a0f028e4622b1387c260f03, 0x8f46a2b110000000008e46401138642609020046c000087c220d02000000113864260f02, 0x8fc6a2d11874220b01004622d100042800000046e2b128642c0103000000000864260800),
    (0x87c2a0901000000000874220f03000000000874220d00000000000864260903, 0x8ec6e29100000000008e4622d110000000008fc6a2d130000000008fc662f10000000102, 0x8f4662f1187c2a0f038e4662b118742a09028e46e2b1187c260b008e46a2d1087c220b02, 0x8e4662b128642a0b018e4662b1086c2a0d028f4622d108642e0d008fc6e2d10864220901, 0x46e2d120000000008e800011287c220b03000000000004260800000000112874220d00, 0x8e8022913004260c000046e29130042c00000046a2f10004200101000000000000000000),
    (0x4260b1f844360f0300476311d84caa4f0200452320087ca21305005e6e9708543a0f63, 0x89eea27f1006a34fe18ffebed16f77a8000089fe227f0f680203108f4e2231796c10010d, 0x86c6a2d1f8e416030086c6a2132f742fcb038ecea6b1285c662b0d8fde66d1d8646a2d13, 0x8f4260b17807afcde19e426290187433cb2389c6a6b1181c2209e19e4660d128ec2e1502, 0xffc77eb00007af2f938d802218084c6a2b0dc7c7c0117004660f0dbec770d118543a1503, 0x89c563717d7c174fa39e45e0d1d9680000009f47e0b1f8f43c0105004570d818eca62d20),
    (0x47e271684c3e04000047e21328443e0121004e80130854aa4b0e89deaeb7181cae0720, 0xffc5225f3d66a7490489fee291e00000000089472331ff600215e188c6235159646a0312, 0x86452251cf642e2e008c0026f1e86417cd2386ce2211e8f41fcb0e8dcee231e85c6e2900, 0x8846a0d11877a7c9e29fc2e0900f743e13e18e80229158f43fcbe287dea6b158e43e0a00, 0x8842e0d1cf6000000088c5a25160046e030f0000237830046229e2bf62e25700046e2c00, 0x864762700816a2110489c26091797002110f0045e0f0381caa2902004e30b808e46e290d),
    (0x45e250280432020000000000086436152300000013384cae1521bf5eeed72844160307, 0x89456371e0000207a38846633150000204008862e37f3f7000011189e2e2b1d004662f0e, 0x8c002271e8ffa206009f8026d138541bc912864626d1ff6c13cf038d5ee6b33844662f10, 0x42a0915814362fe38f46e69128ec3611009f0026932877ae2de0885ee6f168fc321200, 0x87c6209f1f780000008cc20011c004622f050000223f384c1e1313005ee21168fc66050f, 0x452090280ea615069fc720f03004a4010e87426311e8ec34010f0062c018285c320706),
    (0x4360f0d8741a000000442133785ca2199d0044c0135a6c161707af5f40160874be1500, 0x8f6d7e1f2007276dc088c5623f7e7fe401c388c4e211c8cfba270b8c4f231119f4762310, 0x8445a4d1084c62091c9e4aa091cf7febec008cca2691d854220de08c4daab13004e22200, 0x4364d218ffebd7e680c2277158f7a3cfe5ae0024d01f0fe3d5f0af5f6290186c3be800, 0xfdc523f61f4e270bed86c40011d004360107b6802131d89c562bf0bce10011f8d46a27f3, 0x47a131edec070bc099caa350d91e7730009d4660d1d816521106d6cfc018d96c5a1517),
    (0x4720501f740211960043e1763854a605240044249378140e092fafdaef57ca652a050b, 0x887623f11006ef68008dffe3d180079401168e7f7ef15007961a009dcde371c91c62130f, 0x848024b0c85c5febf18d4de4f20e7f9a0e00ae4aa4b32f646bcc0086c664b2000427ea00, 0x24b038e7efd3e49647e4f1789fe3e8009980231168ec3233018f5ae0b1780473ee00, 0x8944a390cf0e7f27ef8047ff600f0c2a07eeb65ae3d90f143e331fb844401608dc522915, 0x43e230dde6ef6996964de23029149721099c4a6250e896eb3304d64eb039288c3e0515),
    (0x43223f68541e17e5004d400009741a0b2600000012385c3a0502b7de2f751a7c321f2f, 0x8dc5be5fc006b346008900231170079c00008ac6e2f12fff9c0000886123b1f9ee2e211d, 0x8e8024f20f441fc3f39ecda49228e4122c00aecd62523864162ded854a60d23ff45e2a00, 0x4ae4901f77a3ebf188c3e371681fbbec00af8020d14807e7cdf3975e64b0689c7fea00, 0xfcfa21506f165f259fb75abe334f4c7629f3b756ecd6183c32011eb7df401638f4322b1d, 0x8043631188443801ad00436151e90e7c010899c7a150d8840e3716006132f359647e3525),
    (0x45a1b0882c0607e7004a2193b82c864a00000000126845261f2ead5d2ff63a4c36514d, 0x8b77e3115006db55b78a80221d3eefd401f7000023bf6fd787711c9b002331e9c6d22b11, 0x8749a232d8c41bee00844d6673feefd62e008d4de4f1cfd463e60087de24f1cef41bca00, 0xa68026d4089c3ff503a680253438e46bd200a6802750588feff00000002090281c37ca00, 0xf8c1b0760f1e370febb7c07d3fdf9c7a1b0accdbb2791f847a210abde7401718c43607f4, 0x90c1a1b10d5ed801b795412011c0064313b7944e2170c88c4c01b5df62b238e004363111),
    (0x402010981420010b004bc01278343a1a00000000134a143e5129ac002d76ca0cb6174f, 0x88f6a3c00e0f6344008b803fd1ae17d801ff8b7c62518fdfd36000890023d1b914023713, 0x87cee6932e6c13c000964a6633cfd41e22008dcda2d2dfdc1bc400865d2292e8cc53e600, 0xa60026932894261400a78021314f9feff3f4a98026d0380c7beff5a600271148f7a7f400, 0xf77c23118f367305ec885e70596f2c4e0f1800597158b824720715b95c8016c8442a091c, 0x4421908d8ee8018d9bcda05180063f4bb6954de09198564f491cd1e631337994721f04),
    (0x42a3d9683c380000000000138824325400a7800015ca1c361d28ad802d400a148e1800, 0x8ac6a21d5e4ebf74008b002371bee79800008a00231f1ff62c00008b00225c19844e391c, 0x854966f1de4c53e1fc8fc9e8d01ee46be800acc96472184c6fec0094dae4d2df7c17e400, 0xa700256008efe3ee00898026d3180fbff000a60025517f87f7f200a78026d0580803f600, 0xf07dba31df26332382004180170f3c5a15febfc4b1bfff540e0512005e401668cc5e03ff, 0x42e1715006d40181904063311946d7170c994b63d0185c3001b7dee77219d9dcae3b08),
    (0x6d6210e85c161e0000486e7298142a0600a5000015d824320600a4002f94d84c0e1b4b, 0x8d446231de9eb77000000022713e8790000000003e514f9fcf53fa8a803c71698cce191f, 0x8dc9e630ee6467c60087c9a653de5c622800854d20f3e84003ea00845ea652ced4100000, 0xaf0025536ffc33f600a18020f77817b3a9d7a80024b07897a7e800a88024f0781003ce00, 0xfe78793e50065b1b8dbcdd40171fac7233e7bd5f63f9c8e42e2ff6bc5e0000084c0e231e, 0x934aa210e006b001a69b4fa2f00006a319b29ac2a05148479f53b0dc6672b919b6d23336),
    (0x47a03fd83408000000002d54183c0e4600000000122a0c121800a5002fb4f85ca2114c, 0x22bdde96f35e008a00239fde8f6c000000002231dfc6bc01f80000001c0956ce3f07, 0x9dcd2472ef7003ca0087492411d85c67c00087cae632fff80228008c802493dec003c400, 0xa180253e7f8fbbe800a143a1503807ebcc00a100217068ffebd600a98025504c9803d600, 0x82fefb7fc00603019600594017ff34123df9bdd8703f2fac3617fbba60000000043e1ffe, 0x994e22b0f006fc01b194c9e371b006bc01ad80c961f1a8fe4001b3d166b3790954a22723),
    (0x44211608240c000000002db2400416500000000014ca4516112ca7002cd7da1c060000, 0x23b14e2f2f7ba8007ca3f14e57ec00008b803e11af46c3560000000011a95f6b731e, 0x8cc92420087003cc0085802013ee5003e00084802410df4003c800870020f1fed803e200, 0xa78027400f7ff60e00ae0020a008843bc800a00020900887b38a00a00025700f7fb3d400, 0xf6f9801f20062b3d88005d8019df24321ff8bf5d00126f04763be5b5dd000000047239e2, 0x92cde330a0040c01b593c3a2704004b801bb9bc8e291c8d6f401a3d864f398f95c7a692f),
    (0x41e1d76004d4000000000016b0041e4c00000000140a74020000ac802f378a340a1c00, 0x2331beaeff720000003ffdffe7580000000023ff2fcf235800000000114946123c00, 0x8d0026400ff803e80086002452100003c400840020d3ce5003e5fe9d802413fe441fc600, 0xae8026a008f43a1000a80024a008942fd000a18027200f07a3ce00ae0024c00880039200, 0xf87e401e7000032189bbd9c0127fa40a2d1eb9dcc017af740625ecbd5ac00000047e3ff5, 0x9b4c6340000000018e98cc63f070068401a99b47635110000001a6d8ecf1993944f27726),
    (0x406c55f00550000000002c37000408000000000014300406020000002c945a24b21200, 0x235d7eb7236600000023bd2ebf68000000002351b0073c00000000001189fe4e1000, 0x960024400e5003e4008c802292f8c803ee00958024d3de78022e00848022521e50000000, 0xa90027000887fff2009700256008fff2080088800000081473c800a90024800890038800, 0xf3ffc01840067b0376005980000004661910bc59c0178f4c46230cb2d9800000047a1deb, 0x9a4161c000000001a49ac321d1f0000001b892cd221020000001b4d56033f9c004dc0124),
    (0x420015000410000000000017c0048c000000000015000538000000002f15c0052c0000, 0x119e3ef8000000000011fe5f5400000000001170075400000000000009d6c00000, 0x26000e5803ce00000022400000000000000026400f70000000000026200e7003cc00, 0xa0000000000003a800af0000000000038e0081000000000003d200a70025000007bfcc00, 0xfe80000000064311810059000000000001f2b459000000000001fe005e800000000001e8, 0x93ce401190000001a89349000000000001a79a49238000000001a2d5800019f00000013c),
    (0x438015100000000000000015a000000000000000151000000000000000152004000000, 0x11ae377c0000000000000eaf300000000000000007040000000000000007740000, 0xe40000000000000000e70000000000024400000000000000024400ec8000000, 0xa8002720000003b60000000000000003f60000000000000000000090800000000003f200, 0x61f1d7dbe53800000000001fabcd8000000000001e00000000000000001fa, 0x924c8011a0000000009246400000000001a195c9c0000000000000d40033d87000000121),
    (0x17d00000000000000015800000000000000014600000000000000014b000000000, 0xe27680000000000000e077c0000000000000006f400000000001e4000000000, 0xe48000000000000000000000000000000000ef803c800, 0xa08000000000000000000000000000000000000000000000000000a10000000000000000, 0x604018e005ec00000000000000056400000000001f9000000000000000000, 0x1a4000000000000000000df803119e000000122),
    (0x17100000000000000015900000000000000014c000000000, 0xea7700000000000000e4f200000000000000006fc0000000000000000000000, 0x0, 0xa88000000000000000000000000000000000000000000000000000000000000000000000, 0x6200000000000000000000000000000000000000000000000000000000000, 0x1ae000000000000000000dd0000000000000000),
    (0x19d000000000000000000000000000000000147000000000, 0xedf5c0000000000000007240000000000000000000000000000000000000000, 0x0, 0xa10000000000000000000000000000000000000000000000000000000000000000000000, 0x6380000000000000000000000000000000000000000000000000000000000, 0x0),
)


def here():
    return lax.axis_index("row"), lax.axis_index("col")


def at(row, col):
    return {"row": row, "col": col}


def unless(own, step):
    if own is None:
        step()
    else:
        pl.when(jnp.logical_not(own))(step)


def copied(src, dst, send, recv, row, col):
    return pltpu.make_async_remote_copy(
        src_ref=src, dst_ref=dst, send_sem=send, recv_sem=recv,
        device_id=at(row, col), device_id_type=MESH,
    )


DIRECTIONS = ((1, 0, 0), (-1, 0, 0), (0, 1, 0), (0, -1, 0), (0, 0, 1), (0, 0, -1))
QUARTER = MEMBERS // ROWS // 4
LAG = 3


def place_of(i):
    return (i % 8) // 4, i % 4, i // 8


def arrivals():
    table = []
    for sends in ROUTES:
        by_direction = []
        for (dx, dy, dz), packed in zip(DIRECTIONS, sends):
            entries = []
            for i in range(32):
                x, y, z = place_of(i)
                fx, fy, fz = (x - dx) % 4, (y - dy) % 4, (z - dz) % 4
                entry = packed >> (9 * (fz * 8 + (fx % 2) * 4 + fy)) & 511
                if entry:
                    pair = (fx // 2) * 4 + fz + (entry >> 5 & 7)
                    entry = 256 | (pair - z) % 8 << 5 | entry & 31
                entries.append(entry)
            by_direction.append(entries)
        table.append(by_direction)
    return table


def departures():
    return [[[packed >> (9 * i) & 511 for i in range(32)] for packed in sends] for sends in ROUTES]


def words(table):
    return [
        [[d[i] | e[i] << 9 | f[i] << 18 for i in range(32)] for d, e, f in (sends[:3], sends[3:])]
        for sends in table
    ]


def looked_up(values, bits):
    if len(set(values)) == 1:
        return jnp.int32(values[0])
    low = looked_up(values[: len(values) // 2], bits[:-1])
    high = looked_up(values[len(values) // 2 :], bits[:-1])
    return jnp.where(bits[-1], high, low)


def gather_members(x_ref, held, send, recv, across_send, across_recv, own_sem, greet_all):
    r, c = here()
    core = lax.rem(c, 2)
    pair = lax.div(c, 2)
    z = lax.rem(pair, 4)
    x = lax.div(pair, 4) * 2 + lax.div(r, 4)
    y = lax.rem(r, 4)
    first = core == 0
    sign = 1 - 2 * core
    index = jnp.where(first, z * 8 + r, (3 - z) * 8 + 7 - r)
    bits = [lax.rem(lax.div(index, 2**b), 2) == 1 for b in range(5)]

    def neighbour(direction):
        dx, dy, dz = DIRECTIONS[direction]
        nx, ny, nz = (lax.rem(v + sign * d + 4, 4) for v, d in ((x, dx), (y, dy), (z, dz)))
        return lax.rem(nx, 2) * 4 + ny, lax.div(nx, 2) * 8 + nz * 2 + core

    sides = [neighbour(d) for d in range(6)]
    other = (r, c + sign)

    across = lax.div(lax.rem(2 * pair - 4 + r + 2 - core - lax.rem(r, 2) + COLS, COLS), 2)

    own = pltpu.make_async_copy(x_ref, held.at[pair, r], own_sem)
    own.start()
    greet_all(sides)
    own.wait()

    def unit(entry):
        relative = lax.rem(lax.div(entry, 32), 8)
        row = lax.rem(lax.div(entry, 4), 8)
        block = lax.rem(pair + sign * relative + 8, 8)
        row = jnp.where(first, row, 7 - row)
        quarter = pl.multiple_of(lax.rem(entry, 4) * QUARTER, QUARTER)
        return block, row, pl.ds(quarter, QUARTER)

    def entries(table):
        found = []
        for word in table:
            word = looked_up(word, bits)
            found += [lax.rem(word, 512), lax.rem(lax.div(word, 512), 512), lax.div(word, 512 * 512)]
        return found

    piece = held.at[pair, r, pl.ds(0, QUARTER)]

    def pass_across(block, row, part):
        @pl.when(block == across)
        def _():
            copied(held.at[block, row, part], held.at[8, row, part], across_send, across_recv, *other).start()

    def take(step):
        for d, entry in enumerate(entries(incoming[step])):
            @pl.when(entry >= 256)
            def _(d=d, entry=entry):
                block, row, part = unit(entry)
                ref = held.at[block, row, part]
                pltpu.make_async_copy(ref, ref, recv.at[step, d]).wait()
                pass_across(block, row, part)

    incoming, outgoing = words(arrivals()), words(departures())
    pass_across(pair, r, pl.ds(0, MEMBERS // ROWS))
    rounds = len(ROUTES)
    for step in range(rounds + LAG):
        if step >= LAG:
            take(step - LAG)
        if step < rounds:
            for d, entry in enumerate(entries(outgoing[step])):
                @pl.when(entry >= 256)
                def _(d=d, entry=entry):
                    block, row, part = unit(entry)
                    ref = held.at[block, row, part]
                    copied(ref, ref, send.at[step, d], recv.at[step, d], *sides[d]).start()

    def finish():
        for step in range(rounds):
            for d, entry in enumerate(entries(outgoing[step])):
                @pl.when(entry >= 256)
                def _(d=d):
                    copied(piece, piece, send.at[step, d], recv.at[step, d], *sides[d]).wait_send()
        copied(held.at[pair], held.at[8], across_send, across_recv, *other).wait_send()

    copied(held.at[pair], held.at[8], across_send, across_recv, *other).wait_recv()
    return finish


def parted(values):
    high = values.astype(jnp.bfloat16)
    low = (values - high.astype(jnp.float32)).astype(jnp.bfloat16)
    return high, low


def dotted(a, b, dims):
    return lax.dot_general(a, b, (dims, ((), ())), preferred_element_type=jnp.float32)


def skewed(rows, shift):
    sub = lax.broadcasted_iota(jnp.int32, rows.shape, 0)
    if shift:
        rows = pltpu.roll(rows, SPAN - shift, 1)
    for bit in (1, 2, 4):
        rows = jnp.where((sub & bit) != 0, pltpu.roll(rows, SPAN - bit, 1), rows)
    return rows[:, :BLOCK]


def main_kernel(
    members_ref, w_ref, local_out, out_ref,
    held, xh, xl, band_ref, high_ref, low_ref, local_ref,
    iterate, near, window, wide, parts, sums, square_ref, row_squares, col_squares, row_total,
    member_send, member_recv, across_send, across_recv, own_sem, store_sem, send_z, recv_z, send_w, recv_w, send_x, send_y, recv_y, send_r, recv_r, send_c, recv_c,
):
    r, c = here()
    core = lax.rem(c, 2)
    pair = lax.div(c, 2)
    other = (r, c + 1 - 2 * core)
    shared = 1 - core
    passes = core == lax.rem(r + 1, 2)

    def greet_all(sides):
        barrier = pltpu.get_barrier_semaphore()
        partners = list(sides)
        for shift in range(1, ROWS):
            row = lax.rem(r + shift, ROWS)
            partners += [(row, 2 * pair), (row, 2 * pair + 1)]
        for shift in range(1, COLS):
            partners.append((r, lax.rem(c + shift, COLS)))
        for row, col in partners:
            pl.semaphore_signal(barrier, inc=1, device_id=at(row, col), device_id_type=MESH)
        pl.semaphore_wait(barrier, len(partners))

    def to_pairs(step, source, away):
        col = lax.rem(c - 2 * away + COLS, COLS)
        return copied(source, near.at[step, away + 2], send_z.at[step, away + 2], recv_z.at[step, away + 2], r, col)

    def targets(away):
        found = []
        for e in range(3):
            row = 2 * away + core + 2 + e
            valid = None
            if away == -2:
                if e == 0:
                    continue
                valid = core == 1 if e == 1 else None
            if away == 2:
                if e == 2:
                    continue
                valid = core == 0 if e == 1 else None
            there = (1, core, 0)[e]
            panel = (1, shared, 0)[e]
            found.append(((away + 2) * 3 + e, row, there, panel, valid))
        return found

    def share(step, source, away, act):
        for slot, row, there, panel, valid in targets(away):
            own = (row == r) & (there == core)
            go = jnp.logical_not(own)
            if valid is not None:
                own, go = own & valid, go & valid

            @pl.when(go)
            def _(slot=slot, row=row, there=there, panel=panel):
                act(copied(
                    source, window.at[step, panel, r], send_w.at[step, slot], recv_w.at[step, panel, r], row, 2 * pair + there
                ), True)

            @pl.when(own)
            def _(panel=panel):
                act(pltpu.make_async_copy(source, window.at[step, panel, r], recv_w.at[step, panel, r]), False)

    def begin(copy, remote):
        copy.start()

    def send_iterate(step, source):
        for away in (-2, 2, -1, 1):
            to_pairs(step, source, away).start()
        share(step, source, 0, begin)

    def spread_iterate(step):
        for away in (-1, 1, -2, 2):
            block = near.at[step, away + 2]
            pltpu.make_async_copy(block, block, recv_z.at[step, away + 2]).wait()
            share(step, block, away, begin)

    def take_iterate(step):
        @pl.when(passes)
        def _():
            for row in range(ROWS):
                block = window.at[step, shared, row]
                pltpu.make_async_copy(block, block, recv_w.at[step, shared, row]).wait()
                there = window.at[step, 1 - shared, row]
                copied(block, there, send_x.at[step, row], recv_w.at[step, 1 - shared, row], *other).start()
                split(step, shared, row)
        for row in range(ROWS):
            landed(step, core, row)
        @pl.when(jnp.logical_not(passes))
        def _():
            for row in range(ROWS):
                landed(step, shared, row)

    def split(step, panel, row):
        high, low = parted(window[step, panel, row])
        first = pl.multiple_of((panel * ROWS + row) * PIECE, PIECE)
        wide[pl.ds(first, PIECE), :PIECE] = high
        wide[pl.ds(first, PIECE), PIECE:] = low

    def landed(step, panel, row):
        block = window.at[step, panel, row]
        pltpu.make_async_copy(block, block, recv_w.at[step, panel, row]).wait()
        split(step, panel, row)

    finish = gather_members(
        members_ref, held, member_send, member_recv, across_send, across_recv, own_sem, greet_all
    )
    send_iterate(0, w_ref)
    spread_iterate(0)

    near_block = lax.div(lax.rem(c + r - 4 + COLS, COLS), 2)
    far_block = lax.div(lax.rem(c + r - 3 + COLS, COLS), 2)
    odd = lax.rem(r, 2) == 1
    for panel, block in enumerate((pair, jnp.where(odd, 8, near_block), jnp.where(odd, far_block, 8))):
        for first in range(0, BLOCK, SUB):
            values = held[block, :, :, first : first + SUB].reshape(MEMBERS, SUB)
            centered = values - jnp.sum(values, 0, keepdims=True) / MEMBERS
            spread = jnp.sqrt(jnp.sum(centered * centered, 0, keepdims=True) + epsilon)
            high, low = parted(centered / spread)
            lo_at = (panel - 1) * BLOCK + first if panel else 2 * BLOCK + first
            xh[:, lo_at : lo_at + SUB] = high
            xl[:, lo_at : lo_at + SUB] = low
    squares = jnp.zeros((8, 128), jnp.float32)
    gap = lax.broadcasted_iota(jnp.int32, (SUB, SPAN), 1) - lax.broadcasted_iota(jnp.int32, (SUB, SPAN), 0)
    taper = jnp.maximum(0.0, 1.0 - jnp.abs(gap + (r * BLOCK - WINDOW)).astype(jnp.float32) / WINDOW)
    taper = jnp.where((gap >= 0) & (gap < BLOCK), taper, 0.0)
    for tile in range(BLOCK // SUB):
        first = tile * SUB
        rows_h = xh[:, 2 * BLOCK + first : 2 * BLOCK + first + SUB]
        rows_l = xl[:, 2 * BLOCK + first : 2 * BLOCK + first + SUB]
        cols_h = xh[:, first : first + SPAN]
        cols_l = xl[:, first : first + SPAN]
        over = ((0,), (0,))
        gram = dotted(rows_h, cols_h, over) + (dotted(rows_h, cols_l, over) + dotted(rows_l, cols_h, over))
        band = gram * taper
        band_ref[tile] = band
        high, low = parted(band)
        high_ref[tile] = high
        low_ref[tile] = low
        squares = squares + jnp.sum((band * band).reshape(SUB // 8, 8, SPAN // 128, 128), (0, 2))
    square_ref[...] = squares

    for shift in range(1, ROWS):
        copied(square_ref, row_squares.at[r], send_r.at[shift], recv_r.at[r], lax.rem(r + shift, ROWS), c).start()
    pltpu.make_async_copy(square_ref, row_squares.at[r], recv_r.at[r]).start()

    stores = []

    def skew(tile):
        first = tile * SUB
        for group in range(0, SUB, 8):
            local_ref[first + group : first + group + 8, :] = skewed(band_ref[tile, group : group + 8, :], group)
        stores.append(pltpu.make_async_copy(local_ref.at[first : first + SUB], local_out.at[first : first + SUB], store_sem.at[tile]))
        stores[-1].start()

    total = None
    summed = power_terms[0] * w_ref[...]
    for step in range(STEPS):
        take_iterate(step)
        for tile in range(BLOCK // SUB):
            first = tile * SUB
            over = ((1,), (0,))
            both = dotted(high_ref[tile], wide[first : first + SPAN, :], over)
            rest = dotted(low_ref[tile], wide[first : first + SPAN, :PIECE], over)
            parts[step, first : first + SUB, :] = both[:, :PIECE] + (both[:, PIECE:] + rest)
            for row in range(first // PIECE, (first + SUB) // PIECE):
                def go(row=row):
                    copied(
                        parts.at[step, row * PIECE : (row + 1) * PIECE], sums.at[step, r],
                        send_y.at[step, row], recv_y.at[step, r], row, c,
                    ).start()

                unless(r == row, go)
        if step == 0:
            for row in range(ROWS):
                pltpu.make_async_copy(square_ref, row_squares.at[row], recv_r.at[row]).wait()
            row_total[...] = jnp.sum(row_squares[...], 0)
            for shift in range(1, COLS):
                copied(row_total, col_squares.at[c], send_c.at[shift], recv_c.at[c], r, lax.rem(c + shift, COLS)).start()
            pltpu.make_async_copy(row_total, col_squares.at[c], recv_c.at[c]).start()
        if step < 2:
            skew(2 * step)
        if step == 0:
            for col in range(COLS):
                pltpu.make_async_copy(row_total, col_squares.at[col], recv_c.at[col]).wait()
            total = jnp.sum(jnp.sum(col_squares[...], 0), keepdims=True) / STATES
        vector = parts[step, pl.ds(pl.multiple_of(r * PIECE, PIECE), PIECE), :]
        for row in range(ROWS):
            def arrived(row=row):
                pltpu.make_async_copy(w_ref, sums.at[step, row], recv_y.at[step, row]).wait()

            unless(r == row, arrived)
            vector = vector + jnp.where(r == row, 0.0, sums[step, row])
        vector = vector / total
        summed = summed + power_terms[step + 1] * vector
        if step < STEPS - 1:
            iterate[step] = vector
            send_iterate(step + 1, iterate.at[step])
            spread_iterate(step + 1)
            skew(2 * step + 1)
    out_ref[...] = jnp.sqrt(total) * summed

    for copy in stores:
        copy.wait()
    finish()
    for shift in range(1, ROWS):
        copied(square_ref, row_squares.at[r], send_r.at[shift], recv_r.at[r], lax.rem(r + shift, ROWS), c).wait_send()
    for shift in range(1, COLS):
        copied(row_total, col_squares.at[c], send_c.at[shift], recv_c.at[c], r, lax.rem(c + shift, COLS)).wait_send()
    for step in range(STEPS):
        for away in (-2, -1, 1, 2):
            to_pairs(step, w_ref, away).wait_send()
        for away in range(-2, 3):
            share(step, w_ref, away, lambda copy, remote: copy.wait_send() if remote else None)
        @pl.when(passes)
        def _(step=step):
            for row in range(ROWS):
                copied(w_ref, window.at[step, core, row], send_x.at[step, row], recv_w.at[step, core, row], *other).wait_send()
        for row in range(ROWS):
            def gone(row=row):
                copied(w_ref, sums.at[step, r], send_y.at[step, row], recv_y.at[step, r], row, c).wait_send()

            unless(r == row, gone)


def band_and_sample(members, probes):
    return pl.pallas_call(
        main_kernel,
        name="band_and_sample",
        out_shape=(
            jax.ShapeDtypeStruct((BLOCK, BLOCK), jnp.float32),
            jax.ShapeDtypeStruct((PIECE, PIECE), jnp.float32),
        ),
        in_specs=[pl.BlockSpec(memory_space=pl.ANY), pl.BlockSpec(memory_space=pltpu.VMEM)],
        out_specs=[pl.BlockSpec(memory_space=pl.ANY), pl.BlockSpec(memory_space=pltpu.VMEM)],
        scratch_shapes=[
            pltpu.VMEM((9, ROWS, MEMBERS // ROWS, BLOCK), jnp.float32),
            pltpu.VMEM((MEMBERS, 3 * BLOCK), jnp.bfloat16),
            pltpu.VMEM((MEMBERS, 3 * BLOCK), jnp.bfloat16),
            pltpu.VMEM((BLOCK // SUB, SUB, SPAN), jnp.float32),
            pltpu.VMEM((BLOCK // SUB, SUB, SPAN), jnp.bfloat16),
            pltpu.VMEM((BLOCK // SUB, SUB, SPAN), jnp.bfloat16),
            pltpu.VMEM((BLOCK, BLOCK), jnp.float32),
            pltpu.VMEM((STEPS - 1, PIECE, PIECE), jnp.float32),
            pltpu.VMEM((STEPS, 5, PIECE, PIECE), jnp.float32),
            pltpu.VMEM((STEPS, 2, ROWS, PIECE, PIECE), jnp.float32),
            pltpu.VMEM((2 * BLOCK, 2 * PIECE), jnp.bfloat16),
            pltpu.VMEM((STEPS, BLOCK, PIECE), jnp.float32),
            pltpu.VMEM((STEPS, ROWS, PIECE, PIECE), jnp.float32),
            pltpu.VMEM((8, 128), jnp.float32),
            pltpu.VMEM((ROWS, 8, 128), jnp.float32),
            pltpu.VMEM((COLS, 8, 128), jnp.float32),
            pltpu.VMEM((8, 128), jnp.float32),
            pltpu.SemaphoreType.DMA((len(ROUTES), 6)),
            pltpu.SemaphoreType.DMA((len(ROUTES), 6)),
            pltpu.SemaphoreType.DMA,
            pltpu.SemaphoreType.DMA,
            pltpu.SemaphoreType.DMA,
            pltpu.SemaphoreType.DMA((BLOCK // SUB,)),
            pltpu.SemaphoreType.DMA((STEPS, 5)),
            pltpu.SemaphoreType.DMA((STEPS, 5)),
            pltpu.SemaphoreType.DMA((STEPS, 15)),
            pltpu.SemaphoreType.DMA((STEPS, 2, ROWS)),
            pltpu.SemaphoreType.DMA((STEPS, ROWS)),
            pltpu.SemaphoreType.DMA((STEPS, ROWS)),
            pltpu.SemaphoreType.DMA((STEPS, ROWS)),
            pltpu.SemaphoreType.DMA((ROWS,)),
            pltpu.SemaphoreType.DMA((ROWS,)),
            pltpu.SemaphoreType.DMA((COLS,)),
            pltpu.SemaphoreType.DMA((COLS,)),
        ],
        compiler_params=pltpu.CompilerParams(
            collective_id=1, has_side_effects=True, vmem_limit_bytes=VMEM_LIMIT
        ),
    )(members, probes)


def on_device(perturbations, probes):
    return band_and_sample(perturbations, probes)


def solution(mesh):
    return jax.shard_map(
        on_device,
        mesh=mesh,
        in_specs=(P("row", "col"), P(("col", "row"), None)),
        out_specs=(P("col", "row"), P(("col", "row"), None)),
        check_vma=False,
    )
```

```python
import functools
import math

import jax
import jax.numpy as jnp
from jax import lax
from jax.experimental import pallas as pl
from jax.experimental.pallas import tpu as pltpu
from jax.sharding import PartitionSpec as P

MEMBERS = 512
STATES = 16384
WINDOW = 4096
ROWS = 8
COLS = 16
BLOCK = 1024
PIECE = 128
HALF = 64
SUB = 256
SPAN = SUB + BLOCK
STEPS = 3
MESH = pl.DeviceIdType.MESH
VMEM_LIMIT = 58 * 2**20

epsilon = 1e-06
power_terms = (
    2.0 / math.pi - 4.0 / (3.0 * math.pi) - 4.0 / (15.0 * math.pi) - 4.0 / (35.0 * math.pi),
    8.0 / (3.0 * math.pi) + 32.0 / (15.0 * math.pi) + 72.0 / (35.0 * math.pi),
    -32.0 / (15.0 * math.pi) - 192.0 / (35.0 * math.pi),
    128.0 / (35.0 * math.pi),
)

ROUTES = (
    (0x22f1386c260b0000000000086c260d0100000000086c260b0100000000086c2a0d01, 0x8e4622f130000000008ec6a2b100000001008f4662b1087c2c01038ec6a2d130042e0d01, 0x8fc622b1386c220b018ec6e2f1086c260d008fc66291386c2e0f018ec622b1186c2a0903, 0x8ec6e2f1386c2209008ec622d11864260b038fc662f1387c260b038ec6a2f118742a0d00, 0x8ec6629100000001038fc6e2b118742e0d010046a2c008742a0b01004622f1086c2e0b01, 0x8e4622f1286c2a0f038f46a2b12004220b018e4622d1386c24010000468000087c220f03),
    (0x8642e0d0200000000087c2e09000000000008642a0f0300000000087c220b02, 0x8fc662d120000000008f46e2f120000000008ec6229110000000008e46e29120042a0b00, 0x8e46e2912864260d028f4622d1287c220b018f46a2f108742a09028f46e2f128742e0d01, 0x8fc622d1087c2e0d028fc6a2f1387c220f018e46e2b1286c2a0f028e4622b1387c260f03, 0x8f46a2b110000000008e46401138642609020046c000087c220d02000000113864260f02, 0x8fc6a2d11874220b01004622d100042800000046e2b128642c0103000000000864260800),
    (0x87c2a0901000000000874220f03000000000874220d00000000000864260903, 0x8ec6e29100000000008e4622d110000000008fc6a2d130000000008fc662f10000000102, 0x8f4662f1187c2a0f038e4662b118742a09028e46e2b1187c260b008e46a2d1087c220b02, 0x8e4662b128642a0b018e4662b1086c2a0d028f4622d108642e0d008fc6e2d10864220901, 0x46e2d120000000008e800011287c220b03000000000004260800000000112874220d00, 0x8e8022913004260c000046e29130042c00000046a2f10004200101000000000000000000),
    (0x4260b1f844360f0300476311d84caa4f0200452320087ca21305005e6e9708543a0f63, 0x89eea27f1006a34fe18ffebed16f77a8000089fe227f0f680203108f4e2231796c10010d, 0x86c6a2d1f8e416030086c6a2132f742fcb038ecea6b1285c662b0d8fde66d1d8646a2d13, 0x8f4260b17807afcde19e426290187433cb2389c6a6b1181c2209e19e4660d128ec2e1502, 0xffc77eb00007af2f938d802218084c6a2b0dc7c7c0117004660f0dbec770d118543a1503, 0x89c563717d7c174fa39e45e0d1d9680000009f47e0b1f8f43c0105004570d818eca62d20),
    (0x47e271684c3e04000047e21328443e0121004e80130854aa4b0e89deaeb7181cae0720, 0xffc5225f3d66a7490489fee291e00000000089472331ff600215e188c6235159646a0312, 0x86452251cf642e2e008c0026f1e86417cd2386ce2211e8f41fcb0e8dcee231e85c6e2900, 0x8846a0d11877a7c9e29fc2e0900f743e13e18e80229158f43fcbe287dea6b158e43e0a00, 0x8842e0d1cf6000000088c5a25160046e030f0000237830046229e2bf62e25700046e2c00, 0x864762700816a2110489c26091797002110f0045e0f0381caa2902004e30b808e46e290d),
    (0x45e250280432020000000000086436152300000013384cae1521bf5eeed72844160307, 0x89456371e0000207a38846633150000204008862e37f3f7000011189e2e2b1d004662f0e, 0x8c002271e8ffa206009f8026d138541bc912864626d1ff6c13cf038d5ee6b33844662f10, 0x42a0915814362fe38f46e69128ec3611009f0026932877ae2de0885ee6f168fc321200, 0x87c6209f1f780000008cc20011c004622f050000223f384c1e1313005ee21168fc66050f, 0x452090280ea615069fc720f03004a4010e87426311e8ec34010f0062c018285c320706),
    (0x4360f0d8741a000000442133785ca2199d0044c0135a6c161707af5f40160874be1500, 0x8f6d7e1f2007276dc088c5623f7e7fe401c388c4e211c8cfba270b8c4f231119f4762310, 0x8445a4d1084c62091c9e4aa091cf7febec008cca2691d854220de08c4daab13004e22200, 0x4364d218ffebd7e680c2277158f7a3cfe5ae0024d01f0fe3d5f0af5f6290186c3be800, 0xfdc523f61f4e270bed86c40011d004360107b6802131d89c562bf0bce10011f8d46a27f3, 0x47a131edec070bc099caa350d91e7730009d4660d1d816521106d6cfc018d96c5a1517),
    (0x4720501f740211960043e1763854a605240044249378140e092fafdaef57ca652a050b, 0x887623f11006ef68008dffe3d180079401168e7f7ef15007961a009dcde371c91c62130f, 0x848024b0c85c5febf18d4de4f20e7f9a0e00ae4aa4b32f646bcc0086c664b2000427ea00, 0x24b038e7efd3e49647e4f1789fe3e8009980231168ec3233018f5ae0b1780473ee00, 0x8944a390cf0e7f27ef8047ff600f0c2a07eeb65ae3d90f143e331fb844401608dc522915, 0x43e230dde6ef6996964de23029149721099c4a6250e896eb3304d64eb039288c3e0515),
    (0x43223f68541e17e5004d400009741a0b2600000012385c3a0502b7de2f751a7c321f2f, 0x8dc5be5fc006b346008900231170079c00008ac6e2f12fff9c0000886123b1f9ee2e211d, 0x8e8024f20f441fc3f39ecda49228e4122c00aecd62523864162ded854a60d23ff45e2a00, 0x4ae4901f77a3ebf188c3e371681fbbec00af8020d14807e7cdf3975e64b0689c7fea00, 0xfcfa21506f165f259fb75abe334f4c7629f3b756ecd6183c32011eb7df401638f4322b1d, 0x8043631188443801ad00436151e90e7c010899c7a150d8840e3716006132f359647e3525),
    (0x45a1b0882c0607e7004a2193b82c864a00000000126845261f2ead5d2ff63a4c36514d, 0x8b77e3115006db55b78a80221d3eefd401f7000023bf6fd787711c9b002331e9c6d22b11, 0x8749a232d8c41bee00844d6673feefd62e008d4de4f1cfd463e60087de24f1cef41bca00, 0xa68026d4089c3ff503a680253438e46bd200a6802750588feff00000002090281c37ca00, 0xf8c1b0760f1e370febb7c07d3fdf9c7a1b0accdbb2791f847a210abde7401718c43607f4, 0x90c1a1b10d5ed801b795412011c0064313b7944e2170c88c4c01b5df62b238e004363111),
    (0x402010981420010b004bc01278343a1a00000000134a143e5129ac002d76ca0cb6174f, 0x88f6a3c00e0f6344008b803fd1ae17d801ff8b7c62518fdfd36000890023d1b914023713, 0x87cee6932e6c13c000964a6633cfd41e22008dcda2d2dfdc1bc400865d2292e8cc53e600, 0xa60026932894261400a78021314f9feff3f4a98026d0380c7beff5a600271148f7a7f400, 0xf77c23118f367305ec885e70596f2c4e0f1800597158b824720715b95c8016c8442a091c, 0x4421908d8ee8018d9bcda05180063f4bb6954de09198564f491cd1e631337994721f04),
    (0x42a3d9683c380000000000138824325400a7800015ca1c361d28ad802d400a148e1800, 0x8ac6a21d5e4ebf74008b002371bee79800008a00231f1ff62c00008b00225c19844e391c, 0x854966f1de4c53e1fc8fc9e8d01ee46be800acc96472184c6fec0094dae4d2df7c17e400, 0xa700256008efe3ee00898026d3180fbff000a60025517f87f7f200a78026d0580803f600, 0xf07dba31df26332382004180170f3c5a15febfc4b1bfff540e0512005e401668cc5e03ff, 0x42e1715006d40181904063311946d7170c994b63d0185c3001b7dee77219d9dcae3b08),
    (0x6d6210e85c161e0000486e7298142a0600a5000015d824320600a4002f94d84c0e1b4b, 0x8d446231de9eb77000000022713e8790000000003e514f9fcf53fa8a803c71698cce191f, 0x8dc9e630ee6467c60087c9a653de5c622800854d20f3e84003ea00845ea652ced4100000, 0xaf0025536ffc33f600a18020f77817b3a9d7a80024b07897a7e800a88024f0781003ce00, 0xfe78793e50065b1b8dbcdd40171fac7233e7bd5f63f9c8e42e2ff6bc5e0000084c0e231e, 0x934aa210e006b001a69b4fa2f00006a319b29ac2a05148479f53b0dc6672b919b6d23336),
    (0x47a03fd83408000000002d54183c0e4600000000122a0c121800a5002fb4f85ca2114c, 0x22bdde96f35e008a00239fde8f6c000000002231dfc6bc01f80000001c0956ce3f07, 0x9dcd2472ef7003ca0087492411d85c67c00087cae632fff80228008c802493dec003c400, 0xa180253e7f8fbbe800a143a1503807ebcc00a100217068ffebd600a98025504c9803d600, 0x82fefb7fc00603019600594017ff34123df9bdd8703f2fac3617fbba60000000043e1ffe, 0x994e22b0f006fc01b194c9e371b006bc01ad80c961f1a8fe4001b3d166b3790954a22723),
    (0x44211608240c000000002db2400416500000000014ca4516112ca7002cd7da1c060000, 0x23b14e2f2f7ba8007ca3f14e57ec00008b803e11af46c3560000000011a95f6b731e, 0x8cc92420087003cc0085802013ee5003e00084802410df4003c800870020f1fed803e200, 0xa78027400f7ff60e00ae0020a008843bc800a00020900887b38a00a00025700f7fb3d400, 0xf6f9801f20062b3d88005d8019df24321ff8bf5d00126f04763be5b5dd000000047239e2, 0x92cde330a0040c01b593c3a2704004b801bb9bc8e291c8d6f401a3d864f398f95c7a692f),
    (0x41e1d76004d4000000000016b0041e4c00000000140a74020000ac802f378a340a1c00, 0x2331beaeff720000003ffdffe7580000000023ff2fcf235800000000114946123c00, 0x8d0026400ff803e80086002452100003c400840020d3ce5003e5fe9d802413fe441fc600, 0xae8026a008f43a1000a80024a008942fd000a18027200f07a3ce00ae0024c00880039200, 0xf87e401e7000032189bbd9c0127fa40a2d1eb9dcc017af740625ecbd5ac00000047e3ff5, 0x9b4c6340000000018e98cc63f070068401a99b47635110000001a6d8ecf1993944f27726),
    (0x406c55f00550000000002c37000408000000000014300406020000002c945a24b21200, 0x235d7eb7236600000023bd2ebf68000000002351b0073c00000000001189fe4e1000, 0x960024400e5003e4008c802292f8c803ee00958024d3de78022e00848022521e50000000, 0xa90027000887fff2009700256008fff2080088800000081473c800a90024800890038800, 0xf3ffc01840067b0376005980000004661910bc59c0178f4c46230cb2d9800000047a1deb, 0x9a4161c000000001a49ac321d1f0000001b892cd221020000001b4d56033f9c004dc0124),
    (0x420015000410000000000017c0048c000000000015000538000000002f15c0052c0000, 0x119e3ef8000000000011fe5f5400000000001170075400000000000009d6c00000, 0x26000e5803ce00000022400000000000000026400f70000000000026200e7003cc00, 0xa0000000000003a800af0000000000038e0081000000000003d200a70025000007bfcc00, 0xfe80000000064311810059000000000001f2b459000000000001fe005e800000000001e8, 0x93ce401190000001a89349000000000001a79a49238000000001a2d5800019f00000013c),
    (0x438015100000000000000015a000000000000000151000000000000000152004000000, 0x11ae377c0000000000000eaf300000000000000007040000000000000007740000, 0xe40000000000000000e70000000000024400000000000000024400ec8000000, 0xa8002720000003b60000000000000003f60000000000000000000090800000000003f200, 0x61f1d7dbe53800000000001fabcd8000000000001e00000000000000001fa, 0x924c8011a0000000009246400000000001a195c9c0000000000000d40033d87000000121),
    (0x17d00000000000000015800000000000000014600000000000000014b000000000, 0xe27680000000000000e077c0000000000000006f400000000001e4000000000, 0xe48000000000000000000000000000000000ef803c800, 0xa08000000000000000000000000000000000000000000000000000a10000000000000000, 0x604018e005ec00000000000000056400000000001f9000000000000000000, 0x1a4000000000000000000df803119e000000122),
    (0x17100000000000000015900000000000000014c000000000, 0xea7700000000000000e4f200000000000000006fc0000000000000000000000, 0x0, 0xa88000000000000000000000000000000000000000000000000000000000000000000000, 0x6200000000000000000000000000000000000000000000000000000000000, 0x1ae000000000000000000dd0000000000000000),
    (0x19d000000000000000000000000000000000147000000000, 0xedf5c0000000000000007240000000000000000000000000000000000000000, 0x0, 0xa10000000000000000000000000000000000000000000000000000000000000000000000, 0x6380000000000000000000000000000000000000000000000000000000000, 0x0),
)


def here():
    return lax.axis_index("row"), lax.axis_index("col")


def at(row, col):
    return {"row": row, "col": col}


def unless(own, step):
    if own is None:
        step()
    else:
        pl.when(jnp.logical_not(own))(step)


def copied(src, dst, send, recv, row, col):
    return pltpu.make_async_remote_copy(
        src_ref=src, dst_ref=dst, send_sem=send, recv_sem=recv,
        device_id=at(row, col), device_id_type=MESH,
    )


DIRECTIONS = ((1, 0, 0), (-1, 0, 0), (0, 1, 0), (0, -1, 0), (0, 0, 1), (0, 0, -1))
QUARTER = MEMBERS // ROWS // 4
LAG = 3


def place_of(i):
    return (i % 8) // 4, i % 4, i // 8


def arrivals():
    table = []
    for sends in ROUTES:
        by_direction = []
        for (dx, dy, dz), packed in zip(DIRECTIONS, sends):
            entries = []
            for i in range(32):
                x, y, z = place_of(i)
                fx, fy, fz = (x - dx) % 4, (y - dy) % 4, (z - dz) % 4
                entry = packed >> (9 * (fz * 8 + (fx % 2) * 4 + fy)) & 511
                if entry:
                    pair = (fx // 2) * 4 + fz + (entry >> 5 & 7)
                    entry = 256 | (pair - z) % 8 << 5 | entry & 31
                entries.append(entry)
            by_direction.append(entries)
        table.append(by_direction)
    return table


def departures():
    return [[[packed >> (9 * i) & 511 for i in range(32)] for packed in sends] for sends in ROUTES]


def words(table):
    return [
        [[d[i] | e[i] << 9 | f[i] << 18 for i in range(32)] for d, e, f in (sends[:3], sends[3:])]
        for sends in table
    ]


def looked_up(values, bits):
    if len(set(values)) == 1:
        return jnp.int32(values[0])
    low = looked_up(values[: len(values) // 2], bits[:-1])
    high = looked_up(values[len(values) // 2 :], bits[:-1])
    return jnp.where(bits[-1], high, low)


def gather_members(x_ref, held, send, recv, across_send, across_recv, own_sem, greet_all):
    r, c = here()
    core = lax.rem(c, 2)
    pair = lax.div(c, 2)
    z = lax.rem(pair, 4)
    x = lax.div(pair, 4) * 2 + lax.div(r, 4)
    y = lax.rem(r, 4)
    first = core == 0
    sign = 1 - 2 * core
    index = jnp.where(first, z * 8 + r, (3 - z) * 8 + 7 - r)
    bits = [lax.rem(lax.div(index, 2**b), 2) == 1 for b in range(5)]

    def neighbour(direction):
        dx, dy, dz = DIRECTIONS[direction]
        nx, ny, nz = (lax.rem(v + sign * d + 4, 4) for v, d in ((x, dx), (y, dy), (z, dz)))
        return lax.rem(nx, 2) * 4 + ny, lax.div(nx, 2) * 8 + nz * 2 + core

    sides = [neighbour(d) for d in range(6)]
    other = (r, c + sign)

    across = lax.div(lax.rem(2 * pair - 4 + r + 2 - core - lax.rem(r, 2) + COLS, COLS), 2)

    own = pltpu.make_async_copy(x_ref, held.at[pair, r], own_sem)
    own.start()
    greet_all(sides)
    own.wait()

    def unit(entry):
        relative = lax.rem(lax.div(entry, 32), 8)
        row = lax.rem(lax.div(entry, 4), 8)
        block = lax.rem(pair + sign * relative + 8, 8)
        row = jnp.where(first, row, 7 - row)
        quarter = pl.multiple_of(lax.rem(entry, 4) * QUARTER, QUARTER)
        return block, row, pl.ds(quarter, QUARTER)

    def entries(table):
        found = []
        for word in table:
            word = looked_up(word, bits)
            found += [lax.rem(word, 512), lax.rem(lax.div(word, 512), 512), lax.div(word, 512 * 512)]
        return found

    piece = held.at[pair, r, pl.ds(0, QUARTER)]

    def pass_across(block, row, part):
        @pl.when(block == across)
        def _():
            copied(held.at[block, row, part], held.at[8, row, part], across_send, across_recv, *other).start()

    def take(step):
        for d, entry in enumerate(entries(incoming[step])):
            @pl.when(entry >= 256)
            def _(d=d, entry=entry):
                block, row, part = unit(entry)
                ref = held.at[block, row, part]
                pltpu.make_async_copy(ref, ref, recv.at[step, d]).wait()
                pass_across(block, row, part)

    incoming, outgoing = words(arrivals()), words(departures())
    pass_across(pair, r, pl.ds(0, MEMBERS // ROWS))
    rounds = len(ROUTES)
    for step in range(rounds + LAG):
        if step >= LAG:
            take(step - LAG)
        if step < rounds:
            for d, entry in enumerate(entries(outgoing[step])):
                @pl.when(entry >= 256)
                def _(d=d, entry=entry):
                    block, row, part = unit(entry)
                    ref = held.at[block, row, part]
                    copied(ref, ref, send.at[step, d], recv.at[step, d], *sides[d]).start()

    def finish():
        for step in range(rounds):
            for d, entry in enumerate(entries(outgoing[step])):
                @pl.when(entry >= 256)
                def _(d=d):
                    copied(piece, piece, send.at[step, d], recv.at[step, d], *sides[d]).wait_send()
        copied(held.at[pair], held.at[8], across_send, across_recv, *other).wait_send()

    copied(held.at[pair], held.at[8], across_send, across_recv, *other).wait_recv()
    return finish


def parted(values):
    high = values.astype(jnp.bfloat16)
    low = (values - high.astype(jnp.float32)).astype(jnp.bfloat16)
    return high, low


def dotted(a, b, dims):
    return lax.dot_general(a, b, (dims, ((), ())), preferred_element_type=jnp.float32)


def skewed(rows, shift):
    sub = lax.broadcasted_iota(jnp.int32, rows.shape, 0)
    if shift:
        rows = pltpu.roll(rows, SPAN - shift, 1)
    for bit in (1, 2, 4):
        rows = jnp.where((sub & bit) != 0, pltpu.roll(rows, SPAN - bit, 1), rows)
    return rows[:, :BLOCK]


def main_kernel(
    members_ref, w_ref, local_out, out_ref,
    held, xh, xl, band_ref, high_ref, low_ref, local_ref,
    iterate, near, window, wide, parts, sums, square_ref, row_squares, col_squares, row_total,
    member_send, member_recv, across_send, across_recv, own_sem, store_sem, send_z, recv_z, send_w, recv_w, send_x, recv_x, send_y, recv_y, send_r, recv_r, send_c, recv_c,
):
    r, c = here()
    core = lax.rem(c, 2)
    pair = lax.div(c, 2)
    other = (r, c + 1 - 2 * core)
    shared = 1 - core
    passes = core == lax.rem(r + 1, 2)

    def greet_all(sides):
        barrier = pltpu.get_barrier_semaphore()
        partners = list(sides)
        for shift in range(1, ROWS):
            row = lax.rem(r + shift, ROWS)
            partners += [(row, 2 * pair), (row, 2 * pair + 1)]
        for shift in range(1, COLS):
            partners.append((r, lax.rem(c + shift, COLS)))
        for row, col in partners:
            pl.semaphore_signal(barrier, inc=1, device_id=at(row, col), device_id_type=MESH)
        pl.semaphore_wait(barrier, len(partners))

    def to_pairs(step, half, source, away):
        col = lax.rem(c - 2 * away + COLS, COLS)
        slot = step, half, away + 2
        return copied(source, near.at[slot], send_z.at[slot], recv_z.at[slot], r, col)

    def targets(away):
        found = []
        for e in range(3):
            row = 2 * away + core + 2 + e
            valid = None
            if away == -2:
                if e == 0:
                    continue
                valid = core == 1 if e == 1 else None
            if away == 2:
                if e == 2:
                    continue
                valid = core == 0 if e == 1 else None
            there = (1, core, 0)[e]
            panel = (1, shared, 0)[e]
            found.append(((away + 2) * 3 + e, row, there, panel, valid))
        return found

    def share(step, half, source, away, act):
        for slot, row, there, panel, valid in targets(away):
            own = (row == r) & (there == core)
            go = jnp.logical_not(own)
            if valid is not None:
                own, go = own & valid, go & valid

            @pl.when(go)
            def _(slot=slot, row=row, there=there, panel=panel):
                act(copied(
                    source, window.at[step, half, panel, r], send_w.at[step, half, slot],
                    recv_w.at[step, half, panel, r], row, 2 * pair + there,
                ), True)

            @pl.when(own)
            def _(panel=panel):
                act(pltpu.make_async_copy(
                    source, window.at[step, half, panel, r], recv_w.at[step, half, panel, r]
                ), False)

    def begin(copy, remote):
        copy.start()

    def send_iterate(step, half):
        source = iterate.at[step, half]
        for away in (-2, 2, -1, 1):
            to_pairs(step, half, source, away).start()
        share(step, half, source, 0, begin)

    def spread_iterate(step, half):
        for away in (-1, 1, -2, 2):
            block = near.at[step, half, away + 2]
            pltpu.make_async_copy(block, block, recv_z.at[step, half, away + 2]).wait()
            share(step, half, block, away, begin)

    def across_copy(step, half):
        return copied(
            window.at[step, half, shared], window.at[step, half, 1 - shared],
            send_x.at[step, half], recv_x.at[step, half], *other
        )

    def landed(step, half, panel):
        for row in range(ROWS):
            block = window.at[step, half, panel, row]
            pltpu.make_async_copy(block, block, recv_w.at[step, half, panel, row]).wait()

    def widened(step, half, panel):
        for row in range(ROWS):
            packed = window[step, half, panel, row]
            values = jnp.concatenate([packed, pltpu.roll(packed, HALF, 1)], 0)
            high = values.astype(jnp.bfloat16).astype(jnp.float32)
            low = pltpu.roll(values - high, HALF, 1)
            first = pl.multiple_of((panel * ROWS + row) * PIECE, PIECE)
            wide[half, pl.ds(first, PIECE), :] = jnp.where(left, high, low).astype(jnp.bfloat16)

    def take_iterate(step, half):
        @pl.when(passes)
        def _():
            landed(step, half, shared)
            across_copy(step, half).start()
            widened(step, half, shared)

        landed(step, half, core)
        widened(step, half, core)

        @pl.when(jnp.logical_not(passes))
        def _():
            across_copy(step, half).wait_recv()
            widened(step, half, shared)

    left = lax.broadcasted_iota(jnp.int32, (PIECE, PIECE), 1) < HALF
    left_half = left[:HALF]

    finish = gather_members(
        members_ref, held, member_send, member_recv, across_send, across_recv, own_sem, greet_all
    )
    top, bottom = w_ref[:HALF, :], w_ref[HALF:, :]
    iterate[0, 0] = jnp.where(left_half, top, pltpu.roll(bottom, HALF, 1))
    iterate[0, 1] = jnp.where(left_half, pltpu.roll(top, HALF, 1), bottom)
    for half in range(2):
        send_iterate(0, half)
    for half in range(2):
        spread_iterate(0, half)

    near_block = lax.div(lax.rem(c + r - 4 + COLS, COLS), 2)
    far_block = lax.div(lax.rem(c + r - 3 + COLS, COLS), 2)
    odd = lax.rem(r, 2) == 1
    for panel, block in enumerate((pair, jnp.where(odd, 8, near_block), jnp.where(odd, far_block, 8))):
        for first in range(0, BLOCK, SUB):
            values = held[block, :, :, first : first + SUB].reshape(MEMBERS, SUB)
            centered = values - jnp.sum(values, 0, keepdims=True) / MEMBERS
            spread = jnp.sqrt(jnp.sum(centered * centered, 0, keepdims=True) + epsilon)
            high, low = parted(centered / spread)
            lo_at = (panel - 1) * BLOCK + first if panel else 2 * BLOCK + first
            xh[:, lo_at : lo_at + SUB] = high
            xl[:, lo_at : lo_at + SUB] = low
    squares = jnp.zeros((8, 128), jnp.float32)
    gap = lax.broadcasted_iota(jnp.int32, (SUB, SPAN), 1) - lax.broadcasted_iota(jnp.int32, (SUB, SPAN), 0)
    taper = jnp.maximum(0.0, 1.0 - jnp.abs(gap + (r * BLOCK - WINDOW)).astype(jnp.float32) / WINDOW)
    taper = jnp.where((gap >= 0) & (gap < BLOCK), taper, 0.0)
    for tile in range(BLOCK // SUB):
        first = tile * SUB
        rows_h = xh[:, 2 * BLOCK + first : 2 * BLOCK + first + SUB]
        rows_l = xl[:, 2 * BLOCK + first : 2 * BLOCK + first + SUB]
        cols_h = xh[:, first : first + SPAN]
        cols_l = xl[:, first : first + SPAN]
        over = ((0,), (0,))
        gram = dotted(rows_h, cols_h, over) + (dotted(rows_h, cols_l, over) + dotted(rows_l, cols_h, over))
        band = gram * taper
        band_ref[tile] = band
        high, low = parted(band)
        high_ref[tile] = high
        low_ref[tile] = low
        squares = squares + jnp.sum((band * band).reshape(SUB // 8, 8, SPAN // 128, 128), (0, 2))
    square_ref[...] = squares

    for shift in range(1, ROWS):
        copied(square_ref, row_squares.at[r], send_r.at[shift], recv_r.at[r], lax.rem(r + shift, ROWS), c).start()
    pltpu.make_async_copy(square_ref, row_squares.at[r], recv_r.at[r]).start()

    stores = []

    def skew(tile):
        first = tile * SUB
        for group in range(0, SUB, 8):
            local_ref[first + group : first + group + 8, :] = skewed(band_ref[tile, group : group + 8, :], group)
        stores.append(pltpu.make_async_copy(local_ref.at[first : first + SUB], local_out.at[first : first + SUB], store_sem.at[tile]))
        stores[-1].start()

    def piece_out(step, half, row):
        return copied(
            parts.at[step, half, row * HALF : (row + 1) * HALF], sums.at[step, half, r],
            send_y.at[step, half, row], recv_y.at[step, half, r], row, c,
        )

    def product(step, half):
        for tile in range(BLOCK // SUB):
            first = tile * SUB
            over = ((1,), (0,))
            near_rows = wide[half, first : first + SPAN, :]
            both = dotted(high_ref[tile], near_rows, over) + dotted(low_ref[tile], near_rows, over)
            both = both + pltpu.roll(both, HALF, 1)
            for row in range(first // PIECE, (first + SUB) // PIECE):
                rows = both[row * PIECE - first : (row + 1) * PIECE - first]
                parts[step, half, row * HALF : (row + 1) * HALF, :] = jnp.where(left_half, rows[:HALF], rows[HALF:])
                unless(r == row, lambda row=row: piece_out(step, half, row).start())

    def sent(step):
        for half in range(2):
            for away in (-2, -1, 1, 2):
                to_pairs(step, half, iterate.at[step, half], away).wait_send()
            for away in range(-2, 3):
                share(
                    step, half, iterate.at[step, half], away, lambda copy, remote: copy.wait_send() if remote else None
                )
            pl.when(passes)(lambda half=half: across_copy(step, half).wait_send())

    def pieces_sent(step):
        for half in range(2):
            for row in range(ROWS):
                unless(r == row, lambda half=half, row=row: piece_out(step, half, row).wait_send())

    total = None
    summed = [power_terms[0] * iterate[0, half] for half in range(2)]
    for step in range(STEPS):
        for half in range(2):
            take_iterate(step, half)
            product(step, half)
        if step == 0:
            for row in range(ROWS):
                pltpu.make_async_copy(square_ref, row_squares.at[row], recv_r.at[row]).wait()
            row_total[...] = jnp.sum(row_squares[...], 0)
            for shift in range(1, COLS):
                copied(row_total, col_squares.at[c], send_c.at[shift], recv_c.at[c], r, lax.rem(c + shift, COLS)).start()
            pltpu.make_async_copy(row_total, col_squares.at[c], recv_c.at[c]).start()
            skew(0)
            for col in range(COLS):
                pltpu.make_async_copy(row_total, col_squares.at[col], recv_c.at[col]).wait()
            total = jnp.sum(jnp.sum(col_squares[...], 0), keepdims=True) / STATES
        else:
            sent(step)
            pieces_sent(step - 1)
        for half in range(2):
            own = pl.multiple_of(r * HALF, HALF)
            vector = parts[step, half, pl.ds(own, HALF), :]
            for row in range(ROWS):
                def arrived(half=half, row=row):
                    block = sums.at[step, half, row]
                    pltpu.make_async_copy(block, block, recv_y.at[step, half, row]).wait()

                unless(r == row, arrived)
                vector = vector + jnp.where(r == row, 0.0, sums[step, half, row])
            vector = vector / total
            summed[half] = summed[half] + power_terms[step + 1] * vector
            if step < STEPS - 1:
                iterate[step + 1, half] = vector
                send_iterate(step + 1, half)
        if step < STEPS - 1:
            for half in range(2):
                spread_iterate(step + 1, half)
            if step == 0:
                skew(1)
                finish()
                sent(0)
            else:
                skew(2)
                skew(3)
                for shift in range(1, ROWS):
                    copied(square_ref, row_squares.at[r], send_r.at[shift], recv_r.at[r], lax.rem(r + shift, ROWS), c).wait_send()
                for shift in range(1, COLS):
                    copied(row_total, col_squares.at[c], send_c.at[shift], recv_c.at[c], r, lax.rem(c + shift, COLS)).wait_send()
    even, other_half = summed
    root = jnp.sqrt(total)
    out_ref[:HALF, :] = root * jnp.where(left_half, even, pltpu.roll(other_half, HALF, 1))
    out_ref[HALF:, :] = root * jnp.where(left_half, pltpu.roll(even, HALF, 1), other_half)
    for copy in stores:
        copy.wait()
    pieces_sent(STEPS - 1)


def band_and_sample(members, probes):
    return pl.pallas_call(
        main_kernel,
        name="band_and_sample",
        out_shape=(
            jax.ShapeDtypeStruct((BLOCK, BLOCK), jnp.float32),
            jax.ShapeDtypeStruct((PIECE, PIECE), jnp.float32),
        ),
        in_specs=[pl.BlockSpec(memory_space=pl.ANY), pl.BlockSpec(memory_space=pltpu.VMEM)],
        out_specs=[pl.BlockSpec(memory_space=pl.ANY), pl.BlockSpec(memory_space=pltpu.VMEM)],
        scratch_shapes=[
            pltpu.VMEM((9, ROWS, MEMBERS // ROWS, BLOCK), jnp.float32),
            pltpu.VMEM((MEMBERS, 3 * BLOCK), jnp.bfloat16),
            pltpu.VMEM((MEMBERS, 3 * BLOCK), jnp.bfloat16),
            pltpu.VMEM((BLOCK // SUB, SUB, SPAN), jnp.float32),
            pltpu.VMEM((BLOCK // SUB, SUB, SPAN), jnp.bfloat16),
            pltpu.VMEM((BLOCK // SUB, SUB, SPAN), jnp.bfloat16),
            pltpu.VMEM((BLOCK, BLOCK), jnp.float32),
            pltpu.VMEM((STEPS, 2, HALF, PIECE), jnp.float32),
            pltpu.VMEM((STEPS, 2, 5, HALF, PIECE), jnp.float32),
            pltpu.VMEM((STEPS, 2, 2, ROWS, HALF, PIECE), jnp.float32),
            pltpu.VMEM((2, 2 * BLOCK, PIECE), jnp.bfloat16),
            pltpu.VMEM((STEPS, 2, BLOCK // 2, PIECE), jnp.float32),
            pltpu.VMEM((STEPS, 2, ROWS, HALF, PIECE), jnp.float32),
            pltpu.VMEM((8, 128), jnp.float32),
            pltpu.VMEM((ROWS, 8, 128), jnp.float32),
            pltpu.VMEM((COLS, 8, 128), jnp.float32),
            pltpu.VMEM((8, 128), jnp.float32),
            pltpu.SemaphoreType.DMA((len(ROUTES), 6)),
            pltpu.SemaphoreType.DMA((len(ROUTES), 6)),
            pltpu.SemaphoreType.DMA,
            pltpu.SemaphoreType.DMA,
            pltpu.SemaphoreType.DMA,
            pltpu.SemaphoreType.DMA((BLOCK // SUB,)),
            pltpu.SemaphoreType.DMA((STEPS, 2, 5)),
            pltpu.SemaphoreType.DMA((STEPS, 2, 5)),
            pltpu.SemaphoreType.DMA((STEPS, 2, 15)),
            pltpu.SemaphoreType.DMA((STEPS, 2, 2, ROWS)),
            pltpu.SemaphoreType.DMA((STEPS, 2)),
            pltpu.SemaphoreType.DMA((STEPS, 2)),
            pltpu.SemaphoreType.DMA((STEPS, 2, ROWS)),
            pltpu.SemaphoreType.DMA((STEPS, 2, ROWS)),
            pltpu.SemaphoreType.DMA((ROWS,)),
            pltpu.SemaphoreType.DMA((ROWS,)),
            pltpu.SemaphoreType.DMA((COLS,)),
            pltpu.SemaphoreType.DMA((COLS,)),
        ],
        compiler_params=pltpu.CompilerParams(
            collective_id=1, has_side_effects=True, vmem_limit_bytes=VMEM_LIMIT
        ),
    )(members, probes)


def on_device(perturbations, probes):
    return band_and_sample(perturbations, probes)


def solution(mesh):
    return jax.shard_map(
        on_device,
        mesh=mesh,
        in_specs=(P("row", "col"), P(("col", "row"), None)),
        out_specs=(P("col", "row"), P(("col", "row"), None)),
        check_vma=False,
    )
```

```python
import functools
import math

import jax
import jax.numpy as jnp
from jax import lax
from jax.experimental import pallas as pl
from jax.experimental.pallas import tpu as pltpu
from jax.sharding import PartitionSpec as P

MEMBERS = 512
STATES = 16384
WINDOW = 4096
ROWS = 8
COLS = 16
BLOCK = 1024
PIECE = 128
SUB = 256
SPAN = SUB + BLOCK
STEPS = 3
MESH = pl.DeviceIdType.MESH
VMEM_LIMIT = 58 * 2**20

epsilon = 1e-06
power_terms = (
    2.0 / math.pi - 4.0 / (3.0 * math.pi) - 4.0 / (15.0 * math.pi) - 4.0 / (35.0 * math.pi),
    8.0 / (3.0 * math.pi) + 32.0 / (15.0 * math.pi) + 72.0 / (35.0 * math.pi),
    -32.0 / (15.0 * math.pi) - 192.0 / (35.0 * math.pi),
    128.0 / (35.0 * math.pi),
)

ROUTES = (
    (0x22f1386c260b0000000000086c260d0100000000086c260b0100000000086c2a0d01, 0x8e4622f130000000008ec6a2b100000001008f4662b1087c2c01038ec6a2d130042e0d01, 0x8fc622b1386c220b018ec6e2f1086c260d008fc66291386c2e0f018ec622b1186c2a0903, 0x8ec6e2f1386c2209008ec622d11864260b038fc662f1387c260b038ec6a2f118742a0d00, 0x8ec6629100000001038fc6e2b118742e0d010046a2c008742a0b01004622f1086c2e0b01, 0x8e4622f1286c2a0f038f46a2b12004220b018e4622d1386c24010000468000087c220f03),
    (0x8642e0d0200000000087c2e09000000000008642a0f0300000000087c220b02, 0x8fc662d120000000008f46e2f120000000008ec6229110000000008e46e29120042a0b00, 0x8e46e2912864260d028f4622d1287c220b018f46a2f108742a09028f46e2f128742e0d01, 0x8fc622d1087c2e0d028fc6a2f1387c220f018e46e2b1286c2a0f028e4622b1387c260f03, 0x8f46a2b110000000008e46401138642609020046c000087c220d02000000113864260f02, 0x8fc6a2d11874220b01004622d100042800000046e2b128642c0103000000000864260800),
    (0x87c2a0901000000000874220f03000000000874220d00000000000864260903, 0x8ec6e29100000000008e4622d110000000008fc6a2d130000000008fc662f10000000102, 0x8f4662f1187c2a0f038e4662b118742a09028e46e2b1187c260b008e46a2d1087c220b02, 0x8e4662b128642a0b018e4662b1086c2a0d028f4622d108642e0d008fc6e2d10864220901, 0x46e2d120000000008e800011287c220b03000000000004260800000000112874220d00, 0x8e8022913004260c000046e29130042c00000046a2f10004200101000000000000000000),
    (0x4260b1f844360f0300476311d84caa4f0200452320087ca21305005e6e9708543a0f63, 0x89eea27f1006a34fe18ffebed16f77a8000089fe227f0f680203108f4e2231796c10010d, 0x86c6a2d1f8e416030086c6a2132f742fcb038ecea6b1285c662b0d8fde66d1d8646a2d13, 0x8f4260b17807afcde19e426290187433cb2389c6a6b1181c2209e19e4660d128ec2e1502, 0xffc77eb00007af2f938d802218084c6a2b0dc7c7c0117004660f0dbec770d118543a1503, 0x89c563717d7c174fa39e45e0d1d9680000009f47e0b1f8f43c0105004570d818eca62d20),
    (0x47e271684c3e04000047e21328443e0121004e80130854aa4b0e89deaeb7181cae0720, 0xffc5225f3d66a7490489fee291e00000000089472331ff600215e188c6235159646a0312, 0x86452251cf642e2e008c0026f1e86417cd2386ce2211e8f41fcb0e8dcee231e85c6e2900, 0x8846a0d11877a7c9e29fc2e0900f743e13e18e80229158f43fcbe287dea6b158e43e0a00, 0x8842e0d1cf6000000088c5a25160046e030f0000237830046229e2bf62e25700046e2c00, 0x864762700816a2110489c26091797002110f0045e0f0381caa2902004e30b808e46e290d),
    (0x45e250280432020000000000086436152300000013384cae1521bf5eeed72844160307, 0x89456371e0000207a38846633150000204008862e37f3f7000011189e2e2b1d004662f0e, 0x8c002271e8ffa206009f8026d138541bc912864626d1ff6c13cf038d5ee6b33844662f10, 0x42a0915814362fe38f46e69128ec3611009f0026932877ae2de0885ee6f168fc321200, 0x87c6209f1f780000008cc20011c004622f050000223f384c1e1313005ee21168fc66050f, 0x452090280ea615069fc720f03004a4010e87426311e8ec34010f0062c018285c320706),
    (0x4360f0d8741a000000442133785ca2199d0044c0135a6c161707af5f40160874be1500, 0x8f6d7e1f2007276dc088c5623f7e7fe401c388c4e211c8cfba270b8c4f231119f4762310, 0x8445a4d1084c62091c9e4aa091cf7febec008cca2691d854220de08c4daab13004e22200, 0x4364d218ffebd7e680c2277158f7a3cfe5ae0024d01f0fe3d5f0af5f6290186c3be800, 0xfdc523f61f4e270bed86c40011d004360107b6802131d89c562bf0bce10011f8d46a27f3, 0x47a131edec070bc099caa350d91e7730009d4660d1d816521106d6cfc018d96c5a1517),
    (0x4720501f740211960043e1763854a605240044249378140e092fafdaef57ca652a050b, 0x887623f11006ef68008dffe3d180079401168e7f7ef15007961a009dcde371c91c62130f, 0x848024b0c85c5febf18d4de4f20e7f9a0e00ae4aa4b32f646bcc0086c664b2000427ea00, 0x24b038e7efd3e49647e4f1789fe3e8009980231168ec3233018f5ae0b1780473ee00, 0x8944a390cf0e7f27ef8047ff600f0c2a07eeb65ae3d90f143e331fb844401608dc522915, 0x43e230dde6ef6996964de23029149721099c4a6250e896eb3304d64eb039288c3e0515),
    (0x43223f68541e17e5004d400009741a0b2600000012385c3a0502b7de2f751a7c321f2f, 0x8dc5be5fc006b346008900231170079c00008ac6e2f12fff9c0000886123b1f9ee2e211d, 0x8e8024f20f441fc3f39ecda49228e4122c00aecd62523864162ded854a60d23ff45e2a00, 0x4ae4901f77a3ebf188c3e371681fbbec00af8020d14807e7cdf3975e64b0689c7fea00, 0xfcfa21506f165f259fb75abe334f4c7629f3b756ecd6183c32011eb7df401638f4322b1d, 0x8043631188443801ad00436151e90e7c010899c7a150d8840e3716006132f359647e3525),
    (0x45a1b0882c0607e7004a2193b82c864a00000000126845261f2ead5d2ff63a4c36514d, 0x8b77e3115006db55b78a80221d3eefd401f7000023bf6fd787711c9b002331e9c6d22b11, 0x8749a232d8c41bee00844d6673feefd62e008d4de4f1cfd463e60087de24f1cef41bca00, 0xa68026d4089c3ff503a680253438e46bd200a6802750588feff00000002090281c37ca00, 0xf8c1b0760f1e370febb7c07d3fdf9c7a1b0accdbb2791f847a210abde7401718c43607f4, 0x90c1a1b10d5ed801b795412011c0064313b7944e2170c88c4c01b5df62b238e004363111),
    (0x402010981420010b004bc01278343a1a00000000134a143e5129ac002d76ca0cb6174f, 0x88f6a3c00e0f6344008b803fd1ae17d801ff8b7c62518fdfd36000890023d1b914023713, 0x87cee6932e6c13c000964a6633cfd41e22008dcda2d2dfdc1bc400865d2292e8cc53e600, 0xa60026932894261400a78021314f9feff3f4a98026d0380c7beff5a600271148f7a7f400, 0xf77c23118f367305ec885e70596f2c4e0f1800597158b824720715b95c8016c8442a091c, 0x4421908d8ee8018d9bcda05180063f4bb6954de09198564f491cd1e631337994721f04),
    (0x42a3d9683c380000000000138824325400a7800015ca1c361d28ad802d400a148e1800, 0x8ac6a21d5e4ebf74008b002371bee79800008a00231f1ff62c00008b00225c19844e391c, 0x854966f1de4c53e1fc8fc9e8d01ee46be800acc96472184c6fec0094dae4d2df7c17e400, 0xa700256008efe3ee00898026d3180fbff000a60025517f87f7f200a78026d0580803f600, 0xf07dba31df26332382004180170f3c5a15febfc4b1bfff540e0512005e401668cc5e03ff, 0x42e1715006d40181904063311946d7170c994b63d0185c3001b7dee77219d9dcae3b08),
    (0x6d6210e85c161e0000486e7298142a0600a5000015d824320600a4002f94d84c0e1b4b, 0x8d446231de9eb77000000022713e8790000000003e514f9fcf53fa8a803c71698cce191f, 0x8dc9e630ee6467c60087c9a653de5c622800854d20f3e84003ea00845ea652ced4100000, 0xaf0025536ffc33f600a18020f77817b3a9d7a80024b07897a7e800a88024f0781003ce00, 0xfe78793e50065b1b8dbcdd40171fac7233e7bd5f63f9c8e42e2ff6bc5e0000084c0e231e, 0x934aa210e006b001a69b4fa2f00006a319b29ac2a05148479f53b0dc6672b919b6d23336),
    (0x47a03fd83408000000002d54183c0e4600000000122a0c121800a5002fb4f85ca2114c, 0x22bdde96f35e008a00239fde8f6c000000002231dfc6bc01f80000001c0956ce3f07, 0x9dcd2472ef7003ca0087492411d85c67c00087cae632fff80228008c802493dec003c400, 0xa180253e7f8fbbe800a143a1503807ebcc00a100217068ffebd600a98025504c9803d600, 0x82fefb7fc00603019600594017ff34123df9bdd8703f2fac3617fbba60000000043e1ffe, 0x994e22b0f006fc01b194c9e371b006bc01ad80c961f1a8fe4001b3d166b3790954a22723),
    (0x44211608240c000000002db2400416500000000014ca4516112ca7002cd7da1c060000, 0x23b14e2f2f7ba8007ca3f14e57ec00008b803e11af46c3560000000011a95f6b731e, 0x8cc92420087003cc0085802013ee5003e00084802410df4003c800870020f1fed803e200, 0xa78027400f7ff60e00ae0020a008843bc800a00020900887b38a00a00025700f7fb3d400, 0xf6f9801f20062b3d88005d8019df24321ff8bf5d00126f04763be5b5dd000000047239e2, 0x92cde330a0040c01b593c3a2704004b801bb9bc8e291c8d6f401a3d864f398f95c7a692f),
    (0x41e1d76004d4000000000016b0041e4c00000000140a74020000ac802f378a340a1c00, 0x2331beaeff720000003ffdffe7580000000023ff2fcf235800000000114946123c00, 0x8d0026400ff803e80086002452100003c400840020d3ce5003e5fe9d802413fe441fc600, 0xae8026a008f43a1000a80024a008942fd000a18027200f07a3ce00ae0024c00880039200, 0xf87e401e7000032189bbd9c0127fa40a2d1eb9dcc017af740625ecbd5ac00000047e3ff5, 0x9b4c6340000000018e98cc63f070068401a99b47635110000001a6d8ecf1993944f27726),
    (0x406c55f00550000000002c37000408000000000014300406020000002c945a24b21200, 0x235d7eb7236600000023bd2ebf68000000002351b0073c00000000001189fe4e1000, 0x960024400e5003e4008c802292f8c803ee00958024d3de78022e00848022521e50000000, 0xa90027000887fff2009700256008fff2080088800000081473c800a90024800890038800, 0xf3ffc01840067b0376005980000004661910bc59c0178f4c46230cb2d9800000047a1deb, 0x9a4161c000000001a49ac321d1f0000001b892cd221020000001b4d56033f9c004dc0124),
    (0x420015000410000000000017c0048c000000000015000538000000002f15c0052c0000, 0x119e3ef8000000000011fe5f5400000000001170075400000000000009d6c00000, 0x26000e5803ce00000022400000000000000026400f70000000000026200e7003cc00, 0xa0000000000003a800af0000000000038e0081000000000003d200a70025000007bfcc00, 0xfe80000000064311810059000000000001f2b459000000000001fe005e800000000001e8, 0x93ce401190000001a89349000000000001a79a49238000000001a2d5800019f00000013c),
    (0x438015100000000000000015a000000000000000151000000000000000152004000000, 0x11ae377c0000000000000eaf300000000000000007040000000000000007740000, 0xe40000000000000000e70000000000024400000000000000024400ec8000000, 0xa8002720000003b60000000000000003f60000000000000000000090800000000003f200, 0x61f1d7dbe53800000000001fabcd8000000000001e00000000000000001fa, 0x924c8011a0000000009246400000000001a195c9c0000000000000d40033d87000000121),
    (0x17d00000000000000015800000000000000014600000000000000014b000000000, 0xe27680000000000000e077c0000000000000006f400000000001e4000000000, 0xe48000000000000000000000000000000000ef803c800, 0xa08000000000000000000000000000000000000000000000000000a10000000000000000, 0x604018e005ec00000000000000056400000000001f9000000000000000000, 0x1a4000000000000000000df803119e000000122),
    (0x17100000000000000015900000000000000014c000000000, 0xea7700000000000000e4f200000000000000006fc0000000000000000000000, 0x0, 0xa88000000000000000000000000000000000000000000000000000000000000000000000, 0x6200000000000000000000000000000000000000000000000000000000000, 0x1ae000000000000000000dd0000000000000000),
    (0x19d000000000000000000000000000000000147000000000, 0xedf5c0000000000000007240000000000000000000000000000000000000000, 0x0, 0xa10000000000000000000000000000000000000000000000000000000000000000000000, 0x6380000000000000000000000000000000000000000000000000000000000, 0x0),
)


def here():
    return lax.axis_index("row"), lax.axis_index("col")


def at(row, col):
    return {"row": row, "col": col}


def unless(own, step):
    if own is None:
        step()
    else:
        pl.when(jnp.logical_not(own))(step)


def copied(src, dst, send, recv, row, col):
    return pltpu.make_async_remote_copy(
        src_ref=src, dst_ref=dst, send_sem=send, recv_sem=recv,
        device_id=at(row, col), device_id_type=MESH,
    )


DIRECTIONS = ((1, 0, 0), (-1, 0, 0), (0, 1, 0), (0, -1, 0), (0, 0, 1), (0, 0, -1))
QUARTER = MEMBERS // ROWS // 4
LAG = 3
UNITS = 4 * ROWS


def place_of(i):
    return (i % 8) // 4, i % 4, i // 8


def arrivals():
    table = []
    for sends in ROUTES:
        by_direction = []
        for (dx, dy, dz), packed in zip(DIRECTIONS, sends):
            entries = []
            for i in range(32):
                x, y, z = place_of(i)
                fx, fy, fz = (x - dx) % 4, (y - dy) % 4, (z - dz) % 4
                entry = packed >> (9 * (fz * 8 + (fx % 2) * 4 + fy)) & 511
                if entry:
                    pair = (fx // 2) * 4 + fz + (entry >> 5 & 7)
                    entry = 256 | (pair - z) % 8 << 5 | entry & 31
                entries.append(entry)
            by_direction.append(entries)
        table.append(by_direction)
    return table


def departures():
    return [[[packed >> (9 * i) & 511 for i in range(32)] for packed in sends] for sends in ROUTES]


def words(table):
    return [
        [[d[i] | e[i] << 9 | f[i] << 18 for i in range(32)] for d, e, f in (sends[:3], sends[3:])]
        for sends in table
    ]


def looked_up(values, bits):
    if len(set(values)) == 1:
        return jnp.int32(values[0])
    low = looked_up(values[: len(values) // 2], bits[:-1])
    high = looked_up(values[len(values) // 2 :], bits[:-1])
    return jnp.where(bits[-1], high, low)


def gather_members(x_ref, held, send, recv, across_send, across_recv, own_sem, greet_all):
    r, c = here()
    core = lax.rem(c, 2)
    pair = lax.div(c, 2)
    z = lax.rem(pair, 4)
    x = lax.div(pair, 4) * 2 + lax.div(r, 4)
    y = lax.rem(r, 4)
    first = core == 0
    sign = 1 - 2 * core
    index = jnp.where(first, z * 8 + r, (3 - z) * 8 + 7 - r)
    bits = [lax.rem(lax.div(index, 2**b), 2) == 1 for b in range(5)]

    def neighbour(direction):
        dx, dy, dz = DIRECTIONS[direction]
        nx, ny, nz = (lax.rem(v + sign * d + 4, 4) for v, d in ((x, dx), (y, dy), (z, dz)))
        return lax.rem(nx, 2) * 4 + ny, lax.div(nx, 2) * 8 + nz * 2 + core

    sides = [neighbour(d) for d in range(6)]
    other = (r, c + sign)

    own_units = pl.ds(pl.multiple_of((pair * ROWS + r) * 4, 4), 4)
    across = lax.div(lax.rem(2 * pair - 4 + r + 2 - core - lax.rem(r, 2) + COLS, COLS), 2)

    own = pltpu.make_async_copy(x_ref, held.at[own_units], own_sem)
    own.start()
    greet_all(sides)
    own.wait()

    def unit(entry):
        relative = lax.rem(lax.div(entry, 32), 8)
        row = lax.rem(lax.div(entry, 4), 8)
        block = lax.rem(pair + sign * relative + 8, 8)
        row = jnp.where(first, row, 7 - row)
        return block, row * 4 + lax.rem(entry, 4)

    def entries(table):
        found = []
        for word in table:
            word = looked_up(word, bits)
            found += [lax.rem(word, 512), lax.rem(lax.div(word, 512), 512), lax.div(word, 512 * 512)]
        return found

    def across_copy(mine, there):
        return copied(held.at[mine], held.at[there], across_send, across_recv, *other)

    def take(step):
        for d, entry in enumerate(entries(incoming[step])):
            @pl.when(entry >= 256)
            def _(d=d, entry=entry):
                block, number = unit(entry)
                ref = held.at[block * UNITS + number]
                pltpu.make_async_copy(ref, ref, recv.at[step, d]).wait()

                @pl.when(block == across)
                def _():
                    across_copy(block * UNITS + number, 8 * UNITS + number).start()

    incoming, outgoing = words(arrivals()), words(departures())

    @pl.when(pair == across)
    def _():
        across_copy(own_units, pl.ds(8 * UNITS + r * 4, 4)).start()

    rounds = len(ROUTES)
    for step in range(rounds + LAG):
        if step >= LAG:
            take(step - LAG)
        if step < rounds:
            for d, entry in enumerate(entries(outgoing[step])):
                @pl.when(entry >= 256)
                def _(d=d, entry=entry):
                    block, number = unit(entry)
                    ref = held.at[block * UNITS + number]
                    copied(ref, ref, send, recv.at[step, d], *sides[d]).start()

    whole = across_copy(pl.ds(0, UNITS), pl.ds(8 * UNITS, UNITS))
    counts = [sum((packed >> (9 * i) & 256) // 256 for sends in ROUTES for packed in sends) for i in range(32)]
    count = looked_up(counts, bits)

    def finish():
        for total in sorted(set(counts)):
            @pl.when(count == total)
            def _(total=total):
                units = held.at[pl.ds(0, total)]
                copied(units, units, send, recv.at[0, 0], *sides[0]).wait_send()
        whole.wait_send()

    whole.wait_recv()
    return finish


def parted(values):
    high = values.astype(jnp.bfloat16)
    low = (values - high.astype(jnp.float32)).astype(jnp.bfloat16)
    return high, low


def dotted(a, b, dims):
    return lax.dot_general(a, b, (dims, ((), ())), preferred_element_type=jnp.float32)


def skewed(rows, shift):
    sub = lax.broadcasted_iota(jnp.int32, rows.shape, 0)
    if shift:
        rows = pltpu.roll(rows, SPAN - shift, 1)
    for bit in (1, 2, 4):
        rows = jnp.where((sub & bit) != 0, pltpu.roll(rows, SPAN - bit, 1), rows)
    return rows[:, :BLOCK]


def main_kernel(
    members_ref, w_ref, local_out, out_ref,
    held, xh, xl, band_ref, high_ref, low_ref, local_ref,
    iterate, near, window, wide, parts, sums, square_ref, row_squares, col_squares, row_total,
    member_send, member_recv, across_send, across_recv, own_sem, store_sem, send_z, recv_z, send_w, recv_w, send_x, recv_x, send_y, recv_y, send_r, recv_r, send_c, recv_c,
):
    r, c = here()
    core = lax.rem(c, 2)
    pair = lax.div(c, 2)
    other = (r, c + 1 - 2 * core)
    shared = 1 - core
    passes = core == lax.rem(r + 1, 2)

    def greet_all(sides):
        barrier = pltpu.get_barrier_semaphore()
        partners = list(sides)
        for shift in range(1, ROWS):
            row = lax.rem(r + shift, ROWS)
            partners += [(row, 2 * pair), (row, 2 * pair + 1)]
        for shift in range(1, COLS):
            partners.append((r, lax.rem(c + shift, COLS)))
        for row, col in partners:
            pl.semaphore_signal(barrier, inc=1, device_id=at(row, col), device_id_type=MESH)
        pl.semaphore_wait(barrier, len(partners))

    def to_pairs(step, source, away):
        col = lax.rem(c - 2 * away + COLS, COLS)
        return copied(source, near.at[step, away + 2], send_z.at[step], recv_z.at[step, away + 2], r, col)

    def targets(away):
        found = []
        for e in range(3):
            row = 2 * away + core + 2 + e
            valid = None
            if away == -2:
                if e == 0:
                    continue
                valid = core == 1 if e == 1 else None
            if away == 2:
                if e == 2:
                    continue
                valid = core == 0 if e == 1 else None
            there = (1, core, 0)[e]
            panel = (1, shared, 0)[e]
            found.append((row, there, panel, valid))
        return found

    def share(step, source, away, act):
        for row, there, panel, valid in targets(away):
            own = (row == r) & (there == core)
            go = jnp.logical_not(own)
            if valid is not None:
                own, go = own & valid, go & valid

            @pl.when(go)
            def _(row=row, there=there, panel=panel):
                act(copied(
                    source, window.at[step, panel, r], send_w.at[step], recv_w.at[step, panel], row, 2 * pair + there
                ))

            @pl.when(own)
            def _(panel=panel):
                act(pltpu.make_async_copy(source, window.at[step, panel, r], recv_w.at[step, panel]))

    def begin(copy):
        copy.start()

    def send_iterate(step, source):
        for away in (-2, 2, -1, 1):
            to_pairs(step, source, away).start()
        share(step, source, 0, begin)

    def spread_iterate(step):
        for away in (-1, 1, -2, 2):
            block = near.at[step, away + 2]
            pltpu.make_async_copy(block, block, recv_z.at[step, away + 2]).wait()
            share(step, block, away, begin)

    def across_copy(step):
        return copied(
            window.at[step, shared], window.at[step, 1 - shared], send_x.at[step], recv_x.at[step], *other
        )

    def split(step, panel):
        high, low = parted(window[step, panel].reshape(BLOCK, PIECE))
        first = pl.multiple_of(panel * BLOCK, BLOCK)
        wide[pl.ds(first, BLOCK), :PIECE] = high
        wide[pl.ds(first, BLOCK), PIECE:] = low

    def landed(step, panel):
        block = window.at[step, panel]
        pltpu.make_async_copy(block, block, recv_w.at[step, panel]).wait()

    def take_iterate(step):
        @pl.when(passes)
        def _():
            landed(step, shared)
            across_copy(step).start()
            split(step, shared)

        landed(step, core)
        split(step, core)

        @pl.when(jnp.logical_not(passes))
        def _():
            across_copy(step).wait_recv()
            split(step, shared)

    finish = gather_members(
        members_ref, held, member_send, member_recv, across_send, across_recv, own_sem, greet_all
    )
    send_iterate(0, w_ref)
    spread_iterate(0)

    near_block = lax.div(lax.rem(c + r - 4 + COLS, COLS), 2)
    far_block = lax.div(lax.rem(c + r - 3 + COLS, COLS), 2)
    odd = lax.rem(r, 2) == 1
    for panel, block in enumerate((pair, jnp.where(odd, 8, near_block), jnp.where(odd, far_block, 8))):
        for first in range(0, BLOCK, SUB):
            values = held[pl.ds(block * UNITS, UNITS), :, first : first + SUB].reshape(MEMBERS, SUB)
            centered = values - jnp.sum(values, 0, keepdims=True) / MEMBERS
            spread = jnp.sqrt(jnp.sum(centered * centered, 0, keepdims=True) + epsilon)
            high, low = parted(centered / spread)
            lo_at = (panel - 1) * BLOCK + first if panel else 2 * BLOCK + first
            xh[:, lo_at : lo_at + SUB] = high
            xl[:, lo_at : lo_at + SUB] = low
    squares = jnp.zeros((8, 128), jnp.float32)
    gap = lax.broadcasted_iota(jnp.int32, (SUB, SPAN), 1) - lax.broadcasted_iota(jnp.int32, (SUB, SPAN), 0)
    taper = jnp.maximum(0.0, 1.0 - jnp.abs(gap + (r * BLOCK - WINDOW)).astype(jnp.float32) / WINDOW)
    taper = jnp.where((gap >= 0) & (gap < BLOCK), taper, 0.0)
    for tile in range(BLOCK // SUB):
        first = tile * SUB
        rows_h = xh[:, 2 * BLOCK + first : 2 * BLOCK + first + SUB]
        rows_l = xl[:, 2 * BLOCK + first : 2 * BLOCK + first + SUB]
        cols_h = xh[:, first : first + SPAN]
        cols_l = xl[:, first : first + SPAN]
        over = ((0,), (0,))
        gram = dotted(rows_h, cols_h, over) + (dotted(rows_h, cols_l, over) + dotted(rows_l, cols_h, over))
        band = gram * taper
        band_ref[tile] = band
        high, low = parted(band)
        high_ref[tile] = high
        low_ref[tile] = low
        squares = squares + jnp.sum((band * band).reshape(SUB // 8, 8, SPAN // 128, 128), (0, 2))
    square_ref[...] = squares

    for shift in range(1, ROWS):
        copied(square_ref, row_squares.at[r], send_r, recv_r, lax.rem(r + shift, ROWS), c).start()

    stores = []

    def skew(tile):
        first = tile * SUB
        for group in range(0, SUB, 8):
            local_ref[first + group : first + group + 8, :] = skewed(band_ref[tile, group : group + 8, :], group)
        stores.append(pltpu.make_async_copy(local_ref.at[first : first + SUB], local_out.at[first : first + SUB], store_sem.at[tile]))
        stores[-1].start()

    def several(ref, send, recv):
        return copied(ref, ref, send, recv, *other)

    def piece_out(step, row):
        return copied(
            parts.at[step, row * PIECE : (row + 1) * PIECE], sums.at[step * ROWS + r],
            send_y.at[step], recv_y.at[step], row, c,
        )

    def sent(step):
        several(near.at[step, pl.ds(0, 4)], send_z.at[step], recv_z.at[step, 0]).wait_send()
        several(sums.at[pl.ds(0, 11)], send_w.at[step], recv_w.at[step, 0]).wait_send()
        pl.when(passes)(lambda: across_copy(step).wait_send())

    def pieces(step):
        return several(sums.at[pl.ds(step * ROWS, ROWS - 1)], send_y.at[step], recv_y.at[step])

    row_copies = several(row_squares.at[pl.ds(0, ROWS - 1)], send_r, recv_r)
    col_copies = several(col_squares.at[pl.ds(0, COLS - 1)], send_c, recv_c)
    total = None
    summed = power_terms[0] * w_ref[...]
    for step in range(STEPS):
        take_iterate(step)
        for tile in range(BLOCK // SUB):
            first = tile * SUB
            over = ((1,), (0,))
            both = dotted(high_ref[tile], wide[first : first + SPAN, :], over)
            rest = dotted(low_ref[tile], wide[first : first + SPAN, :PIECE], over)
            parts[step, first : first + SUB, :] = both[:, :PIECE] + (both[:, PIECE:] + rest)
            for row in range(first // PIECE, (first + SUB) // PIECE):
                unless(r == row, lambda row=row: piece_out(step, row).start())
        if step == 0:
            row_copies.wait_recv()
            squares = jnp.zeros((8, 128), jnp.float32)
            for row in range(ROWS):
                squares = squares + jnp.where(r == row, square_ref[...], row_squares[row])
            row_total[...] = squares
            for shift in range(1, COLS):
                copied(row_total, col_squares.at[c], send_c, recv_c, r, lax.rem(c + shift, COLS)).start()
            skew(0)
            col_copies.wait_recv()
            squares = jnp.zeros((8, 128), jnp.float32)
            for col in range(COLS):
                squares = squares + jnp.where(c == col, row_total[...], col_squares[col])
            total = jnp.sum(squares, keepdims=True) / STATES
        elif step == 1:
            skew(2)
        else:
            sent(1)
            sent(2)
            pieces(0).wait_send()
            pieces(1).wait_send()
        vector = parts[step, pl.ds(pl.multiple_of(r * PIECE, PIECE), PIECE), :]
        pieces(step).wait_recv()
        for row in range(ROWS):
            vector = vector + jnp.where(r == row, 0.0, sums[step * ROWS + row])
        vector = vector / total
        summed = summed + power_terms[step + 1] * vector
        if step < STEPS - 1:
            iterate[step] = vector
            send_iterate(step + 1, iterate.at[step])
            if step == 0:
                finish()
                sent(0)
            else:
                row_copies.wait_send()
                col_copies.wait_send()
            spread_iterate(step + 1)
            skew(2 * step + 1)
    out_ref[...] = jnp.sqrt(total) * summed

    for copy in stores:
        copy.wait()
    pieces(STEPS - 1).wait_send()


def band_and_sample(members, probes):
    return pl.pallas_call(
        main_kernel,
        name="band_and_sample",
        out_shape=(
            jax.ShapeDtypeStruct((BLOCK, BLOCK), jnp.float32),
            jax.ShapeDtypeStruct((PIECE, PIECE), jnp.float32),
        ),
        in_specs=[pl.BlockSpec(memory_space=pl.ANY), pl.BlockSpec(memory_space=pltpu.VMEM)],
        out_specs=[pl.BlockSpec(memory_space=pl.ANY), pl.BlockSpec(memory_space=pltpu.VMEM)],
        scratch_shapes=[
            pltpu.VMEM((9 * UNITS, QUARTER, BLOCK), jnp.float32),
            pltpu.VMEM((MEMBERS, 3 * BLOCK), jnp.bfloat16),
            pltpu.VMEM((MEMBERS, 3 * BLOCK), jnp.bfloat16),
            pltpu.VMEM((BLOCK // SUB, SUB, SPAN), jnp.float32),
            pltpu.VMEM((BLOCK // SUB, SUB, SPAN), jnp.bfloat16),
            pltpu.VMEM((BLOCK // SUB, SUB, SPAN), jnp.bfloat16),
            pltpu.VMEM((BLOCK, BLOCK), jnp.float32),
            pltpu.VMEM((STEPS - 1, PIECE, PIECE), jnp.float32),
            pltpu.VMEM((STEPS, 5, PIECE, PIECE), jnp.float32),
            pltpu.VMEM((STEPS, 2, ROWS, PIECE, PIECE), jnp.float32),
            pltpu.VMEM((2 * BLOCK, 2 * PIECE), jnp.bfloat16),
            pltpu.VMEM((STEPS, BLOCK, PIECE), jnp.float32),
            pltpu.VMEM((STEPS * ROWS, PIECE, PIECE), jnp.float32),
            pltpu.VMEM((8, 128), jnp.float32),
            pltpu.VMEM((ROWS, 8, 128), jnp.float32),
            pltpu.VMEM((COLS, 8, 128), jnp.float32),
            pltpu.VMEM((8, 128), jnp.float32),
            pltpu.SemaphoreType.DMA,
            pltpu.SemaphoreType.DMA((len(ROUTES), 6)),
            pltpu.SemaphoreType.DMA,
            pltpu.SemaphoreType.DMA,
            pltpu.SemaphoreType.DMA,
            pltpu.SemaphoreType.DMA((BLOCK // SUB,)),
            pltpu.SemaphoreType.DMA((STEPS,)),
            pltpu.SemaphoreType.DMA((STEPS, 5)),
            pltpu.SemaphoreType.DMA((STEPS,)),
            pltpu.SemaphoreType.DMA((STEPS, 2)),
            pltpu.SemaphoreType.DMA((STEPS,)),
            pltpu.SemaphoreType.DMA((STEPS,)),
            pltpu.SemaphoreType.DMA((STEPS,)),
            pltpu.SemaphoreType.DMA((STEPS,)),
            pltpu.SemaphoreType.DMA,
            pltpu.SemaphoreType.DMA,
            pltpu.SemaphoreType.DMA,
            pltpu.SemaphoreType.DMA,
        ],
        compiler_params=pltpu.CompilerParams(
            collective_id=1, has_side_effects=True, vmem_limit_bytes=VMEM_LIMIT
        ),
    )(members, probes)


def on_device(perturbations, probes):
    return band_and_sample(perturbations.reshape(4, QUARTER, BLOCK), probes)


def solution(mesh):
    return jax.shard_map(
        on_device,
        mesh=mesh,
        in_specs=(P("row", "col"), P(("col", "row"), None)),
        out_specs=(P("col", "row"), P(("col", "row"), None)),
        check_vma=False,
    )
```

```python
import functools
import math

import jax
import jax.numpy as jnp
from jax import lax
from jax.experimental import pallas as pl
from jax.experimental.pallas import tpu as pltpu
from jax.sharding import PartitionSpec as P

MEMBERS = 512
STATES = 16384
WINDOW = 4096
ROWS = 8
COLS = 16
BLOCK = 1024
PIECE = 128
SUB = 256
SPAN = SUB + BLOCK
STEPS = 3
MESH = pl.DeviceIdType.MESH
VMEM_LIMIT = 58 * 2**20

epsilon = 1e-06
power_terms = (
    2.0 / math.pi - 4.0 / (3.0 * math.pi) - 4.0 / (15.0 * math.pi) - 4.0 / (35.0 * math.pi),
    8.0 / (3.0 * math.pi) + 32.0 / (15.0 * math.pi) + 72.0 / (35.0 * math.pi),
    -32.0 / (15.0 * math.pi) - 192.0 / (35.0 * math.pi),
    128.0 / (35.0 * math.pi),
)

ROUTES = (
    (0x22f1386c260b0000000000086c260d0100000000086c260b0100000000086c2a0d01, 0x8e4622f130000000008ec6a2b100000001008f4662b1087c2c01038ec6a2d130042e0d01, 0x8fc622b1386c220b018ec6e2f1086c260d008fc66291386c2e0f018ec622b1186c2a0903, 0x8ec6e2f1386c2209008ec622d11864260b038fc662f1387c260b038ec6a2f118742a0d00, 0x8ec6629100000001038fc6e2b118742e0d010046a2c008742a0b01004622f1086c2e0b01, 0x8e4622f1286c2a0f038f46a2b12004220b018e4622d1386c24010000468000087c220f03),
    (0x8642e0d0200000000087c2e09000000000008642a0f0300000000087c220b02, 0x8fc662d120000000008f46e2f120000000008ec6229110000000008e46e29120042a0b00, 0x8e46e2912864260d028f4622d1287c220b018f46a2f108742a09028f46e2f128742e0d01, 0x8fc622d1087c2e0d028fc6a2f1387c220f018e46e2b1286c2a0f028e4622b1387c260f03, 0x8f46a2b110000000008e46401138642609020046c000087c220d02000000113864260f02, 0x8fc6a2d11874220b01004622d100042800000046e2b128642c0103000000000864260800),
    (0x87c2a0901000000000874220f03000000000874220d00000000000864260903, 0x8ec6e29100000000008e4622d110000000008fc6a2d130000000008fc662f10000000102, 0x8f4662f1187c2a0f038e4662b118742a09028e46e2b1187c260b008e46a2d1087c220b02, 0x8e4662b128642a0b018e4662b1086c2a0d028f4622d108642e0d008fc6e2d10864220901, 0x46e2d120000000008e800011287c220b03000000000004260800000000112874220d00, 0x8e8022913004260c000046e29130042c00000046a2f10004200101000000000000000000),
    (0x4260b1f844360f0300476311d84caa4f0200452320087ca21305005e6e9708543a0f63, 0x89eea27f1006a34fe18ffebed16f77a8000089fe227f0f680203108f4e2231796c10010d, 0x86c6a2d1f8e416030086c6a2132f742fcb038ecea6b1285c662b0d8fde66d1d8646a2d13, 0x8f4260b17807afcde19e426290187433cb2389c6a6b1181c2209e19e4660d128ec2e1502, 0xffc77eb00007af2f938d802218084c6a2b0dc7c7c0117004660f0dbec770d118543a1503, 0x89c563717d7c174fa39e45e0d1d9680000009f47e0b1f8f43c0105004570d818eca62d20),
    (0x47e271684c3e04000047e21328443e0121004e80130854aa4b0e89deaeb7181cae0720, 0xffc5225f3d66a7490489fee291e00000000089472331ff600215e188c6235159646a0312, 0x86452251cf642e2e008c0026f1e86417cd2386ce2211e8f41fcb0e8dcee231e85c6e2900, 0x8846a0d11877a7c9e29fc2e0900f743e13e18e80229158f43fcbe287dea6b158e43e0a00, 0x8842e0d1cf6000000088c5a25160046e030f0000237830046229e2bf62e25700046e2c00, 0x864762700816a2110489c26091797002110f0045e0f0381caa2902004e30b808e46e290d),
    (0x45e250280432020000000000086436152300000013384cae1521bf5eeed72844160307, 0x89456371e0000207a38846633150000204008862e37f3f7000011189e2e2b1d004662f0e, 0x8c002271e8ffa206009f8026d138541bc912864626d1ff6c13cf038d5ee6b33844662f10, 0x42a0915814362fe38f46e69128ec3611009f0026932877ae2de0885ee6f168fc321200, 0x87c6209f1f780000008cc20011c004622f050000223f384c1e1313005ee21168fc66050f, 0x452090280ea615069fc720f03004a4010e87426311e8ec34010f0062c018285c320706),
    (0x4360f0d8741a000000442133785ca2199d0044c0135a6c161707af5f40160874be1500, 0x8f6d7e1f2007276dc088c5623f7e7fe401c388c4e211c8cfba270b8c4f231119f4762310, 0x8445a4d1084c62091c9e4aa091cf7febec008cca2691d854220de08c4daab13004e22200, 0x4364d218ffebd7e680c2277158f7a3cfe5ae0024d01f0fe3d5f0af5f6290186c3be800, 0xfdc523f61f4e270bed86c40011d004360107b6802131d89c562bf0bce10011f8d46a27f3, 0x47a131edec070bc099caa350d91e7730009d4660d1d816521106d6cfc018d96c5a1517),
    (0x4720501f740211960043e1763854a605240044249378140e092fafdaef57ca652a050b, 0x887623f11006ef68008dffe3d180079401168e7f7ef15007961a009dcde371c91c62130f, 0x848024b0c85c5febf18d4de4f20e7f9a0e00ae4aa4b32f646bcc0086c664b2000427ea00, 0x24b038e7efd3e49647e4f1789fe3e8009980231168ec3233018f5ae0b1780473ee00, 0x8944a390cf0e7f27ef8047ff600f0c2a07eeb65ae3d90f143e331fb844401608dc522915, 0x43e230dde6ef6996964de23029149721099c4a6250e896eb3304d64eb039288c3e0515),
    (0x43223f68541e17e5004d400009741a0b2600000012385c3a0502b7de2f751a7c321f2f, 0x8dc5be5fc006b346008900231170079c00008ac6e2f12fff9c0000886123b1f9ee2e211d, 0x8e8024f20f441fc3f39ecda49228e4122c00aecd62523864162ded854a60d23ff45e2a00, 0x4ae4901f77a3ebf188c3e371681fbbec00af8020d14807e7cdf3975e64b0689c7fea00, 0xfcfa21506f165f259fb75abe334f4c7629f3b756ecd6183c32011eb7df401638f4322b1d, 0x8043631188443801ad00436151e90e7c010899c7a150d8840e3716006132f359647e3525),
    (0x45a1b0882c0607e7004a2193b82c864a00000000126845261f2ead5d2ff63a4c36514d, 0x8b77e3115006db55b78a80221d3eefd401f7000023bf6fd787711c9b002331e9c6d22b11, 0x8749a232d8c41bee00844d6673feefd62e008d4de4f1cfd463e60087de24f1cef41bca00, 0xa68026d4089c3ff503a680253438e46bd200a6802750588feff00000002090281c37ca00, 0xf8c1b0760f1e370febb7c07d3fdf9c7a1b0accdbb2791f847a210abde7401718c43607f4, 0x90c1a1b10d5ed801b795412011c0064313b7944e2170c88c4c01b5df62b238e004363111),
    (0x402010981420010b004bc01278343a1a00000000134a143e5129ac002d76ca0cb6174f, 0x88f6a3c00e0f6344008b803fd1ae17d801ff8b7c62518fdfd36000890023d1b914023713, 0x87cee6932e6c13c000964a6633cfd41e22008dcda2d2dfdc1bc400865d2292e8cc53e600, 0xa60026932894261400a78021314f9feff3f4a98026d0380c7beff5a600271148f7a7f400, 0xf77c23118f367305ec885e70596f2c4e0f1800597158b824720715b95c8016c8442a091c, 0x4421908d8ee8018d9bcda05180063f4bb6954de09198564f491cd1e631337994721f04),
    (0x42a3d9683c380000000000138824325400a7800015ca1c361d28ad802d400a148e1800, 0x8ac6a21d5e4ebf74008b002371bee79800008a00231f1ff62c00008b00225c19844e391c, 0x854966f1de4c53e1fc8fc9e8d01ee46be800acc96472184c6fec0094dae4d2df7c17e400, 0xa700256008efe3ee00898026d3180fbff000a60025517f87f7f200a78026d0580803f600, 0xf07dba31df26332382004180170f3c5a15febfc4b1bfff540e0512005e401668cc5e03ff, 0x42e1715006d40181904063311946d7170c994b63d0185c3001b7dee77219d9dcae3b08),
    (0x6d6210e85c161e0000486e7298142a0600a5000015d824320600a4002f94d84c0e1b4b, 0x8d446231de9eb77000000022713e8790000000003e514f9fcf53fa8a803c71698cce191f, 0x8dc9e630ee6467c60087c9a653de5c622800854d20f3e84003ea00845ea652ced4100000, 0xaf0025536ffc33f600a18020f77817b3a9d7a80024b07897a7e800a88024f0781003ce00, 0xfe78793e50065b1b8dbcdd40171fac7233e7bd5f63f9c8e42e2ff6bc5e0000084c0e231e, 0x934aa210e006b001a69b4fa2f00006a319b29ac2a05148479f53b0dc6672b919b6d23336),
    (0x47a03fd83408000000002d54183c0e4600000000122a0c121800a5002fb4f85ca2114c, 0x22bdde96f35e008a00239fde8f6c000000002231dfc6bc01f80000001c0956ce3f07, 0x9dcd2472ef7003ca0087492411d85c67c00087cae632fff80228008c802493dec003c400, 0xa180253e7f8fbbe800a143a1503807ebcc00a100217068ffebd600a98025504c9803d600, 0x82fefb7fc00603019600594017ff34123df9bdd8703f2fac3617fbba60000000043e1ffe, 0x994e22b0f006fc01b194c9e371b006bc01ad80c961f1a8fe4001b3d166b3790954a22723),
    (0x44211608240c000000002db2400416500000000014ca4516112ca7002cd7da1c060000, 0x23b14e2f2f7ba8007ca3f14e57ec00008b803e11af46c3560000000011a95f6b731e, 0x8cc92420087003cc0085802013ee5003e00084802410df4003c800870020f1fed803e200, 0xa78027400f7ff60e00ae0020a008843bc800a00020900887b38a00a00025700f7fb3d400, 0xf6f9801f20062b3d88005d8019df24321ff8bf5d00126f04763be5b5dd000000047239e2, 0x92cde330a0040c01b593c3a2704004b801bb9bc8e291c8d6f401a3d864f398f95c7a692f),
    (0x41e1d76004d4000000000016b0041e4c00000000140a74020000ac802f378a340a1c00, 0x2331beaeff720000003ffdffe7580000000023ff2fcf235800000000114946123c00, 0x8d0026400ff803e80086002452100003c400840020d3ce5003e5fe9d802413fe441fc600, 0xae8026a008f43a1000a80024a008942fd000a18027200f07a3ce00ae0024c00880039200, 0xf87e401e7000032189bbd9c0127fa40a2d1eb9dcc017af740625ecbd5ac00000047e3ff5, 0x9b4c6340000000018e98cc63f070068401a99b47635110000001a6d8ecf1993944f27726),
    (0x406c55f00550000000002c37000408000000000014300406020000002c945a24b21200, 0x235d7eb7236600000023bd2ebf68000000002351b0073c00000000001189fe4e1000, 0x960024400e5003e4008c802292f8c803ee00958024d3de78022e00848022521e50000000, 0xa90027000887fff2009700256008fff2080088800000081473c800a90024800890038800, 0xf3ffc01840067b0376005980000004661910bc59c0178f4c46230cb2d9800000047a1deb, 0x9a4161c000000001a49ac321d1f0000001b892cd221020000001b4d56033f9c004dc0124),
    (0x420015000410000000000017c0048c000000000015000538000000002f15c0052c0000, 0x119e3ef8000000000011fe5f5400000000001170075400000000000009d6c00000, 0x26000e5803ce00000022400000000000000026400f70000000000026200e7003cc00, 0xa0000000000003a800af0000000000038e0081000000000003d200a70025000007bfcc00, 0xfe80000000064311810059000000000001f2b459000000000001fe005e800000000001e8, 0x93ce401190000001a89349000000000001a79a49238000000001a2d5800019f00000013c),
    (0x438015100000000000000015a000000000000000151000000000000000152004000000, 0x11ae377c0000000000000eaf300000000000000007040000000000000007740000, 0xe40000000000000000e70000000000024400000000000000024400ec8000000, 0xa8002720000003b60000000000000003f60000000000000000000090800000000003f200, 0x61f1d7dbe53800000000001fabcd8000000000001e00000000000000001fa, 0x924c8011a0000000009246400000000001a195c9c0000000000000d40033d87000000121),
    (0x17d00000000000000015800000000000000014600000000000000014b000000000, 0xe27680000000000000e077c0000000000000006f400000000001e4000000000, 0xe48000000000000000000000000000000000ef803c800, 0xa08000000000000000000000000000000000000000000000000000a10000000000000000, 0x604018e005ec00000000000000056400000000001f9000000000000000000, 0x1a4000000000000000000df803119e000000122),
    (0x17100000000000000015900000000000000014c000000000, 0xea7700000000000000e4f200000000000000006fc0000000000000000000000, 0x0, 0xa88000000000000000000000000000000000000000000000000000000000000000000000, 0x6200000000000000000000000000000000000000000000000000000000000, 0x1ae000000000000000000dd0000000000000000),
    (0x19d000000000000000000000000000000000147000000000, 0xedf5c0000000000000007240000000000000000000000000000000000000000, 0x0, 0xa10000000000000000000000000000000000000000000000000000000000000000000000, 0x6380000000000000000000000000000000000000000000000000000000000, 0x0),
)


def here():
    return lax.axis_index("row"), lax.axis_index("col")


def at(row, col):
    return {"row": row, "col": col}


def unless(own, step):
    if own is None:
        step()
    else:
        pl.when(jnp.logical_not(own))(step)


def copied(src, dst, send, recv, row, col):
    return pltpu.make_async_remote_copy(
        src_ref=src, dst_ref=dst, send_sem=send, recv_sem=recv,
        device_id=at(row, col), device_id_type=MESH,
    )


DIRECTIONS = ((1, 0, 0), (-1, 0, 0), (0, 1, 0), (0, -1, 0), (0, 0, 1), (0, 0, -1))
QUARTER = MEMBERS // ROWS // 4
LAG = 3
UNITS = 4 * ROWS


def place_of(i):
    return (i % 8) // 4, i % 4, i // 8


def arrivals():
    table = []
    for sends in ROUTES:
        by_direction = []
        for (dx, dy, dz), packed in zip(DIRECTIONS, sends):
            entries = []
            for i in range(32):
                x, y, z = place_of(i)
                fx, fy, fz = (x - dx) % 4, (y - dy) % 4, (z - dz) % 4
                entry = packed >> (9 * (fz * 8 + (fx % 2) * 4 + fy)) & 511
                if entry:
                    pair = (fx // 2) * 4 + fz + (entry >> 5 & 7)
                    entry = 256 | (pair - z) % 8 << 5 | entry & 31
                entries.append(entry)
            by_direction.append(entries)
        table.append(by_direction)
    return table


def departures():
    return [[[packed >> (9 * i) & 511 for i in range(32)] for packed in sends] for sends in ROUTES]


def words(table):
    return [
        [[d[i] | e[i] << 9 | f[i] << 18 for i in range(32)] for d, e, f in (sends[:3], sends[3:])]
        for sends in table
    ]


def looked_up(values, bits):
    if len(set(values)) == 1:
        return jnp.int32(values[0])
    low = looked_up(values[: len(values) // 2], bits[:-1])
    high = looked_up(values[len(values) // 2 :], bits[:-1])
    return jnp.where(bits[-1], high, low)


def gather_members(x_ref, held, send, recv, across_send, across_recv, own_sem, greet_all):
    r, c = here()
    core = lax.rem(c, 2)
    pair = lax.div(c, 2)
    z = lax.rem(pair, 4)
    x = lax.div(pair, 4) * 2 + lax.div(r, 4)
    y = lax.rem(r, 4)
    first = core == 0
    sign = 1 - 2 * core
    index = jnp.where(first, z * 8 + r, (3 - z) * 8 + 7 - r)
    bits = [lax.rem(lax.div(index, 2**b), 2) == 1 for b in range(5)]

    def neighbour(direction):
        dx, dy, dz = DIRECTIONS[direction]
        nx, ny, nz = (lax.rem(v + sign * d + 4, 4) for v, d in ((x, dx), (y, dy), (z, dz)))
        return lax.rem(nx, 2) * 4 + ny, lax.div(nx, 2) * 8 + nz * 2 + core

    sides = [neighbour(d) for d in range(6)]
    other = (r, c + sign)

    own_units = pl.ds(pl.multiple_of((pair * ROWS + r) * 4, 4), 4)
    across = lax.div(lax.rem(2 * pair - 4 + r + 2 - core - lax.rem(r, 2) + COLS, COLS), 2)

    own = pltpu.make_async_copy(x_ref, held.at[own_units], own_sem)
    own.start()
    greet_all(sides)
    own.wait()

    def unit(entry):
        relative = lax.rem(lax.div(entry, 32), 8)
        row = lax.rem(lax.div(entry, 4), 8)
        block = lax.rem(pair + sign * relative + 8, 8)
        row = jnp.where(first, row, 7 - row)
        return block, row * 4 + lax.rem(entry, 4)

    def entries(table):
        found = []
        for word in table:
            word = looked_up(word, bits)
            found += [lax.rem(word, 512), lax.rem(lax.div(word, 512), 512), lax.div(word, 512 * 512)]
        return found

    def across_copy(mine, there):
        return copied(held.at[mine], held.at[there], across_send, across_recv, *other)

    def take(step):
        for d, entry in enumerate(entries(incoming[step])):
            @pl.when(entry >= 256)
            def _(d=d, entry=entry):
                block, number = unit(entry)
                ref = held.at[block * UNITS + number]
                pltpu.make_async_copy(ref, ref, recv.at[step, d]).wait()

                @pl.when(block == across)
                def _():
                    across_copy(block * UNITS + number, 8 * UNITS + number).start()

    incoming, outgoing = words(arrivals()), words(departures())

    @pl.when(pair == across)
    def _():
        across_copy(own_units, pl.ds(8 * UNITS + r * 4, 4)).start()

    rounds = len(ROUTES)
    for step in range(rounds + LAG):
        if step >= LAG:
            take(step - LAG)
        if step < rounds:
            for d, entry in enumerate(entries(outgoing[step])):
                @pl.when(entry >= 256)
                def _(d=d, entry=entry):
                    block, number = unit(entry)
                    ref = held.at[block * UNITS + number]
                    copied(ref, ref, send, recv.at[step, d], *sides[d]).start()

    whole = across_copy(pl.ds(0, UNITS), pl.ds(8 * UNITS, UNITS))
    counts = [sum((packed >> (9 * i) & 256) // 256 for sends in ROUTES for packed in sends) for i in range(32)]
    count = looked_up(counts, bits)

    def finish():
        for total in sorted(set(counts)):
            @pl.when(count == total)
            def _(total=total):
                units = held.at[pl.ds(0, total)]
                copied(units, units, send, recv.at[0, 0], *sides[0]).wait_send()
        whole.wait_send()

    whole.wait_recv()
    return finish


def parted(values):
    high = values.astype(jnp.bfloat16)
    low = (values - high.astype(jnp.float32)).astype(jnp.bfloat16)
    return high, low


def dotted(a, b, dims):
    return lax.dot_general(a, b, (dims, ((), ())), preferred_element_type=jnp.float32)


def skewed(rows, shift):
    sub = lax.broadcasted_iota(jnp.int32, rows.shape, 0)
    if shift:
        rows = pltpu.roll(rows, SPAN - shift, 1)
    for bit in (1, 2, 4):
        rows = jnp.where((sub & bit) != 0, pltpu.roll(rows, SPAN - bit, 1), rows)
    return rows[:, :BLOCK]


def main_kernel(
    members_ref, w_ref, local_out, out_ref,
    held, xh, xl, band_ref, high_ref, low_ref, local_ref,
    iterate, near, window, wide, parts, sums, square_ref, row_squares, col_squares, row_total,
    member_send, member_recv, across_send, across_recv, own_sem, store_sem, send_z, recv_z, send_w, recv_w, send_x, recv_x, send_y, recv_y, send_r, recv_r, send_c, recv_c,
):
    r, c = here()
    core = lax.rem(c, 2)
    pair = lax.div(c, 2)
    other = (r, c + 1 - 2 * core)
    shared = 1 - core
    passes = core == lax.rem(r + 1, 2)

    def greet_all(sides):
        barrier = pltpu.get_barrier_semaphore()
        partners = list(sides)
        for shift in range(1, ROWS):
            row = lax.rem(r + shift, ROWS)
            partners += [(row, 2 * pair), (row, 2 * pair + 1)]
        for shift in range(1, COLS):
            partners.append((r, lax.rem(c + shift, COLS)))
        for row, col in partners:
            pl.semaphore_signal(barrier, inc=1, device_id=at(row, col), device_id_type=MESH)
        pl.semaphore_wait(barrier, len(partners))

    def to_pairs(step, source, away):
        col = lax.rem(c - 2 * away + COLS, COLS)
        return copied(source, near.at[step, away + 2], send_z.at[step], recv_z.at[step, away + 2], r, col)

    def targets(away):
        found = []
        for e in range(3):
            row = 2 * away + core + 2 + e
            valid = None
            if away == -2:
                if e == 0:
                    continue
                valid = core == 1 if e == 1 else None
            if away == 2:
                if e == 2:
                    continue
                valid = core == 0 if e == 1 else None
            there = (1, core, 0)[e]
            panel = (1, shared, 0)[e]
            found.append((row, there, panel, valid))
        return found

    def share(step, source, away, act):
        for row, there, panel, valid in targets(away):
            own = (row == r) & (there == core)
            go = jnp.logical_not(own)
            if valid is not None:
                own, go = own & valid, go & valid

            @pl.when(go)
            def _(row=row, there=there, panel=panel):
                act(copied(
                    source, window.at[step, panel, r], send_w.at[step], recv_w.at[step, panel], row, 2 * pair + there
                ))

            @pl.when(own)
            def _(panel=panel):
                act(pltpu.make_async_copy(source, window.at[step, panel, r], recv_w.at[step, panel]))

    def begin(copy):
        copy.start()

    def send_iterate(step, source):
        for away in (-2, 2, -1, 1):
            to_pairs(step, source, away).start()
        share(step, source, 0, begin)

    def spread_iterate(step):
        for away in (-1, 1, -2, 2):
            block = near.at[step, away + 2]
            pltpu.make_async_copy(block, block, recv_z.at[step, away + 2]).wait()
            share(step, block, away, begin)

    def across_copy(step):
        return copied(
            window.at[step, shared], window.at[step, 1 - shared], send_x.at[step], recv_x.at[step], *other
        )

    def split(step, panel):
        high, low = parted(window[step, panel].reshape(BLOCK, PIECE))
        first = pl.multiple_of(panel * BLOCK, BLOCK)
        wide[pl.ds(first, BLOCK), :PIECE] = high
        wide[pl.ds(first, BLOCK), PIECE:] = low

    def landed(step, panel):
        block = window.at[step, panel]
        pltpu.make_async_copy(block, block, recv_w.at[step, panel]).wait()

    def take_iterate(step):
        @pl.when(passes)
        def _():
            landed(step, shared)
            across_copy(step).start()
            split(step, shared)

        landed(step, core)
        split(step, core)

        @pl.when(jnp.logical_not(passes))
        def _():
            across_copy(step).wait_recv()
            split(step, shared)

    finish = gather_members(
        members_ref, held, member_send, member_recv, across_send, across_recv, own_sem, greet_all
    )
    send_iterate(0, w_ref)
    spread_iterate(0)

    near_block = lax.div(lax.rem(c + r - 4 + COLS, COLS), 2)
    far_block = lax.div(lax.rem(c + r - 3 + COLS, COLS), 2)
    odd = lax.rem(r, 2) == 1
    for panel, block in enumerate((pair, jnp.where(odd, 8, near_block), jnp.where(odd, far_block, 8))):
        for first in range(0, BLOCK, SUB):
            values = held[pl.ds(block * UNITS, UNITS), :, first : first + SUB].reshape(MEMBERS, SUB)
            centered = values - jnp.sum(values, 0, keepdims=True) / MEMBERS
            spread = jnp.sqrt(jnp.sum(centered * centered, 0, keepdims=True) + epsilon)
            high, low = parted(centered / spread)
            lo_at = (panel - 1) * BLOCK + first if panel else 2 * BLOCK + first
            xh[:, lo_at : lo_at + SUB] = high
            xl[:, lo_at : lo_at + SUB] = low
    squares = jnp.zeros((8, 128), jnp.float32)
    gap = lax.broadcasted_iota(jnp.int32, (SUB, SPAN), 1) - lax.broadcasted_iota(jnp.int32, (SUB, SPAN), 0)
    taper = jnp.maximum(0.0, 1.0 - jnp.abs(gap + (r * BLOCK - WINDOW)).astype(jnp.float32) / WINDOW)
    taper = jnp.where((gap >= 0) & (gap < BLOCK), taper, 0.0)
    for tile in range(BLOCK // SUB):
        first = tile * SUB
        rows_h = xh[:, 2 * BLOCK + first : 2 * BLOCK + first + SUB]
        rows_l = xl[:, 2 * BLOCK + first : 2 * BLOCK + first + SUB]
        cols_h = xh[:, first : first + SPAN]
        cols_l = xl[:, first : first + SPAN]
        over = ((0,), (0,))
        gram = dotted(rows_h, cols_h, over) + (dotted(rows_h, cols_l, over) + dotted(rows_l, cols_h, over))
        band = gram * taper
        band_ref[tile] = band
        high, low = parted(band)
        high_ref[tile] = high
        low_ref[tile] = low
        squares = squares + jnp.sum((band * band).reshape(SUB // 8, 8, SPAN // 128, 128), (0, 2))
    square_ref[...] = squares

    for shift in range(1, ROWS):
        copied(square_ref, row_squares.at[r], send_r, recv_r, lax.rem(r + shift, ROWS), c).start()

    stores = []

    def skew(tile):
        first = tile * SUB
        for group in range(0, SUB, 8):
            local_ref[first + group : first + group + 8, :] = skewed(band_ref[tile, group : group + 8, :], group)
        stores.append(pltpu.make_async_copy(local_ref.at[first : first + SUB], local_out.at[first : first + SUB], store_sem.at[tile]))
        stores[-1].start()

    def several(ref, send, recv):
        return copied(ref, ref, send, recv, *other)

    def piece_out(step, row):
        return copied(
            parts.at[step, row * PIECE : (row + 1) * PIECE], sums.at[step * ROWS + r],
            send_y.at[step], recv_y.at[step], row, c,
        )

    def sent(step):
        several(near.at[step, pl.ds(0, 4)], send_z.at[step], recv_z.at[step, 0]).wait_send()
        several(sums.at[pl.ds(0, 11)], send_w.at[step], recv_w.at[step, 0]).wait_send()
        pl.when(passes)(lambda: across_copy(step).wait_send())

    def pieces(step):
        return several(sums.at[pl.ds(step * ROWS, ROWS - 1)], send_y.at[step], recv_y.at[step])

    row_copies = several(row_squares.at[pl.ds(0, ROWS - 1)], send_r, recv_r)
    col_copies = several(col_squares.at[pl.ds(0, COLS - 1)], send_c, recv_c)
    total = None
    summed = power_terms[0] * w_ref[...]
    for step in range(STEPS):
        take_iterate(step)
        for tile in range(BLOCK // SUB):
            first = tile * SUB
            over = ((1,), (0,))
            both = dotted(high_ref[tile], wide[first : first + SPAN, :], over)
            rest = dotted(low_ref[tile], wide[first : first + SPAN, :PIECE], over)
            parts[step, first : first + SUB, :] = both[:, :PIECE] + (both[:, PIECE:] + rest)
            for row in range(first // PIECE, (first + SUB) // PIECE):
                unless(r == row, lambda row=row: piece_out(step, row).start())
        if step == 0:
            row_copies.wait_recv()
            squares = jnp.zeros((8, 128), jnp.float32)
            for row in range(ROWS):
                squares = squares + jnp.where(r == row, square_ref[...], row_squares[row])
            row_total[...] = squares
            for shift in range(1, COLS):
                copied(row_total, col_squares.at[c], send_c, recv_c, r, lax.rem(c + shift, COLS)).start()
            skew(0)
            col_copies.wait_recv()
            squares = jnp.zeros((8, 128), jnp.float32)
            for col in range(COLS):
                squares = squares + jnp.where(c == col, row_total[...], col_squares[col])
            total = jnp.sum(squares, keepdims=True) / STATES
        elif step == 1:
            skew(2)
        else:
            sent(1)
            sent(2)
            pieces(0).wait_send()
            pieces(1).wait_send()
        vector = parts[step, pl.ds(pl.multiple_of(r * PIECE, PIECE), PIECE), :]
        pieces(step).wait_recv()
        for row in range(ROWS):
            vector = vector + jnp.where(r == row, 0.0, sums[step * ROWS + row])
        vector = vector / total
        summed = summed + power_terms[step + 1] * vector
        if step < STEPS - 1:
            iterate[step] = vector
            send_iterate(step + 1, iterate.at[step])
            if step == 0:
                finish()
                sent(0)
            else:
                row_copies.wait_send()
                col_copies.wait_send()
            spread_iterate(step + 1)
            skew(2 * step + 1)
    out_ref[...] = jnp.sqrt(total) * summed

    for copy in stores:
        copy.wait()
    pieces(STEPS - 1).wait_send()


def band_and_sample(members, probes):
    return pl.pallas_call(
        main_kernel,
        name="band_and_sample",
        out_shape=(
            jax.ShapeDtypeStruct((BLOCK, BLOCK), jnp.float32),
            jax.ShapeDtypeStruct((PIECE, PIECE), jnp.float32),
        ),
        in_specs=[pl.BlockSpec(memory_space=pl.ANY), pl.BlockSpec(memory_space=pltpu.VMEM)],
        out_specs=[pl.BlockSpec(memory_space=pl.ANY), pl.BlockSpec(memory_space=pltpu.VMEM)],
        scratch_shapes=[
            pltpu.VMEM((9 * UNITS, QUARTER, BLOCK), jnp.float32),
            pltpu.VMEM((MEMBERS, 3 * BLOCK), jnp.bfloat16),
            pltpu.VMEM((MEMBERS, 3 * BLOCK), jnp.bfloat16),
            pltpu.VMEM((BLOCK // SUB, SUB, SPAN), jnp.float32),
            pltpu.VMEM((BLOCK // SUB, SUB, SPAN), jnp.bfloat16),
            pltpu.VMEM((BLOCK // SUB, SUB, SPAN), jnp.bfloat16),
            pltpu.VMEM((BLOCK, BLOCK), jnp.float32),
            pltpu.VMEM((STEPS - 1, PIECE, PIECE), jnp.float32),
            pltpu.VMEM((STEPS, 5, PIECE, PIECE), jnp.float32),
            pltpu.VMEM((STEPS, 2, ROWS, PIECE, PIECE), jnp.float32),
            pltpu.VMEM((2 * BLOCK, 2 * PIECE), jnp.bfloat16),
            pltpu.VMEM((STEPS, BLOCK, PIECE), jnp.float32),
            pltpu.VMEM((STEPS * ROWS, PIECE, PIECE), jnp.float32),
            pltpu.VMEM((8, 128), jnp.float32),
            pltpu.VMEM((ROWS, 8, 128), jnp.float32),
            pltpu.VMEM((COLS, 8, 128), jnp.float32),
            pltpu.VMEM((8, 128), jnp.float32),
            pltpu.SemaphoreType.DMA,
            pltpu.SemaphoreType.DMA((len(ROUTES), 6)),
            pltpu.SemaphoreType.DMA,
            pltpu.SemaphoreType.DMA,
            pltpu.SemaphoreType.DMA,
            pltpu.SemaphoreType.DMA((BLOCK // SUB,)),
            pltpu.SemaphoreType.DMA((STEPS,)),
            pltpu.SemaphoreType.DMA((STEPS, 5)),
            pltpu.SemaphoreType.DMA((STEPS,)),
            pltpu.SemaphoreType.DMA((STEPS, 2)),
            pltpu.SemaphoreType.DMA((STEPS,)),
            pltpu.SemaphoreType.DMA((STEPS,)),
            pltpu.SemaphoreType.DMA((STEPS,)),
            pltpu.SemaphoreType.DMA((STEPS,)),
            pltpu.SemaphoreType.DMA,
            pltpu.SemaphoreType.DMA,
            pltpu.SemaphoreType.DMA,
            pltpu.SemaphoreType.DMA,
        ],
        compiler_params=pltpu.CompilerParams(
            collective_id=1, has_side_effects=True, vmem_limit_bytes=VMEM_LIMIT
        ),
    )(members, probes)


def hand_over_kernel(local_ref, sampled_ref, local_out, sampled_out, held, held_sampled, load_sem, store_sem):
    parts = BLOCK // SUB
    moves = []
    for source, middle, target, n in [(sampled_ref, held_sampled, sampled_out, parts)] + [
        (*(ref.at[n * SUB : (n + 1) * SUB] for ref in (local_ref, held, local_out)), n) for n in range(parts)
    ]:
        load = pltpu.make_async_copy(source, middle, load_sem.at[n])
        load.start()
        moves.append((load, pltpu.make_async_copy(middle, target, store_sem.at[n])))
    for load, store in moves:
        load.wait()
        store.start()
    for _, store in moves:
        store.wait()


def handed_over(localized, sampled):
    parts = BLOCK // SUB + 1
    return pl.pallas_call(
        hand_over_kernel,
        name="hand_over",
        out_shape=(
            jax.ShapeDtypeStruct((BLOCK, BLOCK), jnp.float32),
            jax.ShapeDtypeStruct((PIECE, PIECE), jnp.float32),
        ),
        in_specs=[pl.BlockSpec(memory_space=pl.ANY)] * 2,
        out_specs=[pl.BlockSpec(memory_space=pl.ANY)] * 2,
        scratch_shapes=[
            pltpu.VMEM((BLOCK, BLOCK), jnp.float32),
            pltpu.VMEM((PIECE, PIECE), jnp.float32),
            pltpu.SemaphoreType.DMA((parts,)),
            pltpu.SemaphoreType.DMA((parts,)),
        ],
        compiler_params=pltpu.CompilerParams(vmem_limit_bytes=16 * 2**20),
    )(localized, sampled)


def on_device(perturbations, probes):
    return handed_over(*band_and_sample(perturbations.reshape(4, QUARTER, BLOCK), probes))


def solution(mesh):
    return jax.shard_map(
        on_device,
        mesh=mesh,
        in_specs=(P("row", "col"), P(("col", "row"), None)),
        out_specs=(P("col", "row"), P(("col", "row"), None)),
        check_vma=False,
    )
```

```python
import functools
import math

import jax
import jax.numpy as jnp
from jax import lax
from jax.experimental import pallas as pl
from jax.experimental.pallas import tpu as pltpu
from jax.sharding import PartitionSpec as P

MEMBERS = 512
STATES = 16384
WINDOW = 4096
ROWS = 8
COLS = 16
BLOCK = 1024
PIECE = 128
SUB = 256
SPAN = SUB + BLOCK
STEPS = 3
MESH = pl.DeviceIdType.MESH
VMEM_LIMIT = 58 * 2**20

epsilon = 1e-06
power_terms = (
    2.0 / math.pi - 4.0 / (3.0 * math.pi) - 4.0 / (15.0 * math.pi) - 4.0 / (35.0 * math.pi),
    8.0 / (3.0 * math.pi) + 32.0 / (15.0 * math.pi) + 72.0 / (35.0 * math.pi),
    -32.0 / (15.0 * math.pi) - 192.0 / (35.0 * math.pi),
    128.0 / (35.0 * math.pi),
)

ROUTES = (
    (0x22f1386c260b0000000000086c260d0100000000086c260b0100000000086c2a0d01, 0x8e4622f130000000008ec6a2b100000001008f4662b1087c2c01038ec6a2d130042e0d01, 0x8fc622b1386c220b018ec6e2f1086c260d008fc66291386c2e0f018ec622b1186c2a0903, 0x8ec6e2f1386c2209008ec622d11864260b038fc662f1387c260b038ec6a2f118742a0d00, 0x8ec6629100000001038fc6e2b118742e0d010046a2c008742a0b01004622f1086c2e0b01, 0x8e4622f1286c2a0f038f46a2b12004220b018e4622d1386c24010000468000087c220f03),
    (0x8642e0d0200000000087c2e09000000000008642a0f0300000000087c220b02, 0x8fc662d120000000008f46e2f120000000008ec6229110000000008e46e29120042a0b00, 0x8e46e2912864260d028f4622d1287c220b018f46a2f108742a09028f46e2f128742e0d01, 0x8fc622d1087c2e0d028fc6a2f1387c220f018e46e2b1286c2a0f028e4622b1387c260f03, 0x8f46a2b110000000008e46401138642609020046c000087c220d02000000113864260f02, 0x8fc6a2d11874220b01004622d100042800000046e2b128642c0103000000000864260800),
    (0x87c2a0901000000000874220f03000000000874220d00000000000864260903, 0x8ec6e29100000000008e4622d110000000008fc6a2d130000000008fc662f10000000102, 0x8f4662f1187c2a0f038e4662b118742a09028e46e2b1187c260b008e46a2d1087c220b02, 0x8e4662b128642a0b018e4662b1086c2a0d028f4622d108642e0d008fc6e2d10864220901, 0x46e2d120000000008e800011287c220b03000000000004260800000000112874220d00, 0x8e8022913004260c000046e29130042c00000046a2f10004200101000000000000000000),
    (0x4260b1f844360f0300476311d84caa4f0200452320087ca21305005e6e9708543a0f63, 0x89eea27f1006a34fe18ffebed16f77a8000089fe227f0f680203108f4e2231796c10010d, 0x86c6a2d1f8e416030086c6a2132f742fcb038ecea6b1285c662b0d8fde66d1d8646a2d13, 0x8f4260b17807afcde19e426290187433cb2389c6a6b1181c2209e19e4660d128ec2e1502, 0xffc77eb00007af2f938d802218084c6a2b0dc7c7c0117004660f0dbec770d118543a1503, 0x89c563717d7c174fa39e45e0d1d9680000009f47e0b1f8f43c0105004570d818eca62d20),
    (0x47e271684c3e04000047e21328443e0121004e80130854aa4b0e89deaeb7181cae0720, 0xffc5225f3d66a7490489fee291e00000000089472331ff600215e188c6235159646a0312, 0x86452251cf642e2e008c0026f1e86417cd2386ce2211e8f41fcb0e8dcee231e85c6e2900, 0x8846a0d11877a7c9e29fc2e0900f743e13e18e80229158f43fcbe287dea6b158e43e0a00, 0x8842e0d1cf6000000088c5a25160046e030f0000237830046229e2bf62e25700046e2c00, 0x864762700816a2110489c26091797002110f0045e0f0381caa2902004e30b808e46e290d),
    (0x45e250280432020000000000086436152300000013384cae1521bf5eeed72844160307, 0x89456371e0000207a38846633150000204008862e37f3f7000011189e2e2b1d004662f0e, 0x8c002271e8ffa206009f8026d138541bc912864626d1ff6c13cf038d5ee6b33844662f10, 0x42a0915814362fe38f46e69128ec3611009f0026932877ae2de0885ee6f168fc321200, 0x87c6209f1f780000008cc20011c004622f050000223f384c1e1313005ee21168fc66050f, 0x452090280ea615069fc720f03004a4010e87426311e8ec34010f0062c018285c320706),
    (0x4360f0d8741a000000442133785ca2199d0044c0135a6c161707af5f40160874be1500, 0x8f6d7e1f2007276dc088c5623f7e7fe401c388c4e211c8cfba270b8c4f231119f4762310, 0x8445a4d1084c62091c9e4aa091cf7febec008cca2691d854220de08c4daab13004e22200, 0x4364d218ffebd7e680c2277158f7a3cfe5ae0024d01f0fe3d5f0af5f6290186c3be800, 0xfdc523f61f4e270bed86c40011d004360107b6802131d89c562bf0bce10011f8d46a27f3, 0x47a131edec070bc099caa350d91e7730009d4660d1d816521106d6cfc018d96c5a1517),
    (0x4720501f740211960043e1763854a605240044249378140e092fafdaef57ca652a050b, 0x887623f11006ef68008dffe3d180079401168e7f7ef15007961a009dcde371c91c62130f, 0x848024b0c85c5febf18d4de4f20e7f9a0e00ae4aa4b32f646bcc0086c664b2000427ea00, 0x24b038e7efd3e49647e4f1789fe3e8009980231168ec3233018f5ae0b1780473ee00, 0x8944a390cf0e7f27ef8047ff600f0c2a07eeb65ae3d90f143e331fb844401608dc522915, 0x43e230dde6ef6996964de23029149721099c4a6250e896eb3304d64eb039288c3e0515),
    (0x43223f68541e17e5004d400009741a0b2600000012385c3a0502b7de2f751a7c321f2f, 0x8dc5be5fc006b346008900231170079c00008ac6e2f12fff9c0000886123b1f9ee2e211d, 0x8e8024f20f441fc3f39ecda49228e4122c00aecd62523864162ded854a60d23ff45e2a00, 0x4ae4901f77a3ebf188c3e371681fbbec00af8020d14807e7cdf3975e64b0689c7fea00, 0xfcfa21506f165f259fb75abe334f4c7629f3b756ecd6183c32011eb7df401638f4322b1d, 0x8043631188443801ad00436151e90e7c010899c7a150d8840e3716006132f359647e3525),
    (0x45a1b0882c0607e7004a2193b82c864a00000000126845261f2ead5d2ff63a4c36514d, 0x8b77e3115006db55b78a80221d3eefd401f7000023bf6fd787711c9b002331e9c6d22b11, 0x8749a232d8c41bee00844d6673feefd62e008d4de4f1cfd463e60087de24f1cef41bca00, 0xa68026d4089c3ff503a680253438e46bd200a6802750588feff00000002090281c37ca00, 0xf8c1b0760f1e370febb7c07d3fdf9c7a1b0accdbb2791f847a210abde7401718c43607f4, 0x90c1a1b10d5ed801b795412011c0064313b7944e2170c88c4c01b5df62b238e004363111),
    (0x402010981420010b004bc01278343a1a00000000134a143e5129ac002d76ca0cb6174f, 0x88f6a3c00e0f6344008b803fd1ae17d801ff8b7c62518fdfd36000890023d1b914023713, 0x87cee6932e6c13c000964a6633cfd41e22008dcda2d2dfdc1bc400865d2292e8cc53e600, 0xa60026932894261400a78021314f9feff3f4a98026d0380c7beff5a600271148f7a7f400, 0xf77c23118f367305ec885e70596f2c4e0f1800597158b824720715b95c8016c8442a091c, 0x4421908d8ee8018d9bcda05180063f4bb6954de09198564f491cd1e631337994721f04),
    (0x42a3d9683c380000000000138824325400a7800015ca1c361d28ad802d400a148e1800, 0x8ac6a21d5e4ebf74008b002371bee79800008a00231f1ff62c00008b00225c19844e391c, 0x854966f1de4c53e1fc8fc9e8d01ee46be800acc96472184c6fec0094dae4d2df7c17e400, 0xa700256008efe3ee00898026d3180fbff000a60025517f87f7f200a78026d0580803f600, 0xf07dba31df26332382004180170f3c5a15febfc4b1bfff540e0512005e401668cc5e03ff, 0x42e1715006d40181904063311946d7170c994b63d0185c3001b7dee77219d9dcae3b08),
    (0x6d6210e85c161e0000486e7298142a0600a5000015d824320600a4002f94d84c0e1b4b, 0x8d446231de9eb77000000022713e8790000000003e514f9fcf53fa8a803c71698cce191f, 0x8dc9e630ee6467c60087c9a653de5c622800854d20f3e84003ea00845ea652ced4100000, 0xaf0025536ffc33f600a18020f77817b3a9d7a80024b07897a7e800a88024f0781003ce00, 0xfe78793e50065b1b8dbcdd40171fac7233e7bd5f63f9c8e42e2ff6bc5e0000084c0e231e, 0x934aa210e006b001a69b4fa2f00006a319b29ac2a05148479f53b0dc6672b919b6d23336),
    (0x47a03fd83408000000002d54183c0e4600000000122a0c121800a5002fb4f85ca2114c, 0x22bdde96f35e008a00239fde8f6c000000002231dfc6bc01f80000001c0956ce3f07, 0x9dcd2472ef7003ca0087492411d85c67c00087cae632fff80228008c802493dec003c400, 0xa180253e7f8fbbe800a143a1503807ebcc00a100217068ffebd600a98025504c9803d600, 0x82fefb7fc00603019600594017ff34123df9bdd8703f2fac3617fbba60000000043e1ffe, 0x994e22b0f006fc01b194c9e371b006bc01ad80c961f1a8fe4001b3d166b3790954a22723),
    (0x44211608240c000000002db2400416500000000014ca4516112ca7002cd7da1c060000, 0x23b14e2f2f7ba8007ca3f14e57ec00008b803e11af46c3560000000011a95f6b731e, 0x8cc92420087003cc0085802013ee5003e00084802410df4003c800870020f1fed803e200, 0xa78027400f7ff60e00ae0020a008843bc800a00020900887b38a00a00025700f7fb3d400, 0xf6f9801f20062b3d88005d8019df24321ff8bf5d00126f04763be5b5dd000000047239e2, 0x92cde330a0040c01b593c3a2704004b801bb9bc8e291c8d6f401a3d864f398f95c7a692f),
    (0x41e1d76004d4000000000016b0041e4c00000000140a74020000ac802f378a340a1c00, 0x2331beaeff720000003ffdffe7580000000023ff2fcf235800000000114946123c00, 0x8d0026400ff803e80086002452100003c400840020d3ce5003e5fe9d802413fe441fc600, 0xae8026a008f43a1000a80024a008942fd000a18027200f07a3ce00ae0024c00880039200, 0xf87e401e7000032189bbd9c0127fa40a2d1eb9dcc017af740625ecbd5ac00000047e3ff5, 0x9b4c6340000000018e98cc63f070068401a99b47635110000001a6d8ecf1993944f27726),
    (0x406c55f00550000000002c37000408000000000014300406020000002c945a24b21200, 0x235d7eb7236600000023bd2ebf68000000002351b0073c00000000001189fe4e1000, 0x960024400e5003e4008c802292f8c803ee00958024d3de78022e00848022521e50000000, 0xa90027000887fff2009700256008fff2080088800000081473c800a90024800890038800, 0xf3ffc01840067b0376005980000004661910bc59c0178f4c46230cb2d9800000047a1deb, 0x9a4161c000000001a49ac321d1f0000001b892cd221020000001b4d56033f9c004dc0124),
    (0x420015000410000000000017c0048c000000000015000538000000002f15c0052c0000, 0x119e3ef8000000000011fe5f5400000000001170075400000000000009d6c00000, 0x26000e5803ce00000022400000000000000026400f70000000000026200e7003cc00, 0xa0000000000003a800af0000000000038e0081000000000003d200a70025000007bfcc00, 0xfe80000000064311810059000000000001f2b459000000000001fe005e800000000001e8, 0x93ce401190000001a89349000000000001a79a49238000000001a2d5800019f00000013c),
    (0x438015100000000000000015a000000000000000151000000000000000152004000000, 0x11ae377c0000000000000eaf300000000000000007040000000000000007740000, 0xe40000000000000000e70000000000024400000000000000024400ec8000000, 0xa8002720000003b60000000000000003f60000000000000000000090800000000003f200, 0x61f1d7dbe53800000000001fabcd8000000000001e00000000000000001fa, 0x924c8011a0000000009246400000000001a195c9c0000000000000d40033d87000000121),
    (0x17d00000000000000015800000000000000014600000000000000014b000000000, 0xe27680000000000000e077c0000000000000006f400000000001e4000000000, 0xe48000000000000000000000000000000000ef803c800, 0xa08000000000000000000000000000000000000000000000000000a10000000000000000, 0x604018e005ec00000000000000056400000000001f9000000000000000000, 0x1a4000000000000000000df803119e000000122),
    (0x17100000000000000015900000000000000014c000000000, 0xea7700000000000000e4f200000000000000006fc0000000000000000000000, 0x0, 0xa88000000000000000000000000000000000000000000000000000000000000000000000, 0x6200000000000000000000000000000000000000000000000000000000000, 0x1ae000000000000000000dd0000000000000000),
    (0x19d000000000000000000000000000000000147000000000, 0xedf5c0000000000000007240000000000000000000000000000000000000000, 0x0, 0xa10000000000000000000000000000000000000000000000000000000000000000000000, 0x6380000000000000000000000000000000000000000000000000000000000, 0x0),
)


def here():
    return lax.axis_index("row"), lax.axis_index("col")


def at(row, col):
    return {"row": row, "col": col}


def unless(own, step):
    if own is None:
        step()
    else:
        pl.when(jnp.logical_not(own))(step)


def copied(src, dst, send, recv, row, col):
    return pltpu.make_async_remote_copy(
        src_ref=src, dst_ref=dst, send_sem=send, recv_sem=recv,
        device_id=at(row, col), device_id_type=MESH,
    )


DIRECTIONS = ((1, 0, 0), (-1, 0, 0), (0, 1, 0), (0, -1, 0), (0, 0, 1), (0, 0, -1))
QUARTER = MEMBERS // ROWS // 4
LAG = 3
UNITS = 4 * ROWS


def place_of(i):
    return (i % 8) // 4, i % 4, i // 8


def arrivals():
    table = []
    for sends in ROUTES:
        by_direction = []
        for (dx, dy, dz), packed in zip(DIRECTIONS, sends):
            entries = []
            for i in range(32):
                x, y, z = place_of(i)
                fx, fy, fz = (x - dx) % 4, (y - dy) % 4, (z - dz) % 4
                entry = packed >> (9 * (fz * 8 + (fx % 2) * 4 + fy)) & 511
                if entry:
                    pair = (fx // 2) * 4 + fz + (entry >> 5 & 7)
                    entry = 256 | (pair - z) % 8 << 5 | entry & 31
                entries.append(entry)
            by_direction.append(entries)
        table.append(by_direction)
    return table


def departures():
    return [[[packed >> (9 * i) & 511 for i in range(32)] for packed in sends] for sends in ROUTES]


def words(table):
    return [
        [[d[i] | e[i] << 9 | f[i] << 18 for i in range(32)] for d, e, f in (sends[:3], sends[3:])]
        for sends in table
    ]


def looked_up(values, bits):
    if len(set(values)) == 1:
        return jnp.int32(values[0])
    low = looked_up(values[: len(values) // 2], bits[:-1])
    high = looked_up(values[len(values) // 2 :], bits[:-1])
    return jnp.where(bits[-1], high, low)


def gather_members(x_ref, held, send, recv, across_send, across_recv, own_sem, greet_all, before, spread_early, beside):
    r, c = here()
    core = lax.rem(c, 2)
    pair = lax.div(c, 2)
    z = lax.rem(pair, 4)
    x = lax.div(pair, 4) * 2 + lax.div(r, 4)
    y = lax.rem(r, 4)
    first = core == 0
    sign = 1 - 2 * core
    index = jnp.where(first, z * 8 + r, (3 - z) * 8 + 7 - r)
    bits = [lax.rem(lax.div(index, 2**b), 2) == 1 for b in range(5)]

    def neighbour(direction):
        dx, dy, dz = DIRECTIONS[direction]
        nx, ny, nz = (lax.rem(v + sign * d + 4, 4) for v, d in ((x, dx), (y, dy), (z, dz)))
        return lax.rem(nx, 2) * 4 + ny, lax.div(nx, 2) * 8 + nz * 2 + core

    sides = [neighbour(d) for d in range(6)]
    other = (r, c + sign)

    own_units = pl.ds(pl.multiple_of((pair * ROWS + r) * 4, 4), 4)
    across = lax.div(lax.rem(2 * pair - 4 + r + 2 - core - lax.rem(r, 2) + COLS, COLS), 2)

    own = pltpu.make_async_copy(x_ref, held.at[own_units], own_sem)
    own.start()
    greet_all(sides)
    own.wait()
    before()

    def unit(entry):
        relative = lax.rem(lax.div(entry, 32), 8)
        row = lax.rem(lax.div(entry, 4), 8)
        block = lax.rem(pair + sign * relative + 8, 8)
        row = jnp.where(first, row, 7 - row)
        return block, row * 4 + lax.rem(entry, 4)

    def entries(table):
        found = []
        for word in table:
            word = looked_up(word, bits)
            found += [lax.rem(word, 512), lax.rem(lax.div(word, 512), 512), lax.div(word, 512 * 512)]
        return found

    def across_copy(mine, there):
        return copied(held.at[mine], held.at[there], across_send, across_recv, *other)

    def take(step):
        for d, entry in enumerate(entries(incoming[step])):
            @pl.when(entry >= 256)
            def _(d=d, entry=entry):
                block, number = unit(entry)
                ref = held.at[block * UNITS + number]
                pltpu.make_async_copy(ref, ref, recv.at[step, d]).wait()

                @pl.when(block == across)
                def _():
                    across_copy(block * UNITS + number, 8 * UNITS + number).start()

    incoming, outgoing = words(arrivals()), words(departures())

    @pl.when(pair == across)
    def _():
        across_copy(own_units, pl.ds(8 * UNITS + r * 4, 4)).start()

    rounds = len(ROUTES)
    for step in range(rounds + LAG):
        if step == rounds:
            spread_early()
        if step >= LAG:
            take(step - LAG)
        if step < rounds:
            for d, entry in enumerate(entries(outgoing[step])):
                @pl.when(entry >= 256)
                def _(d=d, entry=entry):
                    block, number = unit(entry)
                    ref = held.at[block * UNITS + number]
                    copied(ref, ref, send, recv.at[step, d], *sides[d]).start()

    whole = across_copy(pl.ds(0, UNITS), pl.ds(8 * UNITS, UNITS))
    counts = [sum((packed >> (9 * i) & 256) // 256 for sends in ROUTES for packed in sends) for i in range(32)]
    count = looked_up(counts, bits)

    def finish():
        for total in sorted(set(counts)):
            @pl.when(count == total)
            def _(total=total):
                units = held.at[pl.ds(0, total)]
                copied(units, units, send, recv.at[0, 0], *sides[0]).wait_send()
        whole.wait_send()

    beside()
    whole.wait_recv()
    return finish


def parted(values):
    high = values.astype(jnp.bfloat16)
    low = (values - high.astype(jnp.float32)).astype(jnp.bfloat16)
    return high, low


def dotted(a, b, dims):
    return lax.dot_general(a, b, (dims, ((), ())), preferred_element_type=jnp.float32)


def skewed(rows, shift):
    sub = lax.broadcasted_iota(jnp.int32, rows.shape, 0)
    if shift:
        rows = pltpu.roll(rows, SPAN - shift, 1)
    for bit in (1, 2, 4):
        rows = jnp.where((sub & bit) != 0, pltpu.roll(rows, SPAN - bit, 1), rows)
    return rows[:, :BLOCK]


def main_kernel(
    members_ref, w_ref, local_out, out_ref,
    held, xh, xl, band_ref, high_ref, low_ref, local_ref,
    iterate, near, window, wide, parts, sums, square_ref, row_squares, col_squares, row_total,
    member_send, member_recv, across_send, across_recv, own_sem, store_sem, send_z, recv_z, send_w, recv_w, send_x, recv_x, send_y, recv_y, send_r, recv_r, send_c, recv_c,
):
    r, c = here()
    core = lax.rem(c, 2)
    pair = lax.div(c, 2)
    other = (r, c + 1 - 2 * core)
    shared = 1 - core
    passes = core == lax.rem(r + 1, 2)

    def greet_all(sides):
        barrier = pltpu.get_barrier_semaphore()
        partners = list(sides)
        for shift in range(1, ROWS):
            row = lax.rem(r + shift, ROWS)
            partners += [(row, 2 * pair), (row, 2 * pair + 1)]
        for shift in range(1, COLS):
            partners.append((r, lax.rem(c + shift, COLS)))
        for row, col in partners:
            pl.semaphore_signal(barrier, inc=1, device_id=at(row, col), device_id_type=MESH)
        pl.semaphore_wait(barrier, len(partners))

    def to_pairs(step, source, away):
        col = lax.rem(c - 2 * away + COLS, COLS)
        return copied(source, near.at[step, away + 2], send_z.at[step], recv_z.at[step, away + 2], r, col)

    def targets(away):
        found = []
        for e in range(3):
            row = 2 * away + core + 2 + e
            valid = None
            if away == -2:
                if e == 0:
                    continue
                valid = core == 1 if e == 1 else None
            if away == 2:
                if e == 2:
                    continue
                valid = core == 0 if e == 1 else None
            there = (1, core, 0)[e]
            panel = (1, shared, 0)[e]
            found.append((row, there, panel, valid))
        return found

    def share(step, source, away, act):
        for row, there, panel, valid in targets(away):
            own = (row == r) & (there == core)
            go = jnp.logical_not(own)
            if valid is not None:
                own, go = own & valid, go & valid

            @pl.when(go)
            def _(row=row, there=there, panel=panel):
                act(copied(
                    source, window.at[step, panel, r], send_w.at[step], recv_w.at[step, panel], row, 2 * pair + there
                ))

            @pl.when(own)
            def _(panel=panel):
                act(pltpu.make_async_copy(source, window.at[step, panel, r], recv_w.at[step, panel]))

    def begin(copy):
        copy.start()

    def send_iterate(step, source):
        for away in (-2, 2, -1, 1):
            to_pairs(step, source, away).start()
        share(step, source, 0, begin)

    def spread_iterate(step):
        for away in (-1, 1, -2, 2):
            block = near.at[step, away + 2]
            pltpu.make_async_copy(block, block, recv_z.at[step, away + 2]).wait()
            share(step, block, away, begin)

    def across_copy(step):
        return copied(
            window.at[step, shared], window.at[step, 1 - shared], send_x.at[step], recv_x.at[step], *other
        )

    def split(step, panel):
        high, low = parted(window[step, panel].reshape(BLOCK, PIECE))
        first = pl.multiple_of(panel * BLOCK, BLOCK)
        wide[pl.ds(first, BLOCK), :PIECE] = high
        wide[pl.ds(first, BLOCK), PIECE:] = low

    def landed(step, panel):
        block = window.at[step, panel]
        pltpu.make_async_copy(block, block, recv_w.at[step, panel]).wait()

    def take_iterate(step):
        @pl.when(passes)
        def _():
            landed(step, shared)
            across_copy(step).start()
            split(step, shared)

        landed(step, core)
        split(step, core)

        @pl.when(jnp.logical_not(passes))
        def _():
            across_copy(step).wait_recv()
            split(step, shared)

    def normalise(panel, block):
        for first in range(0, BLOCK, SUB):
            values = held[pl.ds(block * UNITS, UNITS), :, first : first + SUB].reshape(MEMBERS, SUB)
            centered = values - jnp.sum(values, 0, keepdims=True) / MEMBERS
            spread = jnp.sqrt(jnp.sum(centered * centered, 0, keepdims=True) + epsilon)
            high, low = parted(centered / spread)
            lo_at = (panel - 1) * BLOCK + first if panel else 2 * BLOCK + first
            xh[:, lo_at : lo_at + SUB] = high
            xl[:, lo_at : lo_at + SUB] = low

    finish = gather_members(
        members_ref, held, member_send, member_recv, across_send, across_recv, own_sem, greet_all,
        lambda: send_iterate(0, w_ref), lambda: spread_iterate(0), lambda: normalise(0, pair),
    )
    near_block = lax.div(lax.rem(c + r - 4 + COLS, COLS), 2)
    far_block = lax.div(lax.rem(c + r - 3 + COLS, COLS), 2)
    odd = lax.rem(r, 2) == 1
    normalise(1, jnp.where(odd, 8, near_block))
    normalise(2, jnp.where(odd, far_block, 8))
    squares = jnp.zeros((8, 128), jnp.float32)
    gap = lax.broadcasted_iota(jnp.int32, (SUB, SPAN), 1) - lax.broadcasted_iota(jnp.int32, (SUB, SPAN), 0)
    taper = jnp.maximum(0.0, 1.0 - jnp.abs(gap + (r * BLOCK - WINDOW)).astype(jnp.float32) / WINDOW)
    taper = jnp.where((gap >= 0) & (gap < BLOCK), taper, 0.0)
    for tile in range(BLOCK // SUB):
        first = tile * SUB
        rows_h = xh[:, 2 * BLOCK + first : 2 * BLOCK + first + SUB]
        rows_l = xl[:, 2 * BLOCK + first : 2 * BLOCK + first + SUB]
        cols_h = xh[:, first : first + SPAN]
        cols_l = xl[:, first : first + SPAN]
        over = ((0,), (0,))
        gram = dotted(rows_h, cols_h, over) + (dotted(rows_h, cols_l, over) + dotted(rows_l, cols_h, over))
        band = gram * taper
        band_ref[tile] = band
        high, low = parted(band)
        high_ref[tile] = high
        low_ref[tile] = low
        squares = squares + jnp.sum((band * band).reshape(SUB // 8, 8, SPAN // 128, 128), (0, 2))
    square_ref[...] = squares

    for shift in range(1, ROWS):
        copied(square_ref, row_squares.at[r], send_r, recv_r, lax.rem(r + shift, ROWS), c).start()

    stores = []

    def skew(tile):
        first = tile * SUB
        for group in range(0, SUB, 8):
            local_ref[first + group : first + group + 8, :] = skewed(band_ref[tile, group : group + 8, :], group)
        stores.append(pltpu.make_async_copy(local_ref.at[first : first + SUB], local_out.at[first : first + SUB], store_sem.at[tile]))
        stores[-1].start()

    def several(ref, send, recv):
        return copied(ref, ref, send, recv, *other)

    def piece_out(step, row):
        return copied(
            parts.at[step, row * PIECE : (row + 1) * PIECE], sums.at[step * ROWS + r],
            send_y.at[step], recv_y.at[step], row, c,
        )

    def sent(step):
        several(near.at[step, pl.ds(0, 4)], send_z.at[step], recv_z.at[step, 0]).wait_send()
        several(sums.at[pl.ds(0, 11)], send_w.at[step], recv_w.at[step, 0]).wait_send()
        pl.when(passes)(lambda: across_copy(step).wait_send())

    def pieces(step):
        return several(sums.at[pl.ds(step * ROWS, ROWS - 1)], send_y.at[step], recv_y.at[step])

    row_copies = several(row_squares.at[pl.ds(0, ROWS - 1)], send_r, recv_r)
    col_copies = several(col_squares.at[pl.ds(0, COLS - 1)], send_c, recv_c)
    total = None
    summed = power_terms[0] * w_ref[...]
    for step in range(STEPS):
        take_iterate(step)
        for tile in range(BLOCK // SUB):
            first = tile * SUB
            over = ((1,), (0,))
            both = dotted(high_ref[tile], wide[first : first + SPAN, :], over)
            rest = dotted(low_ref[tile], wide[first : first + SPAN, :PIECE], over)
            parts[step, first : first + SUB, :] = both[:, :PIECE] + (both[:, PIECE:] + rest)
            for row in range(first // PIECE, (first + SUB) // PIECE):
                unless(r == row, lambda row=row: piece_out(step, row).start())
        if step == 0:
            row_copies.wait_recv()
            squares = jnp.zeros((8, 128), jnp.float32)
            for row in range(ROWS):
                squares = squares + jnp.where(r == row, square_ref[...], row_squares[row])
            row_total[...] = squares
            for shift in range(1, COLS):
                copied(row_total, col_squares.at[c], send_c, recv_c, r, lax.rem(c + shift, COLS)).start()
            skew(0)
            col_copies.wait_recv()
            squares = jnp.zeros((8, 128), jnp.float32)
            for col in range(COLS):
                squares = squares + jnp.where(c == col, row_total[...], col_squares[col])
            total = jnp.sum(squares, keepdims=True) / STATES
        elif step == 1:
            skew(2)
        else:
            sent(1)
            sent(2)
            pieces(0).wait_send()
            pieces(1).wait_send()
        vector = parts[step, pl.ds(pl.multiple_of(r * PIECE, PIECE), PIECE), :]
        pieces(step).wait_recv()
        for row in range(ROWS):
            vector = vector + jnp.where(r == row, 0.0, sums[step * ROWS + row])
        vector = vector / total
        summed = summed + power_terms[step + 1] * vector
        if step < STEPS - 1:
            iterate[step] = vector
            send_iterate(step + 1, iterate.at[step])
            if step == 0:
                finish()
                sent(0)
            else:
                row_copies.wait_send()
                col_copies.wait_send()
            spread_iterate(step + 1)
            skew(2 * step + 1)
    out_ref[...] = jnp.sqrt(total) * summed

    for copy in stores:
        copy.wait()
    pieces(STEPS - 1).wait_send()


def band_and_sample(members, probes):
    return pl.pallas_call(
        main_kernel,
        name="band_and_sample",
        out_shape=(
            jax.ShapeDtypeStruct((BLOCK, BLOCK), jnp.float32),
            jax.ShapeDtypeStruct((PIECE, PIECE), jnp.float32),
        ),
        in_specs=[pl.BlockSpec(memory_space=pl.ANY), pl.BlockSpec(memory_space=pltpu.VMEM)],
        out_specs=[pl.BlockSpec(memory_space=pl.ANY), pl.BlockSpec(memory_space=pltpu.VMEM)],
        scratch_shapes=[
            pltpu.VMEM((9 * UNITS, QUARTER, BLOCK), jnp.float32),
            pltpu.VMEM((MEMBERS, 3 * BLOCK), jnp.bfloat16),
            pltpu.VMEM((MEMBERS, 3 * BLOCK), jnp.bfloat16),
            pltpu.VMEM((BLOCK // SUB, SUB, SPAN), jnp.float32),
            pltpu.VMEM((BLOCK // SUB, SUB, SPAN), jnp.bfloat16),
            pltpu.VMEM((BLOCK // SUB, SUB, SPAN), jnp.bfloat16),
            pltpu.VMEM((BLOCK, BLOCK), jnp.float32),
            pltpu.VMEM((STEPS - 1, PIECE, PIECE), jnp.float32),
            pltpu.VMEM((STEPS, 5, PIECE, PIECE), jnp.float32),
            pltpu.VMEM((STEPS, 2, ROWS, PIECE, PIECE), jnp.float32),
            pltpu.VMEM((2 * BLOCK, 2 * PIECE), jnp.bfloat16),
            pltpu.VMEM((STEPS, BLOCK, PIECE), jnp.float32),
            pltpu.VMEM((STEPS * ROWS, PIECE, PIECE), jnp.float32),
            pltpu.VMEM((8, 128), jnp.float32),
            pltpu.VMEM((ROWS, 8, 128), jnp.float32),
            pltpu.VMEM((COLS, 8, 128), jnp.float32),
            pltpu.VMEM((8, 128), jnp.float32),
            pltpu.SemaphoreType.DMA,
            pltpu.SemaphoreType.DMA((len(ROUTES), 6)),
            pltpu.SemaphoreType.DMA,
            pltpu.SemaphoreType.DMA,
            pltpu.SemaphoreType.DMA,
            pltpu.SemaphoreType.DMA((BLOCK // SUB,)),
            pltpu.SemaphoreType.DMA((STEPS,)),
            pltpu.SemaphoreType.DMA((STEPS, 5)),
            pltpu.SemaphoreType.DMA((STEPS,)),
            pltpu.SemaphoreType.DMA((STEPS, 2)),
            pltpu.SemaphoreType.DMA((STEPS,)),
            pltpu.SemaphoreType.DMA((STEPS,)),
            pltpu.SemaphoreType.DMA((STEPS,)),
            pltpu.SemaphoreType.DMA((STEPS,)),
            pltpu.SemaphoreType.DMA,
            pltpu.SemaphoreType.DMA,
            pltpu.SemaphoreType.DMA,
            pltpu.SemaphoreType.DMA,
        ],
        compiler_params=pltpu.CompilerParams(
            collective_id=1, has_side_effects=True, vmem_limit_bytes=VMEM_LIMIT
        ),
    )(members, probes)


def on_device(perturbations, probes):
    return band_and_sample(perturbations.reshape(4, QUARTER, BLOCK), probes)


def solution(mesh):
    return jax.shard_map(
        on_device,
        mesh=mesh,
        in_specs=(P("row", "col"), P(("col", "row"), None)),
        out_specs=(P("col", "row"), P(("col", "row"), None)),
        check_vma=False,
    )
```
